256 devices in a mesh: gx: 32 (over y, z_lo, core), gy: 8 (over z_hi, x).
Axes of the slice: x: 4, y: 4, z: 8 (z_hi: 2, z_lo: 4; z = z_hi * 4 + z_lo), core: 2. Of those that a mesh axis runs over, the one named last changes fastest.
Arguments:
- control: bfloat16 [2048, 8, 2048], P('gx', None, 'gy'), may hold values from -6 to 6
- innovation: float32 [2048, 8, 2048], P('gx', None, 'gy'), may hold values from -6 to 6
- obs_weight: float32 [2048, 8, 2048], P('gx', None, 'gy'), may hold values from 0.5 to 4
- courant_x: float32 [2048, 8, 2048], P('gx', None, 'gy'), may hold values from -0.9 to 0.9
- courant_y: float32 [2048, 8, 2048], P('gx', None, 'gy'), may hold values from -0.9 to 0.9
- filter_x: bfloat16 [2048, 2048], P('gx'), may hold values from -3 to 3
- filter_y: bfloat16 [2048, 2048], P('gy'), may hold values from -3 to 3
Outputs:
- end_state: float32 [2048, 8, 2048], P('gx', None, 'gy')
- gradient: float32 [2048, 8, 2048], P('gx', None, 'gy')
The draws below stay inside these ranges and needn't reach their ends.
All inputs are finite; a program needn't handle non-finite values.
Results may differ from the reference program's by a relative error of at most 0.0029.
Values may be sent and summed in bfloat16 or wider, within the bound.
A program may use at most 128 MiB of HBM per device.

```python
import math
import jax
import jax.numpy as jnp

NX = 2048
NY = 2048
LEV = 8


def filter_matrix(key, order):
    key_len = jax.random.fold_in(key, 11)
    key_gain = jax.random.fold_in(key, 12)
    key_far = jax.random.fold_in(key, 13)
    places = jnp.arange(order, dtype=jnp.float32)
    distance = jnp.abs(places[:, None] - places[None, :])
    lengths = jnp.exp(jax.random.uniform(key_len, (order, 1), jnp.float32, math.log(order / 64.0), math.log(order / 4.0)))
    gains = jax.random.uniform(key_gain, (order, order), jnp.float32, 0.5, 1.5)
    local_part = jnp.exp(-distance / lengths) * gains / jnp.sqrt(2.0 * lengths)
    far_part = jnp.clip(jax.random.normal(key_far, (order, order), jnp.float32), -5.0, 5.0) * (0.5 / math.sqrt(order))
    return local_part + far_part + jnp.eye(order, dtype=jnp.float32)


def draw_filter_x(key, part):
    return filter_matrix(key, NX).astype(jnp.bfloat16)


def draw_filter_y(key, part):
    return filter_matrix(jax.random.fold_in(key, 77), NY).astype(jnp.bfloat16)


def block_scale(own_key, dims, shards, least, top_value):
    def one(position, parts):
        steps = jax.random.uniform(jax.random.fold_in(jax.random.fold_in(own_key, 6), position), (parts,), jnp.float32, least / len(shards), top_value / len(shards))
        return jnp.repeat(jnp.exp(steps), dims[position] // parts).reshape((-1,) + (1,) * (len(dims) - position - 1))

    gain = one(*shards[0])
    for cut in shards[1:]:
        gain = gain * one(*cut)
    return gain


def gaussian(rng, dims, deviation, limit, pieces=(), held_as=jnp.bfloat16):
    values = deviation * jax.random.normal(rng, dims, jnp.float32)
    if pieces:
        values = values * block_scale(rng, dims, pieces, -0.22, 0.18)
    return jnp.clip(values, -limit, limit).astype(held_as)


def setup_inputs(seed: int = 0) -> dict:
    streams_of = jax.random.split(jax.random.key(seed), 8)
    return {
        "control": gaussian(streams_of[0], (NX, LEV, NY), 1.0, 6.0, ((0, 32), (2, 8))),
        "innovation": gaussian(streams_of[1], (NX, LEV, NY), 1.0, 6.0, ((0, 32), (2, 8)), jnp.float32),
        "obs_weight": jnp.clip(jnp.exp(math.log(4.0) - 2.0794415 * jax.random.uniform(streams_of[2], (NX, LEV, NY), jnp.float32) ** block_scale(streams_of[2], (NX, LEV, NY), ((0, 32), (2, 8)), -0.2, 0.2)), 0.5, 4.0),
        "courant_x": jnp.clip(jax.random.uniform(streams_of[3], (NX, LEV, NY), jnp.float32, -0.9, 0.9) * block_scale(streams_of[3], (NX, LEV, NY), ((0, 32), (2, 8)), -0.4, 0.0), -0.9, 0.9),
        "courant_y": jnp.clip(jax.random.uniform(streams_of[4], (NX, LEV, NY), jnp.float32, -0.9, 0.9) * block_scale(streams_of[4], (NX, LEV, NY), ((0, 32), (2, 8)), -0.4, 0.0), -0.9, 0.9),
        "filter_x": draw_filter_x(jax.random.fold_in(streams_of[7], 71), 0),
        "filter_y": draw_filter_y(jax.random.fold_in(streams_of[7], 71), 0),
    }


def reference(control, innovation, obs_weight, courant_x, courant_y, filter_x, filter_y):
    matrix_x = filter_x.astype(jnp.float32)
    matrix_y = filter_y.astype(jnp.float32)
    control_f = control.astype(jnp.float32)
    smoothed = jnp.einsum("ij,jlc->ilc", matrix_x, control_f).astype(jnp.bfloat16)
    start_state = jnp.einsum("kc,xlc->xlk", matrix_y, smoothed.astype(jnp.float32))
    padded = jnp.pad(start_state, ((1, 1), (0, 0), (1, 1)))
    end_state = (start_state
                 - courant_x * (padded[2:, :, 1:-1] - padded[:-2, :, 1:-1]) * 0.5
                 - courant_y * (padded[1:-1, :, 2:] - padded[1:-1, :, :-2]) * 0.5)
    misfit = obs_weight * (end_state - innovation)
    flux_x = jnp.pad(courant_x * misfit, ((1, 1), (0, 0), (1, 1)))
    flux_y = jnp.pad(courant_y * misfit, ((1, 1), (0, 0), (1, 1)))
    adjoint = (misfit
               + 0.5 * (flux_x[2:, :, 1:-1] - flux_x[:-2, :, 1:-1])
               + 0.5 * (flux_y[1:-1, :, 2:] - flux_y[1:-1, :, :-2])).astype(jnp.bfloat16)
    pulled = jnp.einsum("kc,xlk->xlc", matrix_y, adjoint.astype(jnp.float32)).astype(jnp.bfloat16)
    gradient = control_f + jnp.einsum("ij,ilc->jlc", matrix_x, pulled.astype(jnp.float32))
    return end_state, gradient
```

```python
import jax
import jax.numpy as jnp
from jax import lax
from jax.experimental import pallas as pl
from jax.experimental.pallas import tpu as pltpu
from jax.sharding import PartitionSpec as P

MESH = pl.DeviceIdType.MESH
F32 = jnp.float32
BF16 = jnp.bfloat16
STEP = {1: 1, 2: 2, 3: 7}


def place(x, y, z, c):
    return (y * 8 + lax.rem(z, 4) * 2 + c, (z // 4) * 4 + x)


def kernel(
    ctl, innov, weight, cou_x, cou_y, fx, fy,
    end_out, grad_out,
    ctl_v, inn_v, wei_v, cx_v, cy_v, end_v, grad_v,
    nat, snd0, cg, fxb, fyb, acc1, s1b, s1g, acc2, s2b, stg,
    st, hys, hyr, hl, hr, qx, py, mis, adj, hps, hpr, ags, ag,
    psend, pown, pg, pb, gsend, gown, gg, gs, go,
    loc_sem, f1_s, f1_r, fo_s, fo_r, f2_s, f2_r, fr_s, fr_r,
    g1_s, g1_r, g2_s, g2_r, gr_s, gr_r,
    s0_s, s0_r, s1_s, s1_r, s2_s, s2_r, s3_s, s3_r,
    h_s, h_r, k_s, k_r, s5_s, s5_r, s6_s, s6_r, s7_s, s7_r, s8_s, s8_r,
):
    gx = lax.axis_index("gx")
    gy = lax.axis_index("gy")
    y = gx // 8
    zl = lax.rem(gx // 2, 4)
    c = lax.rem(gx, 2)
    zh = gy // 4
    x = lax.rem(gy, 4)
    z = zh * 4 + zl
    o = 1 - c
    sib = place(x, y, z, o)
    e = y * 2 + c
    pending = []

    def send(src, dst, ssem, rsem, dev):
        copy = pltpu.make_async_remote_copy(
            src_ref=src, dst_ref=dst, send_sem=ssem, recv_sem=rsem,
            device_id=dev, device_id_type=MESH)
        copy.start()
        pending.append(copy)

    def arrived(dst, rsem):
        pltpu.make_async_copy(dst, dst, rsem).wait()

    xs = [lax.rem(x + t, 4) for t in range(4)]
    ys = [lax.rem(y + t, 4) for t in range(4)]
    zs = [lax.rem(z + t, 8) for t in range(8)]
    up = (lax.rem(gx + 1, 32), gy)
    down = (lax.rem(gx + 31, 32), gy)
    right = (gx, lax.rem(gy + 1, 8))
    left = (gx, lax.rem(gy + 7, 8))

    load_ctl = pltpu.make_async_copy(ctl, ctl_v, loc_sem.at[0])
    load_ctl.start()
    loads = [
        pltpu.make_async_copy(s, d, loc_sem.at[1 + i])
        for i, (s, d) in enumerate([
            (fx, fxb.at[c, 0]), (fy, fyb.at[zh]), (innov, inn_v),
            (weight, wei_v), (cou_x, cx_v), (cou_y, cy_v)])
    ]
    for load in loads:
        load.start()

    barrier = pltpu.get_barrier_semaphore()
    partners = [sib]
    for t in range(1, 8):
        partners += [place(x, y, zs[t], c), place(x, y, zs[t], o)]
    for t in range(1, 4):
        partners += [place(xs[t], y, z, c), place(xs[t], y, z, o)]
        partners += [place(x, ys[t], z, c)]
    partners += [up, down, left, right]
    for dev in partners:
        pl.semaphore_signal(barrier, inc=1, device_id=dev, device_id_type=MESH)

    load_ctl.wait()
    for h in range(2):
        nat[h] = ctl_v[:, :, h * 128:(h + 1) * 128].astype(F32).reshape(512, 128)
    for l in range(8):
        for h in range(2):
            snd0[l, :, h * 128:(h + 1) * 128] = nat[h, pl.ds(l, 64, stride=8), :].astype(BF16)

    pl.semaphore_wait(barrier, len(partners))

    slot0 = zl * 2 + c
    for t in (4, 3, 5, 2, 6, 1, 7):
        send(snd0.at[zs[t]], cg.at[gx], s0_s.at[t], s0_r.at[slot0], place(x, y, zs[t], zh))
    own0 = pltpu.make_async_copy(snd0.at[z], cg.at[gx], s0_r.at[slot0])
    far0 = pltpu.make_async_remote_copy(
        src_ref=snd0.at[z], dst_ref=cg.at[gx], send_sem=s0_s.at[0], recv_sem=s0_r.at[slot0],
        device_id=sib, device_id_type=MESH)

    @pl.when(zh == c)
    def _():
        own0.start()

    @pl.when(zh != c)
    def _():
        far0.start()

    for d in (2, 1, 3):
        dest = place(x, y, lax.rem(z + 8 - STEP[d], 8), c)
        send(fx.at[x], fxb.at[c, d, x], f1_s.at[d - 1], f1_r.at[d - 1], dest)
    send(fx, fxb.at[c, 0], fo_s.at[0], fo_r.at[0], sib)

    for s in range(4):
        for cc in range(2):
            arrived(cg.at[y * 8 + 2 * s + cc], s0_r.at[2 * s + cc])
        block = cg.at[pl.ds(y * 8 + 2 * s, 2)]
        for t in (2, 1, 3):
            send(block, block, s1_s.at[t - 1, s], s1_r.at[t - 1, s], place(x, ys[t], z, c))

    for d in range(1, 4):
        arrived(fxb.at[c, d, x], f1_r.at[d - 1])
    quarter = fxb.at[c, pl.ds(1, 3), x]
    for t in (2, 1, 3):
        send(quarter, quarter, f2_s.at[t - 1], f2_r.at[t - 1], place(xs[t], y, z, c))
    send(quarter, quarter, fr_s.at[0], fr_r.at[0], sib)

    send(fy.at[e], fyb.at[zh, e], g1_s.at[0], g1_r.at[0], place(x, y, zs[4], c))

    for t in (3, 1, 2):
        xq = lax.rem(x + 4 - t, 4)
        part = fxb.at[c, pl.ds(1, 3), xq]
        arrived(part, f2_r.at[t - 1])
        send(part, part, fr_s.at[t], fr_r.at[t], sib)

    loads[0].wait()
    loads[1].wait()
    arrived(fxb.at[o, 0], fo_r.at[0])
    for t in range(4):
        xq = lax.rem(x + 4 - t, 4)
        arrived(fxb.at[o, pl.ds(1, 3), xq], fr_r.at[t])

    def rows_dot(q):
        cols = pl.ds(pl.multiple_of(q * 512, 512), 512)
        a = fxb[:, :, :, :, cols].reshape(512, 512)
        b = cg[pl.ds(q * 8, 8)].reshape(512, 256)
        return jnp.dot(a, b, preferred_element_type=F32)

    acc1[...] = rows_dot(y)
    for t in (3, 1, 2):
        yq = lax.rem(y + 4 - t, 4)
        for s in range(4):
            arrived(cg.at[pl.ds(yq * 8 + 2 * s, 2)], s1_r.at[t - 1, s])
        if t != 2:
            acc1[...] += rows_dot(yq)
        else:
            s1b[...] = (acc1[...] + rows_dot(yq)).astype(BF16).reshape(2, 256, 256)

    mine = c * 4 + x
    for t in (2, 1, 3):
        for r in range(2):
            send(s1b.at[r], s1g.at[mine], s2_s.at[t, r], s2_r.at[t, c], place(xs[t], y, z, r))
    send(s1b.at[o], s1g.at[mine], s2_s.at[0, 0], s2_r.at[0, 0], sib)
    s1g[mine] = s1b[c]

    zo = 1 - zh
    arrived(fyb.at[zo, e], g1_r.at[0])
    for t in (2, 1, 3):
        send(fyb.at[zo, e], fyb.at[zo, e], g2_s.at[t - 1], g2_r.at[t - 1], place(x, ys[t], z, c))
    send(fyb.at[zo, e], fyb.at[zo, e], gr_s.at[0], gr_r.at[0], sib)
    for t in (3, 1, 2):
        eq = lax.rem(y + 4 - t, 4) * 2 + c
        arrived(fyb.at[zo, eq], g2_r.at[t - 1])
        send(fyb.at[zo, eq], fyb.at[zo, eq], gr_s.at[t], gr_r.at[t], sib)
    for t in range(4):
        eq = lax.rem(y + 4 - t, 4) * 2 + o
        arrived(fyb.at[zo, eq], gr_r.at[t])

    def cols_dot(q):
        cols = pl.ds(pl.multiple_of(q * 256, 256), 256)
        b = fyb[:, :, :, cols].reshape(512, 256)
        return lax.dot_general(s1g[q], b, (((1,), (1,)), ((), ())), preferred_element_type=F32)

    acc2[...] = cols_dot(mine)
    arrived(s1g.at[o * 4 + x], s2_r.at[0, 0])
    acc2[...] += cols_dot(o * 4 + x)
    for t in (3, 1, 2):
        xq = lax.rem(x + 4 - t, 4)
        for cc in range(2):
            arrived(s1g.at[cc * 4 + xq], s2_r.at[t, cc])
            acc2[...] += cols_dot(cc * 4 + xq)
    for hh in range(2):
        s2b[hh] = acc2[:, hh * 256:(hh + 1) * 256].astype(BF16).reshape(4, 64, 256)

    for t in (4, 3, 5, 2, 6, 1, 7):
        send(s2b.at[zs[t] // 4, t % 4], stg.at[z], s3_s.at[t - 1], s3_r.at[t - 1], place(x, y, zs[t], c))
    stg[z] = s2b[zh, 0]

    def spread(l):
        value = stg[l].astype(F32)
        for h in range(2):
            st[h, pl.ds(8 + l, 64, stride=8), :] = value[:, h * 128:(h + 1) * 128]

    for t in range(1, 8):
        arrived(stg.at[lax.rem(z + 8 - t, 8)], s3_r.at[t - 1])
    for l in range(8):
        spread(l)

    def edges(field, hsend, hrecv, hleft, hright, ssem, rsem, ref_first, ref_last):
        send(ref_first(0), ref_last(1), ssem.at[0], rsem.at[0], down)
        send(ref_last(0), ref_first(1), ssem.at[1], rsem.at[1], up)
        hsend[0] = field(0).T[0:8]
        send(hsend.at[0], hrecv.at[0], ssem.at[2], rsem.at[2], left)
        hsend[1] = field(1).T[120:128]
        send(hsend.at[1], hrecv.at[1], ssem.at[3], rsem.at[3], right)
        arrived(ref_last(1), rsem.at[0])
        arrived(ref_first(1), rsem.at[1])
        arrived(hrecv.at[0], rsem.at[2])
        arrived(hrecv.at[1], rsem.at[3])
        keep_r = jnp.where(gy == 7, 0.0, 1.0).astype(F32)
        keep_l = jnp.where(gy == 0, 0.0, 1.0).astype(F32)
        hright[...] = jnp.broadcast_to(hrecv[0, 0:1, :] * keep_r, (128, 512)).T
        hleft[...] = jnp.broadcast_to(hrecv[1, 7:8, :] * keep_l, (128, 512)).T

    def fringe(ref):
        first = lambda k: ref.at[:, pl.ds(8, 8)] if k == 0 else ref.at[:, pl.ds(0, 8)]
        last = lambda k: ref.at[:, pl.ds(512, 8)] if k == 0 else ref.at[:, pl.ds(520, 8)]
        return first, last

    def clear(ref):
        @pl.when(gx == 0)
        def _():
            ref[:, 0:8, :] = jnp.zeros((2, 8, 128), F32)

        @pl.when(gx == 31)
        def _():
            ref[:, 520:528, :] = jnp.zeros((2, 8, 128), F32)

    first, last = fringe(st)
    edges(lambda h: st[h, 8:520, :], hys, hyr, hl, hr, h_s, h_r, first, last)
    clear(st)
    for load in loads[2:]:
        load.wait()

    lane = lax.broadcasted_iota(jnp.int32, (64, 128), 1)

    def beside(v0, v1, left_halo, right_halo):
        f0, f1 = pltpu.roll(v0, 127, 1), pltpu.roll(v1, 127, 1)
        b0, b1 = pltpu.roll(v0, 1, 1), pltpu.roll(v1, 1, 1)
        after = (jnp.where(lane == 127, f1, f0), jnp.where(lane == 127, right_halo, f1))
        before = (jnp.where(lane == 0, left_halo, b0), jnp.where(lane == 0, b0, b1))
        return before, after

    @pl.loop(0, 8)
    def _(i):
        at = pl.multiple_of(i * 64, 64)
        xr = pl.ds(i * 8, 8)
        v = [st[h, pl.ds(at + 8, 64), :] for h in range(2)]
        before, after = beside(v[0], v[1], hl[pl.ds(at, 64), :], hr[pl.ds(at, 64), :])
        for h in range(2):
            ln = slice(h * 128, (h + 1) * 128)
            cx = cx_v[xr, :, ln].reshape(64, 128)
            cy = cy_v[xr, :, ln].reshape(64, 128)
            prev = st[h, pl.ds(at, 64), :]
            post = st[h, pl.ds(at + 16, 64), :]
            end = v[h] - cx * (post - prev) * 0.5 - cy * (after[h] - before[h]) * 0.5
            end_v[xr, :, ln] = end.reshape(8, 8, 128)
            m = wei_v[xr, :, ln].reshape(64, 128) * (end - inn_v[xr, :, ln].reshape(64, 128))
            mis[h, pl.ds(at, 64), :] = m
            qx[h, pl.ds(at + 8, 64), :] = cx * m
            py[h, pl.ds(at, 64), :] = cy * m

    store_end = pltpu.make_async_copy(end_v, end_out, loc_sem.at[7])
    store_end.start()

    first, last = fringe(qx)
    edges(lambda h: py[h], hps, hpr, hl, hr, k_s, k_r, first, last)
    clear(qx)

    @pl.loop(0, 8)
    def _(i):
        at = pl.multiple_of(i * 64, 64)
        v = [py[h, pl.ds(at, 64), :] for h in range(2)]
        before, after = beside(v[0], v[1], hl[pl.ds(at, 64), :], hr[pl.ds(at, 64), :])
        for h in range(2):
            prev = qx[h, pl.ds(at, 64), :]
            post = qx[h, pl.ds(at + 16, 64), :]
            adj[h, pl.ds(at, 64), :] = (
                mis[h, pl.ds(at, 64), :] + 0.5 * (post - prev) + 0.5 * (after[h] - before[h]))

    for l in range(8):
        for h in range(2):
            ags[l, :, h * 128:(h + 1) * 128] = adj[h, pl.ds(l, 64, stride=8), :].astype(BF16)

    for t in (4, 3, 5, 2, 6, 1, 7):
        send(ags.at[zs[t]], ag.at[zh, (4 - t % 4) % 4], s5_s.at[t - 1], s5_r.at[t - 1], place(x, y, zs[t], c))
    ag[zh, 0] = ags[z]
    for t in range(1, 8):
        zq = lax.rem(z + 8 - t, 8)
        arrived(ag.at[zq // 4, (4 - t % 4) % 4], s5_r.at[t - 1])

    def share(q):
        cols = pl.ds(pl.multiple_of(q * 256, 256), 256)
        total = None
        for hh in range(2):
            a = ag[hh].reshape(256, 256)
            b = fyb[hh, :, :, cols].reshape(256, 256)
            term = jnp.dot(a, b, preferred_element_type=F32)
            total = term if total is None else total + term
        return total

    for t in (2, 1, 3):
        for r in range(2):
            psend[t, r] = share(r * 4 + xs[t]).astype(BF16)
            send(psend.at[t, r], pg.at[t, c], s6_s.at[t, r], s6_r.at[t, c], place(xs[t], y, z, r))
    psend[0, 0] = share(o * 4 + x).astype(BF16)
    send(psend.at[0, 0], pg.at[0, c], s6_s.at[0, 0], s6_r.at[0, 0], sib)
    pown[...] = share(c * 4 + x)
    arrived(pg.at[0, o], s6_r.at[0, 0])
    for t in range(1, 4):
        for cc in range(2):
            arrived(pg.at[t, cc], s6_r.at[t, cc])
    def three(r):
        return pg[1, r].astype(F32) + pg[2, r].astype(F32) + pg[3, r].astype(F32)

    pb[c] = (three(c) + pown[...]).astype(BF16)
    pb[o] = (three(o) + pg[0, o].astype(F32)).astype(BF16)

    def lines(q):
        cols = pl.ds(pl.multiple_of(q * 512, 512), 512)
        a = fxb[:, :, :, :, cols].reshape(512, 512)
        return lax.dot_general(a, pb[...].reshape(512, 256), (((0,), (0,)), ((), ())), preferred_element_type=F32)

    for t in (2, 1, 3):
        gsend[t - 1] = lines(ys[t]).astype(BF16)
        send(gsend.at[t - 1], gg.at[t - 1], s7_s.at[t - 1], s7_r.at[t - 1], place(x, ys[t], z, c))
    gown[...] = lines(y)
    for t in range(1, 4):
        arrived(gg.at[t - 1], s7_r.at[t - 1])
    gs[...] = (gown[...] + gg[0].astype(F32) + gg[1].astype(F32) + gg[2].astype(F32)).astype(BF16).reshape(8, 64, 256)

    for u in (2, 1, 3, 0):
        zq = lax.rem(zl + u, 4)
        for v in range(2):
            cq = o if v else c
            src = gs.at[zq * 2 + cq]
            if u == 0 and v == 0:
                continue
            send(src, go.at[z], s8_s.at[u, v], s8_r.at[z], place(x, y, c * 4 + zq, cq))
    own8 = pltpu.make_async_copy(gs.at[zl * 2 + c], go.at[z], s8_r.at[z])
    far8 = pltpu.make_async_remote_copy(
        src_ref=gs.at[zl * 2 + c], dst_ref=go.at[z], send_sem=s8_s.at[0, 0], recv_sem=s8_r.at[z],
        device_id=place(x, y, c * 4 + zl, c), device_id_type=MESH)

    @pl.when(zh == c)
    def _():
        own8.start()

    @pl.when(zh != c)
    def _():
        far8.start()

    for l in range(8):
        arrived(go.at[l], s8_r.at[l])
    for l in range(8):
        value = go[l].astype(F32)
        for h in range(2):
            nat[h, pl.ds(l, 64, stride=8), :] = value[:, h * 128:(h + 1) * 128]
    for h in range(2):
        ln = slice(h * 128, (h + 1) * 128)
        grad_v[:, :, ln] = ctl_v[:, :, ln].astype(F32) + nat[h].reshape(64, 8, 128)
    store_grad = pltpu.make_async_copy(grad_v, grad_out, loc_sem.at[8])
    store_grad.start()

    for copy in pending:
        copy.wait_send()

    @pl.when(zh != c)
    def _():
        far0.wait_send()
        far8.wait_send()

    store_end.wait()
    store_grad.wait()


def per_device(control, innovation, obs_weight, courant_x, courant_y, filter_x, filter_y):
    dma = lambda *shape: pltpu.SemaphoreType.DMA(shape)
    big = pltpu.VMEM((64, 8, 256), F32)
    half = pltpu.VMEM((2, 512, 128), F32)
    ext = pltpu.VMEM((2, 528, 128), F32)
    col = pltpu.VMEM((512, 128), F32)
    lev = pltpu.VMEM((8, 64, 256), BF16)
    halo = pltpu.VMEM((2, 8, 512), F32)
    scratch = [
        pltpu.VMEM((64, 8, 256), BF16), big, big, big, big, big, big,
        half, lev,
        pltpu.VMEM((32, 64, 256), BF16),
        pltpu.VMEM((2, 4, 4, 16, 2048), BF16),
        pltpu.VMEM((2, 8, 32, 2048), BF16),
        pltpu.VMEM((512, 256), F32),
        pltpu.VMEM((2, 256, 256), BF16),
        pltpu.VMEM((8, 256, 256), BF16),
        pltpu.VMEM((256, 512), F32),
        pltpu.VMEM((2, 4, 64, 256), BF16),
        lev,
        ext, halo, halo, col, col, ext, half, half, half, halo, halo, lev,
        pltpu.VMEM((2, 4, 64, 256), BF16),
        pltpu.VMEM((4, 2, 256, 256), BF16),
        pltpu.VMEM((256, 256), F32),
        pltpu.VMEM((4, 2, 256, 256), BF16),
        pltpu.VMEM((2, 256, 256), BF16),
        pltpu.VMEM((3, 512, 256), BF16),
        pltpu.VMEM((512, 256), F32),
        pltpu.VMEM((3, 512, 256), BF16),
        lev, lev,
        dma(9), dma(3), dma(3), dma(1), dma(1), dma(3), dma(3), dma(4), dma(4),
        dma(1), dma(1), dma(3), dma(3), dma(4), dma(4),
        dma(8), dma(8), dma(3, 4), dma(3, 4), dma(4, 2), dma(4, 2), dma(7), dma(7),
        dma(4), dma(4), dma(4), dma(4), dma(7), dma(7), dma(4, 2), dma(4, 2), dma(3), dma(3), dma(4, 2), dma(8),
    ]
    out = jax.ShapeDtypeStruct((64, 8, 256), F32)
    anywhere = pl.BlockSpec(memory_space=pl.ANY)
    return pl.pallas_call(
        kernel,
        out_shape=(out, out),
        in_specs=[anywhere] * 7,
        out_specs=(anywhere, anywhere),
        scratch_shapes=scratch,
        compiler_params=pltpu.CompilerParams(
            collective_id=0, has_side_effects=True, vmem_limit_bytes=40 * 1024 * 1024),
        cost_estimate=pl.CostEstimate(flops=2150000000, bytes_accessed=5000000, transcendentals=0),
    )(control, innovation, obs_weight, courant_x, courant_y,
      filter_x.reshape(4, 16, 2048), filter_y.reshape(8, 32, 2048))


def solution(mesh):
    grid = P("gx", None, "gy")
    placed = (grid, grid, grid, grid, grid, P("gx", None), P("gy", None))
    return jax.shard_map(
        per_device, mesh=mesh, in_specs=placed, out_specs=(grid, grid), check_vma=False)
```

```python
import jax
import jax.numpy as jnp
from jax import lax
from jax.experimental import pallas as pl
from jax.experimental.pallas import tpu as pltpu
from jax.sharding import PartitionSpec as P

MESH = pl.DeviceIdType.MESH
F32 = jnp.float32
BF16 = jnp.bfloat16
def place(x, y, z, c):
    return (y * 8 + lax.rem(z, 4) * 2 + c, (z // 4) * 4 + x)


def kernel(
    ctl, innov, weight, cou_x, cou_y, fx, fy,
    end_out, grad_out,
    ctl_v, inn_v, wei_v, cx_v, cy_v, end_v, grad_v,
    nat, snd0, cg, fxb, fyb, acc1, s1b, s1g, acc2, s2b, stg,
    st, hys, hyr, hl, hr, qx, py, mis, adj, hps, hpr, ags, ag,
    psend, pown, pg, pb, gsend, gown, gg, gs, go,
    loc_sem, f1_s, f1_r, fo_s, fo_r, f2_s, f2_r, fr_s, fr_r,
    g1_s, g1_r, g2_s, g2_r, gr_s, gr_r,
    s0_s, s0_r, s1_s, s1_r, s2_s, s2_r, s3_s, s3_r,
    h_s, h_r, k_s, k_r, s5_s, s5_r, s6_s, s6_r, s7_s, s7_r, s8_s, s8_r,
):
    gx = lax.axis_index("gx")
    gy = lax.axis_index("gy")
    y = gx // 8
    zl = lax.rem(gx // 2, 4)
    c = lax.rem(gx, 2)
    zh = gy // 4
    x = lax.rem(gy, 4)
    z = zh * 4 + zl
    o = 1 - c
    sib = place(x, y, z, o)
    e = y * 2 + c
    pending = []

    def send(src, dst, ssem, rsem, dev):
        copy = pltpu.make_async_remote_copy(
            src_ref=src, dst_ref=dst, send_sem=ssem, recv_sem=rsem,
            device_id=dev, device_id_type=MESH)
        copy.start()
        pending.append(copy)

    def arrived(dst, rsem):
        pltpu.make_async_copy(dst, dst, rsem).wait()

    xs = [lax.rem(x + t, 4) for t in range(4)]
    ys = [lax.rem(y + t, 4) for t in range(4)]
    zs = [lax.rem(z + t, 8) for t in range(8)]
    up = (lax.rem(gx + 1, 32), gy)
    down = (lax.rem(gx + 31, 32), gy)
    right = (gx, lax.rem(gy + 1, 8))
    left = (gx, lax.rem(gy + 7, 8))

    load_ctl = pltpu.make_async_copy(ctl, ctl_v, loc_sem.at[0])
    load_ctl.start()
    loads = [
        pltpu.make_async_copy(s, d, loc_sem.at[1 + i])
        for i, (s, d) in enumerate([
            (fx, fxb.at[c, 0]), (fy, fyb.at[zh]), (innov, inn_v),
            (weight, wei_v), (cou_x, cx_v), (cou_y, cy_v)])
    ]
    for load in loads:
        load.start()

    barrier = pltpu.get_barrier_semaphore()
    partners = [sib]
    for t in range(1, 8):
        partners += [place(x, y, zs[t], c), place(x, y, zs[t], o)]
    for t in range(1, 4):
        partners += [place(xs[t], y, z, c), place(xs[t], y, z, o)]
        partners += [place(x, ys[t], z, c)]
    partners += [up, down, left, right]
    for dev in partners:
        pl.semaphore_signal(barrier, inc=1, device_id=dev, device_id_type=MESH)

    load_ctl.wait()
    for h in range(2):
        nat[h] = ctl_v[:, :, h * 128:(h + 1) * 128].astype(F32).reshape(512, 128)
    for l in range(8):
        for h in range(2):
            snd0[h, l] = nat[h, pl.ds(l, 64, stride=8), :].astype(BF16)

    pl.semaphore_wait(barrier, len(partners))

    slot0 = zl * 2 + c
    for h in range(2):
        for t in (4, 3, 5, 2, 6, 1, 7):
            send(snd0.at[h, zs[t]], cg.at[h, gx], s0_s.at[h, t], s0_r.at[h, slot0], place(x, y, zs[t], zh))
    own0 = [pltpu.make_async_copy(snd0.at[h, z], cg.at[h, gx], s0_r.at[h, slot0]) for h in range(2)]
    far0 = [pltpu.make_async_remote_copy(
        src_ref=snd0.at[h, z], dst_ref=cg.at[h, gx], send_sem=s0_s.at[h, 0], recv_sem=s0_r.at[h, slot0],
        device_id=sib, device_id_type=MESH) for h in range(2)]

    @pl.when(zh == c)
    def _():
        own0[0].start()
        own0[1].start()

    @pl.when(zh != c)
    def _():
        far0[0].start()
        far0[1].start()

    x2 = xs[2]
    for d, k, q, dz in ((2, 0, x, 6), (2, 1, x2, 2), (1, 0, x, 7), (3, 0, x, 1), (1, 1, x2, 7), (3, 1, x2, 1)):
        send(fx.at[q], fxb.at[c, d, q], f1_s.at[d - 1, k], f1_r.at[d - 1, k], place(x, y, zs[dz], c))
    send(fx, fxb.at[c, 0], fo_s.at[0], fo_r.at[0], sib)

    for h in range(2):
        for s in range(4):
            for cc in range(2):
                arrived(cg.at[h, y * 8 + 2 * s + cc], s0_r.at[h, 2 * s + cc])
            block = cg.at[h, pl.ds(y * 8 + 2 * s, 2)]
            for t in (2, 1, 3):
                send(block, block, s1_s.at[h, t - 1, s], s1_r.at[h, t - 1, s], place(x, ys[t], z, c))

    for d in range(1, 4):
        arrived(fxb.at[c, d, x], f1_r.at[d - 1, 0])
    quarter = fxb.at[c, pl.ds(1, 3), x]
    for t in (1, 3):
        send(quarter, quarter, f2_s.at[t // 2], f2_r.at[t // 2], place(xs[t], y, z, c))
    send(quarter, quarter, fr_s.at[0], fr_r.at[0], sib)
    for d in range(1, 4):
        arrived(fxb.at[c, d, x2], f1_r.at[d - 1, 1])
    quarter = fxb.at[c, pl.ds(1, 3), x2]
    send(quarter, quarter, fr_s.at[2], fr_r.at[2], sib)

    send(fy.at[e], fyb.at[zh, e], g1_s.at[0], g1_r.at[0], place(x, y, zs[4], c))

    for t in (1, 3):
        part = fxb.at[c, pl.ds(1, 3), xs[4 - t]]
        arrived(part, f2_r.at[t // 2])
        send(part, part, fr_s.at[t], fr_r.at[t], sib)

    loads[0].wait()
    loads[1].wait()
    arrived(fxb.at[o, 0], fo_r.at[0])
    for t in range(4):
        arrived(fxb.at[o, pl.ds(1, 3), xs[(4 - t) % 4]], fr_r.at[t])

    def rows_dot(h, q):
        cols = pl.ds(pl.multiple_of(q * 512, 512), 512)
        a = fxb[:, :, :, :, cols].reshape(512, 512)
        b = cg[h, pl.ds(q * 8, 8)].reshape(512, 128)
        return jnp.dot(a, b, preferred_element_type=F32)

    mine = c * 4 + x
    for h in range(2):
        acc1[...] = rows_dot(h, y)
        for t in (3, 1, 2):
            yq = ys[4 - t]
            for s in range(4):
                arrived(cg.at[h, pl.ds(yq * 8 + 2 * s, 2)], s1_r.at[h, t - 1, s])
            if t != 2:
                acc1[...] += rows_dot(h, yq)
            else:
                s1b[h] = (acc1[...] + rows_dot(h, yq)).astype(BF16).reshape(2, 256, 128)
        for k, rows in ((0, pl.ds(0, 256)),) if h == 0 else ((1, pl.ds(0, 128)), (2, pl.ds(128, 128))):
            for t in (2, 1, 3):
                for r in range(2):
                    send(s1b.at[h, r, rows], s1g.at[h, mine, rows],
                         s2_s.at[k, t, r], s2_r.at[k, t, c], place(xs[t], y, z, r))
            send(s1b.at[h, o, rows], s1g.at[h, mine, rows], s2_s.at[k, 0, 0], s2_r.at[k, 0, 0], sib)
        s1g[h, mine] = s1b[h, c]

    zo = 1 - zh
    arrived(fyb.at[zo, e], g1_r.at[0])
    for t in (2, 1, 3):
        send(fyb.at[zo, e], fyb.at[zo, e], g2_s.at[t - 1], g2_r.at[t - 1], place(x, ys[t], z, c))
    send(fyb.at[zo, e], fyb.at[zo, e], gr_s.at[0], gr_r.at[0], sib)

    def cols_dot(h, q, hh, start, size):
        cols = pl.ds(pl.multiple_of(q * 256 + h * 128, 128), 128)
        b = fyb[hh, :, :, cols].reshape(256, 128)
        a = s1g[h, q, start:start + size, :]
        return lax.dot_general(a, b, (((1,), (1,)), ((), ())), preferred_element_type=F32)

    sources = [(0, 0, mine), (0, 0, o * 4 + x)]
    sources += [(t, cc, cc * 4 + xs[4 - t]) for t in (3, 1, 2) for cc in range(2)]
    for i, (t, cc, q) in enumerate(sources):
        if i:
            arrived(s1g.at[0, q], s2_r.at[0, t, cc])
        term = cols_dot(0, q, zh, 0, 256)
        acc2[zh] = acc2[zh] + term if i else term

    for t in (3, 1, 2):
        eq = ys[4 - t] * 2 + c
        arrived(fyb.at[zo, eq], g2_r.at[t - 1])
        send(fyb.at[zo, eq], fyb.at[zo, eq], gr_s.at[t], gr_r.at[t], sib)
    for t in range(4):
        arrived(fyb.at[zo, ys[(4 - t) % 4] * 2 + o], gr_r.at[t])
    for i, (t, cc, q) in enumerate(sources):
        term = cols_dot(0, q, zo, 0, 256)
        acc2[zo] = acc2[zo] + term if i else term

    for g in range(2):
        rows = pl.ds(g * 128, 128)
        for i, (t, cc, q) in enumerate(sources):
            if i:
                arrived(s1g.at[1, q, rows], s2_r.at[1 + g, t, cc])
            for hh in range(2):
                acc2[hh, rows] += cols_dot(1, q, hh, g * 128, 128)
        for hh in range(2):
            s2b[hh, 2 * g:2 * g + 2] = acc2[hh, rows].astype(BF16).reshape(2, 64, 256)
        for t in ((4, 5, 1) if g == 0 else (3, 2, 6, 7)):
            send(s2b.at[zs[t] // 4, t % 4], stg.at[z], s3_s.at[t - 1], s3_r.at[t - 1], place(x, y, zs[t], c))
    stg[z] = s2b[zh, 0]

    def spread(l):
        value = stg[l].astype(F32)
        for h in range(2):
            st[h, pl.ds(8 + l, 64, stride=8), :] = value[:, h * 128:(h + 1) * 128]

    for t in range(1, 8):
        arrived(stg.at[lax.rem(z + 8 - t, 8)], s3_r.at[t - 1])
    for l in range(8):
        spread(l)

    def edges(field, hsend, hrecv, hleft, hright, ssem, rsem, ref_first, ref_last):
        send(ref_first(0), ref_last(1), ssem.at[0], rsem.at[0], down)
        send(ref_last(0), ref_first(1), ssem.at[1], rsem.at[1], up)
        hsend[0] = field(0).T[0:8]
        send(hsend.at[0], hrecv.at[0], ssem.at[2], rsem.at[2], left)
        hsend[1] = field(1).T[120:128]
        send(hsend.at[1], hrecv.at[1], ssem.at[3], rsem.at[3], right)
        arrived(ref_last(1), rsem.at[0])
        arrived(ref_first(1), rsem.at[1])
        arrived(hrecv.at[0], rsem.at[2])
        arrived(hrecv.at[1], rsem.at[3])
        keep_r = jnp.where(gy == 7, 0.0, 1.0).astype(F32)
        keep_l = jnp.where(gy == 0, 0.0, 1.0).astype(F32)
        hright[...] = jnp.broadcast_to(hrecv[0, 0:1, :] * keep_r, (128, 512)).T
        hleft[...] = jnp.broadcast_to(hrecv[1, 7:8, :] * keep_l, (128, 512)).T

    def fringe(ref):
        first = lambda k: ref.at[:, pl.ds(8, 8)] if k == 0 else ref.at[:, pl.ds(0, 8)]
        last = lambda k: ref.at[:, pl.ds(512, 8)] if k == 0 else ref.at[:, pl.ds(520, 8)]
        return first, last

    def clear(ref):
        @pl.when(gx == 0)
        def _():
            ref[:, 0:8, :] = jnp.zeros((2, 8, 128), F32)

        @pl.when(gx == 31)
        def _():
            ref[:, 520:528, :] = jnp.zeros((2, 8, 128), F32)

    first, last = fringe(st)
    edges(lambda h: st[h, 8:520, :], hys, hyr, hl, hr, h_s, h_r, first, last)
    clear(st)
    for load in loads[2:]:
        load.wait()

    lane = lax.broadcasted_iota(jnp.int32, (64, 128), 1)

    def beside(v0, v1, left_halo, right_halo):
        f0, f1 = pltpu.roll(v0, 127, 1), pltpu.roll(v1, 127, 1)
        b0, b1 = pltpu.roll(v0, 1, 1), pltpu.roll(v1, 1, 1)
        after = (jnp.where(lane == 127, f1, f0), jnp.where(lane == 127, right_halo, f1))
        before = (jnp.where(lane == 0, left_halo, b0), jnp.where(lane == 0, b0, b1))
        return before, after

    @pl.loop(0, 8)
    def _(i):
        at = pl.multiple_of(i * 64, 64)
        xr = pl.ds(i * 8, 8)
        v = [st[h, pl.ds(at + 8, 64), :] for h in range(2)]
        before, after = beside(v[0], v[1], hl[pl.ds(at, 64), :], hr[pl.ds(at, 64), :])
        for h in range(2):
            ln = slice(h * 128, (h + 1) * 128)
            cx = cx_v[xr, :, ln].reshape(64, 128)
            cy = cy_v[xr, :, ln].reshape(64, 128)
            prev = st[h, pl.ds(at, 64), :]
            post = st[h, pl.ds(at + 16, 64), :]
            end = v[h] - cx * (post - prev) * 0.5 - cy * (after[h] - before[h]) * 0.5
            end_v[xr, :, ln] = end.reshape(8, 8, 128)
            m = wei_v[xr, :, ln].reshape(64, 128) * (end - inn_v[xr, :, ln].reshape(64, 128))
            mis[h, pl.ds(at, 64), :] = m
            qx[h, pl.ds(at + 8, 64), :] = cx * m
            py[h, pl.ds(at, 64), :] = cy * m

    store_end = pltpu.make_async_copy(end_v, end_out, loc_sem.at[7])
    store_end.start()

    first, last = fringe(qx)
    edges(lambda h: py[h], hps, hpr, hl, hr, k_s, k_r, first, last)
    clear(qx)

    @pl.loop(0, 8)
    def _(i):
        at = pl.multiple_of(i * 64, 64)
        v = [py[h, pl.ds(at, 64), :] for h in range(2)]
        before, after = beside(v[0], v[1], hl[pl.ds(at, 64), :], hr[pl.ds(at, 64), :])
        for h in range(2):
            prev = qx[h, pl.ds(at, 64), :]
            post = qx[h, pl.ds(at + 16, 64), :]
            adj[h, pl.ds(at, 64), :] = (
                mis[h, pl.ds(at, 64), :] + 0.5 * (post - prev) + 0.5 * (after[h] - before[h]))

    for l in range(8):
        for h in range(2):
            ags[l, :, h * 128:(h + 1) * 128] = adj[h, pl.ds(l, 64, stride=8), :].astype(BF16)

    for t in (4, 3, 7, 2, 6, 5, 1):
        send(ags.at[zs[t]], ag.at[zh, (4 - t % 4) % 4], s5_s.at[t - 1], s5_r.at[t - 1], place(x, y, zs[t], c))
    ag[zh, 0] = ags[z]

    def share(g, q):
        cols = pl.ds(pl.multiple_of(q * 256, 256), 256)
        total = None
        for hh in range(2):
            a = ag[hh, 2 * g:2 * g + 2].reshape(128, 256)
            b = fyb[hh, :, :, cols].reshape(256, 256)
            term = jnp.dot(a, b, preferred_element_type=F32)
            total = term if total is None else total + term
        return total

    targets = [(t, r, r * 4 + xs[t], place(xs[t], y, z, r)) for t in (2, 1, 3) for r in range(2)]
    targets += [(0, 0, o * 4 + x, sib)]

    def hand(h, k, rows):
        for t, r, q, dev in targets:
            send(psend.at[h, t, r, rows], pg.at[h, t, c, rows],
                 s6_s.at[k, t, r], s6_r.at[k, t, c], dev)

    for g in range(2):
        rows = pl.ds(g * 128, 128)
        for t in ((4, 3, 7) if g == 0 else (2, 6, 5, 1)):
            arrived(ag.at[zs[8 - t] // 4, (4 - t % 4) % 4], s5_r.at[t - 1])
        for t, r, q, dev in targets:
            value = share(g, q).astype(BF16)
            for h in range(2):
                psend[h, t, r, rows] = value[:, h * 128:(h + 1) * 128]
            send(psend.at[0, t, r, rows], pg.at[0, t, c, rows],
                 s6_s.at[g, t, r], s6_r.at[g, t, c], dev)
        value = share(g, mine)
        for h in range(2):
            pown[h, rows] = value[:, h * 128:(h + 1) * 128]
    hand(1, 2, pl.ds(0, 256))

    def lines(h, q):
        cols = pl.ds(pl.multiple_of(q * 512, 512), 512)
        a = fxb[:, :, :, :, cols].reshape(512, 512)
        b = pb[h].reshape(512, 128)
        return lax.dot_general(a, b, (((0,), (0,)), ((), ())), preferred_element_type=F32)

    def three(h, r):
        return pg[h, 1, r].astype(F32) + pg[h, 2, r].astype(F32) + pg[h, 3, r].astype(F32)

    for h in range(2):
        for k, rows in ((0, pl.ds(0, 128)), (1, pl.ds(128, 128))) if h == 0 else ((2, pl.ds(0, 256)),):
            arrived(pg.at[h, 0, o, rows], s6_r.at[k, 0, o])
            for t in range(1, 4):
                for cc in range(2):
                    arrived(pg.at[h, t, cc, rows], s6_r.at[k, t, cc])
        pb[h, c] = (three(h, c) + pown[h]).astype(BF16)
        pb[h, o] = (three(h, o) + pg[h, 0, o].astype(F32)).astype(BF16)
        for t in (2, 1, 3):
            gsend[h, t - 1] = lines(h, ys[t]).astype(BF16)
            send(gsend.at[h, t - 1], gg.at[h, t - 1], s7_s.at[h, t - 1], s7_r.at[h, t - 1], place(x, ys[t], z, c))
        gown[h] = lines(h, y)

    own8, far8 = [], []
    for h in range(2):
        for t in range(1, 4):
            arrived(gg.at[h, t - 1], s7_r.at[h, t - 1])
        total = gown[h] + gg[h, 0].astype(F32) + gg[h, 1].astype(F32) + gg[h, 2].astype(F32)
        gs[h] = total.astype(BF16).reshape(8, 64, 128)
        for u in (2, 1, 3, 0):
            zq = lax.rem(zl + u, 4)
            for v in range(2):
                cq = o if v else c
                if u or v:
                    send(gs.at[h, zq * 2 + cq], go.at[h, z], s8_s.at[h, u, v], s8_r.at[h, z],
                         place(x, y, c * 4 + zq, cq))
        src, dst = gs.at[h, zl * 2 + c], go.at[h, z]
        own8.append(pltpu.make_async_copy(src, dst, s8_r.at[h, z]))
        far8.append(pltpu.make_async_remote_copy(
            src_ref=src, dst_ref=dst, send_sem=s8_s.at[h, 0, 0], recv_sem=s8_r.at[h, z],
            device_id=place(x, y, c * 4 + zl, c), device_id_type=MESH))

        @pl.when(zh == c)
        def _():
            own8[h].start()

        @pl.when(zh != c)
        def _():
            far8[h].start()

    for h in range(2):
        ln = slice(h * 128, (h + 1) * 128)
        for l in range(8):
            arrived(go.at[h, l], s8_r.at[h, l])
        for l in range(8):
            nat[h, pl.ds(l, 64, stride=8), :] = go[h, l].astype(F32)
        grad_v[:, :, ln] = ctl_v[:, :, ln].astype(F32) + nat[h].reshape(64, 8, 128)
    store_grad = pltpu.make_async_copy(grad_v, grad_out, loc_sem.at[8])
    store_grad.start()

    for copy in pending:
        copy.wait_send()

    @pl.when(zh != c)
    def _():
        for h in range(2):
            far0[h].wait_send()
            far8[h].wait_send()

    store_end.wait()
    store_grad.wait()


def per_device(control, innovation, obs_weight, courant_x, courant_y, filter_x, filter_y):
    dma = lambda *shape: pltpu.SemaphoreType.DMA(shape)
    big = pltpu.VMEM((64, 8, 256), F32)
    half = pltpu.VMEM((2, 512, 128), F32)
    ext = pltpu.VMEM((2, 528, 128), F32)
    col = pltpu.VMEM((512, 128), F32)
    lev = pltpu.VMEM((8, 64, 256), BF16)
    levh = pltpu.VMEM((2, 8, 64, 128), BF16)
    halo = pltpu.VMEM((2, 8, 512), F32)
    planes = pltpu.VMEM((2, 4, 64, 256), BF16)
    shares = pltpu.VMEM((2, 4, 2, 256, 128), BF16)
    sums = pltpu.VMEM((2, 3, 512, 128), BF16)
    scratch = [
        pltpu.VMEM((64, 8, 256), BF16), big, big, big, big, big, big,
        half, levh,
        pltpu.VMEM((2, 32, 64, 128), BF16),
        pltpu.VMEM((2, 4, 4, 16, 2048), BF16),
        pltpu.VMEM((2, 8, 32, 2048), BF16),
        pltpu.VMEM((512, 128), F32),
        pltpu.VMEM((2, 2, 256, 128), BF16),
        pltpu.VMEM((2, 8, 256, 128), BF16),
        pltpu.VMEM((2, 256, 256), F32),
        planes, lev,
        ext, halo, halo, col, col, ext, half, half, half, halo, halo, lev, planes,
        shares,
        pltpu.VMEM((2, 256, 128), F32),
        shares,
        pltpu.VMEM((2, 2, 256, 128), BF16),
        sums,
        pltpu.VMEM((2, 512, 128), F32),
        sums, levh, levh,
        dma(9), dma(3, 2), dma(3, 2), dma(1), dma(1), dma(2), dma(2), dma(4), dma(4),
        dma(1), dma(1), dma(3), dma(3), dma(4), dma(4),
        dma(2, 8), dma(2, 8), dma(2, 3, 4), dma(2, 3, 4), dma(3, 4, 2), dma(3, 4, 2), dma(7), dma(7),
        dma(4), dma(4), dma(4), dma(4), dma(7), dma(7), dma(3, 4, 2), dma(3, 4, 2),
        dma(2, 3), dma(2, 3), dma(2, 4, 2), dma(2, 8),
    ]
    out = jax.ShapeDtypeStruct((64, 8, 256), F32)
    anywhere = pl.BlockSpec(memory_space=pl.ANY)
    return pl.pallas_call(
        kernel,
        out_shape=(out, out),
        in_specs=[anywhere] * 7,
        out_specs=(anywhere, anywhere),
        scratch_shapes=scratch,
        compiler_params=pltpu.CompilerParams(
            collective_id=0, has_side_effects=True, vmem_limit_bytes=60 * 1024 * 1024),
        cost_estimate=pl.CostEstimate(flops=2150000000, bytes_accessed=5000000, transcendentals=0),
    )(control, innovation, obs_weight, courant_x, courant_y,
      filter_x.reshape(4, 16, 2048), filter_y.reshape(8, 32, 2048))


def solution(mesh):
    grid = P("gx", None, "gy")
    placed = (grid, grid, grid, grid, grid, P("gx", None), P("gy", None))
    return jax.shard_map(
        per_device, mesh=mesh, in_specs=placed, out_specs=(grid, grid), check_vma=False)
```

```python
import jax
import jax.numpy as jnp
from jax import lax
from jax.experimental import pallas as pl
from jax.experimental.pallas import tpu as pltpu
from jax.sharding import PartitionSpec as P

MESH = pl.DeviceIdType.MESH
F32 = jnp.float32
BF16 = jnp.bfloat16
def place(x, y, z, c):
    return (y * 8 + lax.rem(z, 4) * 2 + c, (z // 4) * 4 + x)


def kernel(
    ctl, innov, weight, cou_x, cou_y, fx, fy,
    end_out, grad_out,
    ctl_v, inn_v, wei_v, cx_v, cy_v,
    nat, snd0, cg, fxb, fyb, s1b, s1g, acc2, s2b, stg,
    st, hys, hyr, hl, hr, qx, py, mis, adj, hps, hpr, ags, ag,
    psend, pown, pg, pb, gsend, gown, gg, gs, go,
    loc_sem, f1_s, f1_r, fo_s, fo_r, f2_s, f2_r, fr_s, fr_r,
    g1_s, g1_r, g2_s, g2_r, gr_s, gr_r,
    s0_s, s0_r, s1_s, s1_r, s2_s, s2_r, s3_s, s3_r,
    h_s, h_r, k_s, k_r, s5_s, s5_r, s6_s, s6_r, s7_s, s7_r, s8_s, s8_r,
):
    gx = lax.axis_index("gx")
    gy = lax.axis_index("gy")
    y = gx // 8
    zl = lax.rem(gx // 2, 4)
    c = lax.rem(gx, 2)
    zh = gy // 4
    x = lax.rem(gy, 4)
    z = zh * 4 + zl
    o = 1 - c
    sib = place(x, y, z, o)
    e = y * 2 + c
    pending = []

    def send(src, dst, ssem, rsem, dev):
        copy = pltpu.make_async_remote_copy(
            src_ref=src, dst_ref=dst, send_sem=ssem, recv_sem=rsem,
            device_id=dev, device_id_type=MESH)
        copy.start()
        pending.append(copy)

    def arrived(dst, rsem):
        pltpu.make_async_copy(dst, dst, rsem).wait()

    xs = [lax.rem(x + t, 4) for t in range(4)]
    ys = [lax.rem(y + t, 4) for t in range(4)]
    zs = [lax.rem(z + t, 8) for t in range(8)]
    up = (lax.rem(gx + 1, 32), gy)
    down = (lax.rem(gx + 31, 32), gy)
    right = (gx, lax.rem(gy + 1, 8))
    left = (gx, lax.rem(gy + 7, 8))

    load_ctl = pltpu.make_async_copy(ctl, ctl_v, loc_sem.at[0])
    load_ctl.start()
    loads = [
        pltpu.make_async_copy(s, d, loc_sem.at[1 + i])
        for i, (s, d) in enumerate([
            (fx, fxb.at[c, 0]), (fy, fyb.at[zh]), (innov, inn_v),
            (weight, wei_v), (cou_x, cx_v), (cou_y, cy_v)])
    ]
    for load in loads:
        load.start()

    barrier = pltpu.get_barrier_semaphore()
    partners = [sib]
    for t in range(1, 8):
        partners += [place(x, y, zs[t], c), place(x, y, zs[t], o)]
    for t in range(1, 4):
        partners += [place(xs[t], y, z, c), place(xs[t], y, z, o)]
        partners += [place(x, ys[t], z, c)]
    partners += [up, down, left, right]
    for dev in partners:
        pl.semaphore_signal(barrier, inc=1, device_id=dev, device_id_type=MESH)

    load_ctl.wait()
    for h in range(2):
        nat[h] = ctl_v[:, :, h * 128:(h + 1) * 128].astype(F32).reshape(512, 128)
    for l in range(8):
        for h in range(2):
            snd0[h, l] = nat[h, pl.ds(l, 64, stride=8), :].astype(BF16)

    pl.semaphore_wait(barrier, len(partners))

    slot0 = zl * 2 + c
    for h in range(2):
        for t in (4, 3, 5, 2, 6, 1, 7):
            send(snd0.at[h, zs[t]], cg.at[h, gx], s0_s.at[h, t], s0_r.at[h, slot0], place(x, y, zs[t], zh))
    own0 = [pltpu.make_async_copy(snd0.at[h, z], cg.at[h, gx], s0_r.at[h, slot0]) for h in range(2)]
    far0 = [pltpu.make_async_remote_copy(
        src_ref=snd0.at[h, z], dst_ref=cg.at[h, gx], send_sem=s0_s.at[h, 0], recv_sem=s0_r.at[h, slot0],
        device_id=sib, device_id_type=MESH) for h in range(2)]

    @pl.when(zh == c)
    def _():
        own0[0].start()
        own0[1].start()

    @pl.when(zh != c)
    def _():
        far0[0].start()
        far0[1].start()

    send(fx, fxb.at[c, 0], fo_s.at[0], fo_r.at[0], sib)

    def ring(h):
        for s in range(4):
            for cc in range(2):
                arrived(cg.at[h, y * 8 + 2 * s + cc], s0_r.at[h, 2 * s + cc])
            block = cg.at[h, pl.ds(y * 8 + 2 * s, 2)]
            for t in (2, 1, 3):
                send(block, block, s1_s.at[h, t - 1, s], s1_r.at[h, t - 1, s], place(x, ys[t], z, c))

    ring(0)

    x2 = xs[2]
    for d, k, q, dz in ((2, 0, x, 6), (1, 0, x, 7), (3, 0, x, 1), (2, 1, x2, 2), (1, 1, x2, 7), (3, 1, x2, 1)):
        send(fx.at[q], fxb.at[c, d, q], f1_s.at[d - 1, k], f1_r.at[d - 1, k], place(x, y, zs[dz], c))

    ring(1)

    for d in range(1, 4):
        arrived(fxb.at[c, d, x], f1_r.at[d - 1, 0])
    quarter = fxb.at[c, pl.ds(1, 3), x]
    for t in (1, 3):
        send(quarter, quarter, f2_s.at[t // 2], f2_r.at[t // 2], place(xs[t], y, z, c))
    send(quarter, quarter, fr_s.at[0], fr_r.at[0], sib)
    for d in range(1, 4):
        arrived(fxb.at[c, d, x2], f1_r.at[d - 1, 1])
    quarter = fxb.at[c, pl.ds(1, 3), x2]
    send(quarter, quarter, fr_s.at[2], fr_r.at[2], sib)

    send(fy.at[e], fyb.at[zh, e], g1_s.at[0], g1_r.at[0], place(x, y, zs[4], c))

    mine = c * 4 + x

    def smooth(d):
        a = fxb[:, d].reshape(128, 2048)
        for h in range(2):
            v = jnp.dot(a, cg[h].reshape(2048, 128), preferred_element_type=F32)
            s1b[:, d, :, h * 128:(h + 1) * 128] = v.astype(BF16).reshape(2, 64, 128)
        rows = pl.ds(d * 64, 64)
        for t in (2, 1, 3):
            for r in range(2):
                send(s1b.at[r, d], s1g.at[mine, rows],
                     s2_s.at[d, t, r], s2_r.at[d, t, c], place(xs[t], y, z, r))
        send(s1b.at[o, d], s1g.at[mine, rows], s2_s.at[d, 0, 0], s2_r.at[d, 0, 0], sib)
        s1g[mine, rows] = s1b[c, d]

    for h in range(2):
        for t in (3, 1, 2):
            for s in range(4):
                arrived(cg.at[h, pl.ds(ys[4 - t] * 8 + 2 * s, 2)], s1_r.at[h, t - 1, s])
    loads[0].wait()
    loads[1].wait()
    arrived(fxb.at[o, 0], fo_r.at[0])
    smooth(0)
    for t in (1, 3):
        part = fxb.at[c, pl.ds(1, 3), xs[4 - t]]
        arrived(part, f2_r.at[t // 2])
        send(part, part, fr_s.at[t], fr_r.at[t], sib)
    for t in range(4):
        arrived(fxb.at[o, pl.ds(1, 3), xs[(4 - t) % 4]], fr_r.at[t])
    smooth(1)
    smooth(2)
    smooth(3)

    zo = 1 - zh
    arrived(fyb.at[zo, e], g1_r.at[0])
    for t in (2, 1, 3):
        send(fyb.at[zo, e], fyb.at[zo, e], g2_s.at[t - 1], g2_r.at[t - 1], place(x, ys[t], z, c))
    send(fyb.at[zo, e], fyb.at[zo, e], gr_s.at[0], gr_r.at[0], sib)

    def cols_dot(q, hh, g):
        cols = pl.ds(pl.multiple_of(q * 256, 256), 256)
        b = fyb[hh, :, :, cols].reshape(256, 256)
        a = s1g[q, g * 128:(g + 1) * 128, :]
        return lax.dot_general(a, b, (((1,), (1,)), ((), ())), preferred_element_type=F32)

    for t in (3, 1, 2):
        eq = ys[4 - t] * 2 + c
        arrived(fyb.at[zo, eq], g2_r.at[t - 1])
        send(fyb.at[zo, eq], fyb.at[zo, eq], gr_s.at[t], gr_r.at[t], sib)
    for t in range(4):
        arrived(fyb.at[zo, ys[(4 - t) % 4] * 2 + o], gr_r.at[t])
    sources = [(0, 0, mine), (0, 0, o * 4 + x)]
    sources += [(t, cc, cc * 4 + xs[4 - t]) for t in (3, 1, 2) for cc in range(2)]

    for g in range(2):
        for i, (t, cc, q) in enumerate(sources):
            if i:
                for d in (2 * g, 2 * g + 1):
                    arrived(s1g.at[q, pl.ds(d * 64, 64)], s2_r.at[d, t, cc])
            for hh in range(2):
                term = cols_dot(q, hh, g)
                if i == 0:
                    acc2[hh] = term
                elif i < 7:
                    acc2[hh] += term
                else:
                    s2b[hh, 2 * g:2 * g + 2] = (acc2[hh] + term).astype(BF16).reshape(2, 64, 256)
        for t in ((4, 5, 1) if g == 0 else (3, 2, 6, 7)):
            send(s2b.at[zs[t] // 4, t % 4], stg.at[z], s3_s.at[t - 1], s3_r.at[t - 1], place(x, y, zs[t], c))
    stg[z] = s2b[zh, 0]

    def spread(l):
        value = stg[l].astype(F32)
        for h in range(2):
            st[h, pl.ds(8 + l, 64, stride=8), :] = value[:, h * 128:(h + 1) * 128]

    for t in range(1, 8):
        arrived(stg.at[lax.rem(z + 8 - t, 8)], s3_r.at[t - 1])
    for l in range(8):
        spread(l)

    def edges(field, hsend, hrecv, hleft, hright, ssem, rsem, ref_first, ref_last):
        send(ref_first(0), ref_last(1), ssem.at[0], rsem.at[0], down)
        send(ref_last(0), ref_first(1), ssem.at[1], rsem.at[1], up)
        hsend[0] = field(0).T[0:8]
        send(hsend.at[0], hrecv.at[0], ssem.at[2], rsem.at[2], left)
        hsend[1] = field(1).T[120:128]
        send(hsend.at[1], hrecv.at[1], ssem.at[3], rsem.at[3], right)
        arrived(ref_last(1), rsem.at[0])
        arrived(ref_first(1), rsem.at[1])
        arrived(hrecv.at[0], rsem.at[2])
        arrived(hrecv.at[1], rsem.at[3])
        keep_r = jnp.where(gy == 7, 0.0, 1.0).astype(F32)
        keep_l = jnp.where(gy == 0, 0.0, 1.0).astype(F32)
        hright[...] = jnp.broadcast_to(hrecv[0, 0:1, :] * keep_r, (128, 512)).T
        hleft[...] = jnp.broadcast_to(hrecv[1, 7:8, :] * keep_l, (128, 512)).T

    def fringe(ref):
        first = lambda k: ref.at[:, pl.ds(8, 8)] if k == 0 else ref.at[:, pl.ds(0, 8)]
        last = lambda k: ref.at[:, pl.ds(512, 8)] if k == 0 else ref.at[:, pl.ds(520, 8)]
        return first, last

    def clear(ref):
        @pl.when(gx == 0)
        def _():
            ref[:, 0:8, :] = jnp.zeros((2, 8, 128), F32)

        @pl.when(gx == 31)
        def _():
            ref[:, 520:528, :] = jnp.zeros((2, 8, 128), F32)

    first, last = fringe(st)
    edges(lambda h: st[h, 8:520, :], hys, hyr, hl, hr, h_s, h_r, first, last)
    clear(st)
    for load in loads[2:]:
        load.wait()

    lane = lax.broadcasted_iota(jnp.int32, (64, 128), 1)

    def beside(v0, v1, left_halo, right_halo):
        f0, f1 = pltpu.roll(v0, 127, 1), pltpu.roll(v1, 127, 1)
        b0, b1 = pltpu.roll(v0, 1, 1), pltpu.roll(v1, 1, 1)
        after = (jnp.where(lane == 127, f1, f0), jnp.where(lane == 127, right_halo, f1))
        before = (jnp.where(lane == 0, left_halo, b0), jnp.where(lane == 0, b0, b1))
        return before, after

    @pl.loop(0, 8)
    def _(i):
        at = pl.multiple_of(i * 64, 64)
        xr = pl.ds(i * 8, 8)
        v = [st[h, pl.ds(at + 8, 64), :] for h in range(2)]
        before, after = beside(v[0], v[1], hl[pl.ds(at, 64), :], hr[pl.ds(at, 64), :])
        for h in range(2):
            ln = slice(h * 128, (h + 1) * 128)
            cx = cx_v[xr, :, ln].reshape(64, 128)
            cy = cy_v[xr, :, ln].reshape(64, 128)
            prev = st[h, pl.ds(at, 64), :]
            post = st[h, pl.ds(at + 16, 64), :]
            end = v[h] - cx * (post - prev) * 0.5 - cy * (after[h] - before[h]) * 0.5
            end_out[xr, :, ln] = end.reshape(8, 8, 128)
            m = wei_v[xr, :, ln].reshape(64, 128) * (end - inn_v[xr, :, ln].reshape(64, 128))
            mis[h, pl.ds(at, 64), :] = m
            qx[h, pl.ds(at + 8, 64), :] = cx * m
            py[h, pl.ds(at, 64), :] = cy * m

    first, last = fringe(qx)
    edges(lambda h: py[h], hps, hpr, hl, hr, k_s, k_r, first, last)
    clear(qx)

    @pl.loop(0, 8)
    def _(i):
        at = pl.multiple_of(i * 64, 64)
        v = [py[h, pl.ds(at, 64), :] for h in range(2)]
        before, after = beside(v[0], v[1], hl[pl.ds(at, 64), :], hr[pl.ds(at, 64), :])
        for h in range(2):
            prev = qx[h, pl.ds(at, 64), :]
            post = qx[h, pl.ds(at + 16, 64), :]
            adj[h, pl.ds(at, 64), :] = (
                mis[h, pl.ds(at, 64), :] + 0.5 * (post - prev) + 0.5 * (after[h] - before[h]))

    for l in range(8):
        for h in range(2):
            ags[l, :, h * 128:(h + 1) * 128] = adj[h, pl.ds(l, 64, stride=8), :].astype(BF16)

    for t in (4, 3, 7, 2, 6, 5, 1):
        send(ags.at[zs[t]], ag.at[zh, (4 - t % 4) % 4], s5_s.at[t - 1], s5_r.at[t - 1], place(x, y, zs[t], c))
    ag[zh, 0] = ags[z]

    def share(g, q):
        cols = pl.ds(pl.multiple_of(q * 256, 256), 256)
        total = None
        for hh in range(2):
            a = ag[hh, 2 * g:2 * g + 2].reshape(128, 256)
            b = fyb[hh, :, :, cols].reshape(256, 256)
            term = jnp.dot(a, b, preferred_element_type=F32)
            total = term if total is None else total + term
        return total

    targets = [(t, r, r * 4 + xs[t], place(xs[t], y, z, r)) for t in (2, 1, 3) for r in range(2)]
    targets += [(0, 0, o * 4 + x, sib)]

    def hand(h, k, rows):
        for t, r, q, dev in targets:
            send(psend.at[h, t, r, rows], pg.at[h, t, c, rows],
                 s6_s.at[k, t, r], s6_r.at[k, t, c], dev)

    for g in range(2):
        rows = pl.ds(g * 128, 128)
        for t in ((4, 3, 7) if g == 0 else (2, 6, 5, 1)):
            arrived(ag.at[zs[8 - t] // 4, (4 - t % 4) % 4], s5_r.at[t - 1])
        for t, r, q, dev in targets:
            value = share(g, q).astype(BF16)
            for h in range(2):
                psend[h, t, r, rows] = value[:, h * 128:(h + 1) * 128]
            send(psend.at[0, t, r, rows], pg.at[0, t, c, rows],
                 s6_s.at[g, t, r], s6_r.at[g, t, c], dev)
        value = share(g, mine)
        for h in range(2):
            pown[h, rows] = value[:, h * 128:(h + 1) * 128]

    def lines(h, q):
        cols = pl.ds(pl.multiple_of(q * 512, 512), 512)
        a = fxb[:, :, :, :, cols].reshape(512, 512)
        b = pb[h].reshape(512, 128)
        return lax.dot_general(a, b, (((0,), (0,)), ((), ())), preferred_element_type=F32)

    def three(h, r):
        return pg[h, 1, r].astype(F32) + pg[h, 2, r].astype(F32) + pg[h, 3, r].astype(F32)

    for h in range(2):
        for k, rows in ((0, pl.ds(0, 128)), (1, pl.ds(128, 128))) if h == 0 else ((2, pl.ds(0, 256)),):
            arrived(pg.at[h, 0, o, rows], s6_r.at[k, 0, o])
            for t in (1, 3, 2):
                for cc in range(2):
                    arrived(pg.at[h, t, cc, rows], s6_r.at[k, t, cc])
            if k == 0:
                hand(1, 2, pl.ds(0, 256))
        pb[h, c] = (three(h, c) + pown[h]).astype(BF16)
        pb[h, o] = (three(h, o) + pg[h, 0, o].astype(F32)).astype(BF16)
        for t in (2, 1, 3):
            gsend[h, t - 1] = lines(h, ys[t]).astype(BF16)
            send(gsend.at[h, t - 1], gg.at[h, t - 1], s7_s.at[h, t - 1], s7_r.at[h, t - 1], place(x, ys[t], z, c))
        gown[h] = lines(h, y)

    own8, far8 = [], []
    for h in range(2):
        for t in range(1, 4):
            arrived(gg.at[h, t - 1], s7_r.at[h, t - 1])
        total = gown[h] + gg[h, 0].astype(F32) + gg[h, 1].astype(F32) + gg[h, 2].astype(F32)
        gs[h] = total.astype(BF16).reshape(8, 64, 128)
        for u in (2, 1, 3, 0):
            zq = lax.rem(zl + u, 4)
            for v in range(2):
                cq = o if v else c
                if u or v:
                    send(gs.at[h, zq * 2 + cq], go.at[h, z], s8_s.at[h, u, v], s8_r.at[h, z],
                         place(x, y, c * 4 + zq, cq))
        src, dst = gs.at[h, zl * 2 + c], go.at[h, z]
        own8.append(pltpu.make_async_copy(src, dst, s8_r.at[h, z]))
        far8.append(pltpu.make_async_remote_copy(
            src_ref=src, dst_ref=dst, send_sem=s8_s.at[h, 0, 0], recv_sem=s8_r.at[h, z],
            device_id=place(x, y, c * 4 + zl, c), device_id_type=MESH))

        @pl.when(zh == c)
        def _():
            own8[h].start()

        @pl.when(zh != c)
        def _():
            far8[h].start()

    for h in range(2):
        ln = slice(h * 128, (h + 1) * 128)
        for l in range(8):
            arrived(go.at[h, l], s8_r.at[h, l])
        for l in range(8):
            nat[h, pl.ds(l, 64, stride=8), :] = go[h, l].astype(F32)
        grad_out[:, :, ln] = ctl_v[:, :, ln].astype(F32) + nat[h].reshape(64, 8, 128)
    for copy in pending:
        copy.wait_send()

    @pl.when(zh != c)
    def _():
        for h in range(2):
            far0[h].wait_send()
            far8[h].wait_send()


def per_device(control, innovation, obs_weight, courant_x, courant_y, filter_x, filter_y):
    dma = lambda *shape: pltpu.SemaphoreType.DMA(shape)
    big = pltpu.VMEM((64, 8, 256), F32)
    half = pltpu.VMEM((2, 512, 128), F32)
    ext = pltpu.VMEM((2, 528, 128), F32)
    col = pltpu.VMEM((512, 128), F32)
    lev = pltpu.VMEM((8, 64, 256), BF16)
    levh = pltpu.VMEM((2, 8, 64, 128), BF16)
    halo = pltpu.VMEM((2, 8, 512), F32)
    planes = pltpu.VMEM((2, 4, 64, 256), BF16)
    shares = pltpu.VMEM((2, 4, 2, 256, 128), BF16)
    sums = pltpu.VMEM((2, 3, 512, 128), BF16)
    scratch = [
        pltpu.VMEM((64, 8, 256), BF16), big, big, big, big,
        half, levh,
        pltpu.VMEM((2, 32, 64, 128), BF16),
        pltpu.VMEM((2, 4, 4, 16, 2048), BF16),
        pltpu.VMEM((2, 8, 32, 2048), BF16),
        pltpu.VMEM((2, 4, 64, 256), BF16),
        pltpu.VMEM((8, 256, 256), BF16),
        pltpu.VMEM((2, 128, 256), F32),
        planes, lev,
        ext, halo, halo, col, col, ext, half, half, half, halo, halo, lev, planes,
        shares,
        pltpu.VMEM((2, 256, 128), F32),
        shares,
        pltpu.VMEM((2, 2, 256, 128), BF16),
        sums,
        pltpu.VMEM((2, 512, 128), F32),
        sums, levh, levh,
        dma(7), dma(3, 2), dma(3, 2), dma(1), dma(1), dma(2), dma(2), dma(4), dma(4),
        dma(1), dma(1), dma(3), dma(3), dma(4), dma(4),
        dma(2, 8), dma(2, 8), dma(2, 3, 4), dma(2, 3, 4), dma(4, 4, 2), dma(4, 4, 2), dma(7), dma(7),
        dma(4), dma(4), dma(4), dma(4), dma(7), dma(7), dma(3, 4, 2), dma(3, 4, 2),
        dma(2, 3), dma(2, 3), dma(2, 4, 2), dma(2, 8),
    ]
    out = pltpu.VMEM((64, 8, 256), F32)
    anywhere = pl.BlockSpec(memory_space=pl.ANY)
    return pl.pallas_call(
        kernel,
        out_shape=(out, out),
        in_specs=[anywhere] * 7,
        out_specs=(pl.BlockSpec(memory_space=pltpu.VMEM),) * 2,
        scratch_shapes=scratch,
        compiler_params=pltpu.CompilerParams(
            collective_id=0, has_side_effects=True, vmem_limit_bytes=62 * 1024 * 1024),
        cost_estimate=pl.CostEstimate(flops=2150000000, bytes_accessed=5000000, transcendentals=0),
    )(control, innovation, obs_weight, courant_x, courant_y,
      filter_x.reshape(4, 16, 2048), filter_y.reshape(8, 32, 2048))


def solution(mesh):
    grid = P("gx", None, "gy")
    placed = (grid, grid, grid, grid, grid, P("gx", None), P("gy", None))
    return jax.shard_map(
        per_device, mesh=mesh, in_specs=placed, out_specs=(grid, grid), check_vma=False)
```

```python
import jax
import jax.numpy as jnp
from jax import lax
from jax.experimental import pallas as pl
from jax.experimental.pallas import tpu as pltpu
from jax.sharding import PartitionSpec as P

MESH = pl.DeviceIdType.MESH
F32 = jnp.float32
BF16 = jnp.bfloat16
def place(x, y, z, c):
    return (y * 8 + lax.rem(z, 4) * 2 + c, (z // 4) * 4 + x)


def kernel(
    ctl, innov, weight, cou_x, cou_y, fx, fy,
    end_out, grad_out,
    ctl_v, inn_v, wei_v, cx_v, cy_v,
    nat, snd0, cg, fxb, fyb, s1b, s1g, acc2, s2b, stg,
    st, hys, hyr, cor, frow, fcs, fcr, hl, hr, ql, qr, qx, py, mis, adj, ags, ag,
    psend, pown, pg, pb, gsend, gown, gg, gs, go,
    loc_sem, f1_s, f1_r, fo_s, fo_r, f2_s, f2_r, fr_s, fr_r,
    g1_s, g1_r, g2_s, g2_r, gr_s, gr_r,
    s0_s, s0_r, s1_s, s1_r, s2_s, s2_r, s3_s, s3_r,
    h_s, h_r, fw_s, fw_r, fc_s, fc_r, s5_s, s5_r, s6_s, s6_r, s7_s, s7_r, s8_s, s8_r,
):
    gx = lax.axis_index("gx")
    gy = lax.axis_index("gy")
    y = gx // 8
    zl = lax.rem(gx // 2, 4)
    c = lax.rem(gx, 2)
    zh = gy // 4
    x = lax.rem(gy, 4)
    z = zh * 4 + zl
    o = 1 - c
    sib = place(x, y, z, o)
    e = y * 2 + c
    pending = []

    def send(src, dst, ssem, rsem, dev):
        copy = pltpu.make_async_remote_copy(
            src_ref=src, dst_ref=dst, send_sem=ssem, recv_sem=rsem,
            device_id=dev, device_id_type=MESH)
        copy.start()
        pending.append(copy)

    def arrived(dst, rsem):
        pltpu.make_async_copy(dst, dst, rsem).wait()

    xs = [lax.rem(x + t, 4) for t in range(4)]
    ys = [lax.rem(y + t, 4) for t in range(4)]
    zs = [lax.rem(z + t, 8) for t in range(8)]
    up = (lax.rem(gx + 1, 32), gy)
    down = (lax.rem(gx + 31, 32), gy)
    right = (gx, lax.rem(gy + 1, 8))
    left = (gx, lax.rem(gy + 7, 8))
    corners = [(up[0], right[1]), (up[0], left[1]), (down[0], right[1]), (down[0], left[1])]

    load_ctl = pltpu.make_async_copy(ctl, ctl_v, loc_sem.at[0])
    load_ctl.start()
    loads = [
        pltpu.make_async_copy(s, d, loc_sem.at[1 + i])
        for i, (s, d) in enumerate([
            (fx, fxb.at[c, 0]), (fy, fyb.at[zh]), (innov, inn_v),
            (weight, wei_v), (cou_x, cx_v), (cou_y, cy_v)])
    ]
    for load in loads:
        load.start()

    barrier = pltpu.get_barrier_semaphore()
    partners = [sib]
    for t in range(1, 8):
        partners += [place(x, y, zs[t], c), place(x, y, zs[t], o)]
    for t in range(1, 4):
        partners += [place(xs[t], y, z, c), place(xs[t], y, z, o)]
        partners += [place(x, ys[t], z, c)]
    partners += [up, down, left, right] + corners
    for dev in partners:
        pl.semaphore_signal(barrier, inc=1, device_id=dev, device_id_type=MESH)

    load_ctl.wait()
    for h in range(2):
        nat[h] = ctl_v[:, :, h * 128:(h + 1) * 128].astype(F32).reshape(512, 128)
    for l in range(8):
        for h in range(2):
            snd0[h, l] = nat[h, pl.ds(l, 64, stride=8), :].astype(BF16)

    pl.semaphore_wait(barrier, len(partners))

    slot0 = zl * 2 + c
    for h in range(2):
        for t in (4, 3, 5, 2, 6, 1, 7):
            send(snd0.at[h, zs[t]], cg.at[h, gx], s0_s.at[h, t], s0_r.at[h, slot0], place(x, y, zs[t], zh))
    own0 = [pltpu.make_async_copy(snd0.at[h, z], cg.at[h, gx], s0_r.at[h, slot0]) for h in range(2)]
    far0 = [pltpu.make_async_remote_copy(
        src_ref=snd0.at[h, z], dst_ref=cg.at[h, gx], send_sem=s0_s.at[h, 0], recv_sem=s0_r.at[h, slot0],
        device_id=sib, device_id_type=MESH) for h in range(2)]

    @pl.when(zh == c)
    def _():
        own0[0].start()
        own0[1].start()

    @pl.when(zh != c)
    def _():
        far0[0].start()
        far0[1].start()

    send(fx, fxb.at[c, 0], fo_s.at[0], fo_r.at[0], sib)

    def ring(h):
        for s in range(4):
            for cc in range(2):
                arrived(cg.at[h, y * 8 + 2 * s + cc], s0_r.at[h, 2 * s + cc])
            block = cg.at[h, pl.ds(y * 8 + 2 * s, 2)]
            for t in (2, 1, 3):
                send(block, block, s1_s.at[h, t - 1, s], s1_r.at[h, t - 1, s], place(x, ys[t], z, c))

    ring(0)

    x2 = xs[2]
    for d, k, q, dz in ((2, 0, x, 6), (1, 0, x, 7), (3, 0, x, 1), (2, 1, x2, 2), (1, 1, x2, 7), (3, 1, x2, 1)):
        send(fx.at[q], fxb.at[c, d, q], f1_s.at[d - 1, k], f1_r.at[d - 1, k], place(x, y, zs[dz], c))

    ring(1)

    for d in range(1, 4):
        arrived(fxb.at[c, d, x], f1_r.at[d - 1, 0])
    quarter = fxb.at[c, pl.ds(1, 3), x]
    for t in (1, 3):
        send(quarter, quarter, f2_s.at[t // 2], f2_r.at[t // 2], place(xs[t], y, z, c))
    send(quarter, quarter, fr_s.at[0], fr_r.at[0], sib)
    for d in range(1, 4):
        arrived(fxb.at[c, d, x2], f1_r.at[d - 1, 1])
    quarter = fxb.at[c, pl.ds(1, 3), x2]
    send(quarter, quarter, fr_s.at[2], fr_r.at[2], sib)

    send(fy.at[e], fyb.at[zh, e], g1_s.at[0], g1_r.at[0], place(x, y, zs[4], c))

    mine = c * 4 + x

    def smooth(d):
        a = fxb[:, d].reshape(128, 2048)
        for h in range(2):
            v = jnp.dot(a, cg[h].reshape(2048, 128), preferred_element_type=F32)
            s1b[:, d, :, h * 128:(h + 1) * 128] = v.astype(BF16).reshape(2, 64, 128)
        rows = pl.ds(d * 64, 64)
        for t in (2, 1, 3):
            for r in range(2):
                send(s1b.at[r, d], s1g.at[mine, rows],
                     s2_s.at[d, t, r], s2_r.at[d, t, c], place(xs[t], y, z, r))
        send(s1b.at[o, d], s1g.at[mine, rows], s2_s.at[d, 0, 0], s2_r.at[d, 0, 0], sib)
        s1g[mine, rows] = s1b[c, d]

    for f, (field, held) in enumerate(((innov, inn_v), (weight, wei_v), (cou_x, cx_v), (cou_y, cy_v))):
        loads[2 + f].wait()
        send(field.at[0], frow.at[f, 1], fw_s.at[f, 0], fw_r.at[f, 1], down)
        send(field.at[63], frow.at[f, 0], fw_s.at[f, 1], fw_r.at[f, 0], up)
        fcs[0, f:f + 1, :] = held[:, :, 0:128].reshape(512, 128).T[0:1]
        fcs[1, f:f + 1, :] = held[:, :, 128:256].reshape(512, 128).T[127:128]
    send(fcs.at[0], fcr.at[0], fc_s.at[0], fc_r.at[0], left)
    send(fcs.at[1], fcr.at[1], fc_s.at[1], fc_r.at[1], right)

    for h in range(2):
        for t in (3, 1, 2):
            for s in range(4):
                arrived(cg.at[h, pl.ds(ys[4 - t] * 8 + 2 * s, 2)], s1_r.at[h, t - 1, s])
    loads[0].wait()
    loads[1].wait()
    arrived(fxb.at[o, 0], fo_r.at[0])
    smooth(0)
    for t in (1, 3):
        part = fxb.at[c, pl.ds(1, 3), xs[4 - t]]
        arrived(part, f2_r.at[t // 2])
        send(part, part, fr_s.at[t], fr_r.at[t], sib)
    for t in range(4):
        arrived(fxb.at[o, pl.ds(1, 3), xs[(4 - t) % 4]], fr_r.at[t])
    smooth(1)
    smooth(2)
    smooth(3)

    zo = 1 - zh
    arrived(fyb.at[zo, e], g1_r.at[0])
    for t in (2, 1, 3):
        send(fyb.at[zo, e], fyb.at[zo, e], g2_s.at[t - 1], g2_r.at[t - 1], place(x, ys[t], z, c))
    send(fyb.at[zo, e], fyb.at[zo, e], gr_s.at[0], gr_r.at[0], sib)

    def cols_dot(q, hh, g):
        cols = pl.ds(pl.multiple_of(q * 256, 256), 256)
        b = fyb[hh, :, :, cols].reshape(256, 256)
        a = s1g[q, g * 128:(g + 1) * 128, :]
        return lax.dot_general(a, b, (((1,), (1,)), ((), ())), preferred_element_type=F32)

    for t in (3, 1, 2):
        eq = ys[4 - t] * 2 + c
        arrived(fyb.at[zo, eq], g2_r.at[t - 1])
        send(fyb.at[zo, eq], fyb.at[zo, eq], gr_s.at[t], gr_r.at[t], sib)
    for t in range(4):
        arrived(fyb.at[zo, ys[(4 - t) % 4] * 2 + o], gr_r.at[t])
    sources = [(0, 0, mine), (0, 0, o * 4 + x)]
    sources += [(t, cc, cc * 4 + xs[4 - t]) for t in (3, 1, 2) for cc in range(2)]

    for g in range(2):
        for i, (t, cc, q) in enumerate(sources):
            if i:
                for d in (2 * g, 2 * g + 1):
                    arrived(s1g.at[q, pl.ds(d * 64, 64)], s2_r.at[d, t, cc])
            for hh in range(2):
                term = cols_dot(q, hh, g)
                if i == 0:
                    acc2[hh] = term
                elif i < 7:
                    acc2[hh] += term
                else:
                    s2b[hh, 2 * g:2 * g + 2] = (acc2[hh] + term).astype(BF16).reshape(2, 64, 256)
        for t in ((4, 5, 1) if g == 0 else (3, 2, 6, 7)):
            send(s2b.at[zs[t] // 4, t % 4], stg.at[z], s3_s.at[t - 1], s3_r.at[t - 1], place(x, y, zs[t], c))
    stg[z] = s2b[zh, 0]

    def spread(l):
        value = stg[l].astype(F32)
        for h in range(2):
            st[h, pl.ds(16 + l, 64, stride=8), :] = value[:, h * 128:(h + 1) * 128]

    for t in range(1, 8):
        arrived(stg.at[lax.rem(z + 8 - t, 8)], s3_r.at[t - 1])
    for l in range(8):
        spread(l)

    send(st.at[:, pl.ds(16, 16)], st.at[:, pl.ds(528, 16)], h_s.at[0], h_r.at[0], down)
    send(st.at[:, pl.ds(512, 16)], st.at[:, pl.ds(0, 16)], h_s.at[1], h_r.at[1], up)
    for k, (h, at) in enumerate(((1, 520), (0, 520), (1, 16), (0, 16))):
        send(st.at[h, pl.ds(at, 8)], cor.at[k], h_s.at[4 + k], h_r.at[4 + k], corners[k])
    hys[0] = st[0, 16:528, :].T[0:8]
    send(hys.at[0], hyr.at[0], h_s.at[2], h_r.at[2], left)
    hys[1] = st[1, 16:528, :].T[120:128]
    send(hys.at[1], hyr.at[1], h_s.at[3], h_r.at[3], right)
    for f in range(4):
        for k in range(2):
            arrived(frow.at[f, k], fw_r.at[f, k])
    for k in range(2):
        arrived(fcr.at[k], fc_r.at[k])
    arrived(st.at[:, pl.ds(528, 16)], h_r.at[0])
    arrived(st.at[:, pl.ds(0, 16)], h_r.at[1])
    for k in range(2):
        arrived(hyr.at[k], h_r.at[2 + k])
    for k in range(4):
        arrived(cor.at[k], h_r.at[4 + k])

    @pl.when(gx == 0)
    def _():
        st[:, 0:16, :] = jnp.zeros((2, 16, 128), F32)

    @pl.when(gx == 31)
    def _():
        st[:, 528:544, :] = jnp.zeros((2, 16, 128), F32)

    keep_u = jnp.where(gx == 0, 0.0, 1.0).astype(F32)
    keep_d = jnp.where(gx == 31, 0.0, 1.0).astype(F32)
    keep_l = jnp.where(gy == 0, 0.0, 1.0).astype(F32)
    keep_r = jnp.where(gy == 7, 0.0, 1.0).astype(F32)
    cor[0] = cor[0] * (keep_u * keep_l)
    cor[1] = cor[1] * (keep_u * keep_r)
    cor[2] = cor[2] * (keep_d * keep_l)
    cor[3] = cor[3] * (keep_d * keep_r)
    beyond_l = hyr[1, 6:8, :] * keep_l
    beyond_r = hyr[0, 0:2, :] * keep_r
    hr[...] = jnp.broadcast_to(beyond_r[0:1], (128, 512)).T
    hl[...] = jnp.broadcast_to(beyond_l[1:2], (128, 512)).T

    def beside(v0, v1, left_halo, right_halo):
        lane = lax.broadcasted_iota(jnp.int32, v0.shape, 1)
        f0, f1 = pltpu.roll(v0, 127, 1), pltpu.roll(v1, 127, 1)
        b0, b1 = pltpu.roll(v0, 1, 1), pltpu.roll(v1, 1, 1)
        after = (jnp.where(lane == 127, f1, f0), jnp.where(lane == 127, right_halo, f1))
        before = (jnp.where(lane == 0, left_halo, b0), jnp.where(lane == 0, b0, b1))
        return before, after

    for k, at, to, keep in ((0, 8, 0, keep_u), (1, 528, 520, keep_d)):
        v = [st[h, at:at + 8, :] for h in range(2)]
        before, after = beside(v[0], v[1], pltpu.roll(cor[2 * k], 1, 1), pltpu.roll(cor[2 * k + 1], 127, 1))
        for h in range(2):
            ln = slice(h * 128, (h + 1) * 128)
            cx, cy = frow[2, k, :, ln], frow[3, k, :, ln]
            end = (v[h] - cx * (st[h, at + 8:at + 16, :] - st[h, at - 8:at, :]) * 0.5
                   - cy * (after[h] - before[h]) * 0.5)
            qx[h, to:to + 8, :] = keep * cx * (frow[1, k, :, ln] * (end - frow[0, k, :, ln]))

    spot = lax.broadcasted_iota(jnp.int32, (8, 512), 1)
    level = lax.broadcasted_iota(jnp.int32, (8, 512), 0)
    ahead = lax.broadcasted_iota(jnp.int32, (1, 512), 1)

    def along(k, at):
        column = jnp.broadcast_to(cor[k][:, at:at + 1], (8, 512))
        return jnp.sum(jnp.where(lax.rem(spot, 8) == level, column, 0.0), axis=0, keepdims=True)

    def flux(k, value, low, high, first, last, keep):
        prev = jnp.where(ahead < 8, first, pltpu.roll(value, 8, 1))
        post = jnp.where(ahead >= 504, last, pltpu.roll(value, 504, 1))
        inn, wei, cx, cy = [fcr[k, f:f + 1, :] for f in range(4)]
        end = value - cx * (post - prev) * 0.5 - cy * (high - low) * 0.5
        return jnp.broadcast_to(keep * cy * (wei * (end - inn)), (128, 512)).T

    ql[...] = flux(1, beyond_l[1:2], beyond_l[0:1], hys[0, 0:1, :], along(0, 127), along(2, 127), keep_l)
    qr[...] = flux(0, beyond_r[0:1], hys[1, 7:8, :], beyond_r[1:2], along(1, 0), along(3, 0), keep_r)

    @pl.loop(0, 8)
    def _(i):
        at = pl.multiple_of(i * 64, 64)
        xr = pl.ds(i * 8, 8)
        v = [st[h, pl.ds(at + 16, 64), :] for h in range(2)]
        before, after = beside(v[0], v[1], hl[pl.ds(at, 64), :], hr[pl.ds(at, 64), :])
        for h in range(2):
            ln = slice(h * 128, (h + 1) * 128)
            cx = cx_v[xr, :, ln].reshape(64, 128)
            cy = cy_v[xr, :, ln].reshape(64, 128)
            prev = st[h, pl.ds(at + 8, 64), :]
            post = st[h, pl.ds(at + 24, 64), :]
            end = v[h] - cx * (post - prev) * 0.5 - cy * (after[h] - before[h]) * 0.5
            end_out[xr, :, ln] = end.reshape(8, 8, 128)
            m = wei_v[xr, :, ln].reshape(64, 128) * (end - inn_v[xr, :, ln].reshape(64, 128))
            mis[h, pl.ds(at, 64), :] = m
            qx[h, pl.ds(at + 8, 64), :] = cx * m
            py[h, pl.ds(at, 64), :] = cy * m

    @pl.loop(0, 8)
    def _(i):
        at = pl.multiple_of(i * 64, 64)
        v = [py[h, pl.ds(at, 64), :] for h in range(2)]
        before, after = beside(v[0], v[1], ql[pl.ds(at, 64), :], qr[pl.ds(at, 64), :])
        for h in range(2):
            prev = qx[h, pl.ds(at, 64), :]
            post = qx[h, pl.ds(at + 16, 64), :]
            adj[h, pl.ds(at, 64), :] = (
                mis[h, pl.ds(at, 64), :] + 0.5 * (post - prev) + 0.5 * (after[h] - before[h]))

    for l in range(8):
        for h in range(2):
            ags[l, :, h * 128:(h + 1) * 128] = adj[h, pl.ds(l, 64, stride=8), :].astype(BF16)

    for t in (4, 3, 7, 2, 6, 5, 1):
        send(ags.at[zs[t]], ag.at[zh, (4 - t % 4) % 4], s5_s.at[t - 1], s5_r.at[t - 1], place(x, y, zs[t], c))
    ag[zh, 0] = ags[z]

    def share(g, q):
        cols = pl.ds(pl.multiple_of(q * 256, 256), 256)
        total = None
        for hh in range(2):
            a = ag[hh, 2 * g:2 * g + 2].reshape(128, 256)
            b = fyb[hh, :, :, cols].reshape(256, 256)
            term = jnp.dot(a, b, preferred_element_type=F32)
            total = term if total is None else total + term
        return total

    targets = [(t, r, r * 4 + xs[t], place(xs[t], y, z, r)) for t in (2, 1, 3) for r in range(2)]
    targets += [(0, 0, o * 4 + x, sib)]

    def hand(h, k, rows):
        for t, r, q, dev in targets:
            send(psend.at[h, t, r, rows], pg.at[h, t, c, rows],
                 s6_s.at[k, t, r], s6_r.at[k, t, c], dev)

    for g in range(2):
        rows = pl.ds(g * 128, 128)
        for t in ((4, 3, 7) if g == 0 else (2, 6, 5, 1)):
            arrived(ag.at[zs[8 - t] // 4, (4 - t % 4) % 4], s5_r.at[t - 1])
        for t, r, q, dev in targets:
            value = share(g, q).astype(BF16)
            for h in range(2):
                psend[h, t, r, rows] = value[:, h * 128:(h + 1) * 128]
            send(psend.at[0, t, r, rows], pg.at[0, t, c, rows],
                 s6_s.at[g, t, r], s6_r.at[g, t, c], dev)
        value = share(g, mine)
        for h in range(2):
            pown[h, rows] = value[:, h * 128:(h + 1) * 128]

    def lines(h, q):
        cols = pl.ds(pl.multiple_of(q * 512, 512), 512)
        a = fxb[:, :, :, :, cols].reshape(512, 512)
        b = pb[h].reshape(512, 128)
        return lax.dot_general(a, b, (((0,), (0,)), ((), ())), preferred_element_type=F32)

    def three(h, r):
        return pg[h, 1, r].astype(F32) + pg[h, 2, r].astype(F32) + pg[h, 3, r].astype(F32)

    for h in range(2):
        for k, rows in ((0, pl.ds(0, 128)), (1, pl.ds(128, 128))) if h == 0 else ((2, pl.ds(0, 256)),):
            arrived(pg.at[h, 0, o, rows], s6_r.at[k, 0, o])
            for t in (1, 3, 2):
                for cc in range(2):
                    arrived(pg.at[h, t, cc, rows], s6_r.at[k, t, cc])
            if k == 0:
                hand(1, 2, pl.ds(0, 256))
        pb[h, c] = (three(h, c) + pown[h]).astype(BF16)
        pb[h, o] = (three(h, o) + pg[h, 0, o].astype(F32)).astype(BF16)
        for t in (2, 1, 3):
            gsend[h, t - 1] = lines(h, ys[t]).astype(BF16)
            send(gsend.at[h, t - 1], gg.at[h, t - 1], s7_s.at[h, t - 1], s7_r.at[h, t - 1], place(x, ys[t], z, c))
        gown[h] = lines(h, y)

    own8, far8 = [], []
    for h in range(2):
        for t in range(1, 4):
            arrived(gg.at[h, t - 1], s7_r.at[h, t - 1])
        total = gown[h] + gg[h, 0].astype(F32) + gg[h, 1].astype(F32) + gg[h, 2].astype(F32)
        gs[h] = total.astype(BF16).reshape(8, 64, 128)
        for u in (2, 1, 3, 0):
            zq = lax.rem(zl + u, 4)
            for v in range(2):
                cq = o if v else c
                if u or v:
                    send(gs.at[h, zq * 2 + cq], go.at[h, z], s8_s.at[h, u, v], s8_r.at[h, z],
                         place(x, y, c * 4 + zq, cq))
        src, dst = gs.at[h, zl * 2 + c], go.at[h, z]
        own8.append(pltpu.make_async_copy(src, dst, s8_r.at[h, z]))
        far8.append(pltpu.make_async_remote_copy(
            src_ref=src, dst_ref=dst, send_sem=s8_s.at[h, 0, 0], recv_sem=s8_r.at[h, z],
            device_id=place(x, y, c * 4 + zl, c), device_id_type=MESH))

        @pl.when(zh == c)
        def _():
            own8[h].start()

        @pl.when(zh != c)
        def _():
            far8[h].start()

    for h in range(2):
        ln = slice(h * 128, (h + 1) * 128)
        for l in range(8):
            arrived(go.at[h, l], s8_r.at[h, l])
        for l in range(8):
            nat[h, pl.ds(l, 64, stride=8), :] = go[h, l].astype(F32)
        grad_out[:, :, ln] = ctl_v[:, :, ln].astype(F32) + nat[h].reshape(64, 8, 128)
    for copy in pending:
        copy.wait_send()

    @pl.when(zh != c)
    def _():
        for h in range(2):
            far0[h].wait_send()
            far8[h].wait_send()


def per_device(control, innovation, obs_weight, courant_x, courant_y, filter_x, filter_y):
    dma = lambda *shape: pltpu.SemaphoreType.DMA(shape)
    big = pltpu.VMEM((64, 8, 256), F32)
    half = pltpu.VMEM((2, 512, 128), F32)
    ext = pltpu.VMEM((2, 528, 128), F32)
    col = pltpu.VMEM((512, 128), F32)
    lev = pltpu.VMEM((8, 64, 256), BF16)
    levh = pltpu.VMEM((2, 8, 64, 128), BF16)
    halo = pltpu.VMEM((2, 8, 512), F32)
    planes = pltpu.VMEM((2, 4, 64, 256), BF16)
    shares = pltpu.VMEM((2, 4, 2, 256, 128), BF16)
    sums = pltpu.VMEM((2, 3, 512, 128), BF16)
    scratch = [
        pltpu.VMEM((64, 8, 256), BF16), big, big, big, big,
        half, levh,
        pltpu.VMEM((2, 32, 64, 128), BF16),
        pltpu.VMEM((2, 4, 4, 16, 2048), BF16),
        pltpu.VMEM((2, 8, 32, 2048), BF16),
        pltpu.VMEM((2, 4, 64, 256), BF16),
        pltpu.VMEM((8, 256, 256), BF16),
        pltpu.VMEM((2, 128, 256), F32),
        planes, lev,
        pltpu.VMEM((2, 544, 128), F32), halo, halo,
        pltpu.VMEM((4, 8, 128), F32),
        pltpu.VMEM((4, 2, 8, 256), F32), halo, halo,
        col, col, col, col, ext, half, half, half, lev, planes,
        shares,
        pltpu.VMEM((2, 256, 128), F32),
        shares,
        pltpu.VMEM((2, 2, 256, 128), BF16),
        sums,
        pltpu.VMEM((2, 512, 128), F32),
        sums, levh, levh,
        dma(7), dma(3, 2), dma(3, 2), dma(1), dma(1), dma(2), dma(2), dma(4), dma(4),
        dma(1), dma(1), dma(3), dma(3), dma(4), dma(4),
        dma(2, 8), dma(2, 8), dma(2, 3, 4), dma(2, 3, 4), dma(4, 4, 2), dma(4, 4, 2), dma(7), dma(7),
        dma(8), dma(8), dma(4, 2), dma(4, 2), dma(2), dma(2), dma(7), dma(7), dma(3, 4, 2), dma(3, 4, 2),
        dma(2, 3), dma(2, 3), dma(2, 4, 2), dma(2, 8),
    ]
    out = pltpu.VMEM((64, 8, 256), F32)
    anywhere = pl.BlockSpec(memory_space=pl.ANY)
    return pl.pallas_call(
        kernel,
        out_shape=(out, out),
        in_specs=[anywhere] * 7,
        out_specs=(pl.BlockSpec(memory_space=pltpu.VMEM),) * 2,
        scratch_shapes=scratch,
        compiler_params=pltpu.CompilerParams(
            collective_id=0, has_side_effects=True, vmem_limit_bytes=62 * 1024 * 1024),
        cost_estimate=pl.CostEstimate(flops=2150000000, bytes_accessed=5000000, transcendentals=0),
    )(control, innovation, obs_weight, courant_x, courant_y,
      filter_x.reshape(4, 16, 2048), filter_y.reshape(8, 32, 2048))


def solution(mesh):
    grid = P("gx", None, "gy")
    placed = (grid, grid, grid, grid, grid, P("gx", None), P("gy", None))
    return jax.shard_map(
        per_device, mesh=mesh, in_specs=placed, out_specs=(grid, grid), check_vma=False)
```

```python
import jax
import jax.numpy as jnp
from jax import lax
from jax.experimental import pallas as pl
from jax.experimental.pallas import tpu as pltpu
from jax.sharding import PartitionSpec as P

MESH = pl.DeviceIdType.MESH
F32 = jnp.float32
BF16 = jnp.bfloat16
F_ONE = ((2, 2, pl.ds(0, 1024)), (2, 6, pl.ds(1024, 1024)), (1, 7, pl.ds(0, 2048)), (3, 1, pl.ds(0, 2048)))


def place(x, y, z, c):
    return (y * 8 + lax.rem(z, 4) * 2 + c, (z // 4) * 4 + x)


def kernel(
    ctl, innov, weight, cou_x, cou_y, fx, fy,
    end_out, grad_out,
    ctl_v, inn_v, wei_v, cx_v, cy_v,
    nat, snd0, cg, fxb, fyb, s1b, s1g, acc2, s2b, stg,
    st, hys, hyr, cor, frow, fcs, fcr, hl, hr, ql, qr, qx, py, mis, adj, ags, ag,
    psend, pown, pg, pb, gsend, gown, gg, gs, go,
    loc_sem, f1_s, f1_r, fo_s, fo_r, f2_s, f2_r, fr_s, fr_r,
    g1_s, g1_r, g2_s, g2_r, gr_s, gr_r,
    s0_s, s0_r, s1_s, s1_r, s2_s, s2_r, s3_s, s3_r,
    h_s, h_r, fw_s, fw_r, fc_s, fc_r, s5_s, s5_r, s6_s, s6_r, s7_s, s7_r, s8_s, s8_r,
):
    gx = lax.axis_index("gx")
    gy = lax.axis_index("gy")
    y = gx // 8
    zl = lax.rem(gx // 2, 4)
    c = lax.rem(gx, 2)
    zh = gy // 4
    x = lax.rem(gy, 4)
    z = zh * 4 + zl
    o = 1 - c
    sib = place(x, y, z, o)
    e = y * 2 + c
    pending = []

    def send(src, dst, ssem, rsem, dev):
        copy = pltpu.make_async_remote_copy(
            src_ref=src, dst_ref=dst, send_sem=ssem, recv_sem=rsem,
            device_id=dev, device_id_type=MESH)
        copy.start()
        pending.append(copy)

    def arrived(dst, rsem):
        pltpu.make_async_copy(dst, dst, rsem).wait()

    xs = [lax.rem(x + t, 4) for t in range(4)]
    ys = [lax.rem(y + t, 4) for t in range(4)]
    zs = [lax.rem(z + t, 8) for t in range(8)]
    up = (lax.rem(gx + 1, 32), gy)
    down = (lax.rem(gx + 31, 32), gy)
    right = (gx, lax.rem(gy + 1, 8))
    left = (gx, lax.rem(gy + 7, 8))
    corners = [(up[0], right[1]), (up[0], left[1]), (down[0], right[1]), (down[0], left[1])]

    load_ctl = pltpu.make_async_copy(ctl, ctl_v, loc_sem.at[0])
    load_ctl.start()
    loads = [
        pltpu.make_async_copy(s, d, loc_sem.at[1 + i])
        for i, (s, d) in enumerate([
            (fx, fxb.at[c, 0]), (fy, fyb.at[zh]), (innov, inn_v),
            (weight, wei_v), (cou_x, cx_v), (cou_y, cy_v)])
    ]
    for load in loads:
        load.start()

    barrier = pltpu.get_barrier_semaphore()
    partners = [sib]
    for t in range(1, 8):
        partners += [place(x, y, zs[t], c), place(x, y, zs[t], o)]
    for t in range(1, 4):
        partners += [place(xs[t], y, z, c), place(xs[t], y, z, o)]
        partners += [place(x, ys[t], z, c)]
    partners += [up, down, left, right] + corners
    for dev in partners:
        pl.semaphore_signal(barrier, inc=1, device_id=dev, device_id_type=MESH)

    load_ctl.wait()
    for h in range(2):
        nat[h] = ctl_v[:, :, h * 128:(h + 1) * 128].astype(F32).reshape(512, 128)
    for l in range(8):
        for h in range(2):
            snd0[h, l] = nat[h, pl.ds(l, 64, stride=8), :].astype(BF16)

    pl.semaphore_wait(barrier, len(partners))

    slot0 = zl * 2 + c
    x2 = xs[2]
    own0, far0 = [], []
    for h in range(2):
        for t in (4, 3, 5, 2, 6, 1, 7):
            send(snd0.at[h, zs[t]], cg.at[h, gx], s0_s.at[h, t], s0_r.at[h, slot0], place(x, y, zs[t], zh))
        src, dst = snd0.at[h, z], cg.at[h, gx]
        own0.append(pltpu.make_async_copy(src, dst, s0_r.at[h, slot0]))
        far0.append(pltpu.make_async_remote_copy(
            src_ref=src, dst_ref=dst, send_sem=s0_s.at[h, 0], recv_sem=s0_r.at[h, slot0],
            device_id=sib, device_id_type=MESH))

        @pl.when(zh == c)
        def _():
            own0[h].start()

        @pl.when(zh != c)
        def _():
            far0[h].start()

        q = x2 if h else x
        for k, (d, dz, cols) in enumerate(F_ONE):
            send(fx.at[q, :, cols], fxb.at[c, d, q, :, cols], f1_s.at[k, h], f1_r.at[k, h], place(x, y, zs[dz], c))

    send(fx, fxb.at[c, 0], fo_s.at[0], fo_r.at[0], sib)

    for f, (field, held) in enumerate(((innov, inn_v), (weight, wei_v), (cou_x, cx_v), (cou_y, cy_v))):
        loads[2 + f].wait()
        send(field.at[0], frow.at[f, 1], fw_s.at[f, 0], fw_r.at[f, 1], down)
        send(field.at[63], frow.at[f, 0], fw_s.at[f, 1], fw_r.at[f, 0], up)
        fcs[0, f:f + 1, :] = held[:, :, 0:128].reshape(512, 128).T[0:1]
        fcs[1, f:f + 1, :] = held[:, :, 128:256].reshape(512, 128).T[127:128]
    send(fcs.at[0], fcr.at[0], fc_s.at[0], fc_r.at[0], left)
    send(fcs.at[1], fcr.at[1], fc_s.at[1], fc_r.at[1], right)

    def ring(h):
        for s in range(4):
            for cc in range(2):
                arrived(cg.at[h, y * 8 + 2 * s + cc], s0_r.at[h, 2 * s + cc])
            block = cg.at[h, pl.ds(y * 8 + 2 * s, 2)]
            for t in (2, 1, 3):
                send(block, block, s1_s.at[h, t - 1, s], s1_r.at[h, t - 1, s], place(x, ys[t], z, c))

    ring(0)

    send(fy.at[e], fyb.at[zh, e], g1_s.at[0], g1_r.at[0], place(x, y, zs[4], c))

    for k, (d, dz, cols) in enumerate(F_ONE):
        arrived(fxb.at[c, d, x, :, cols], f1_r.at[k, 0])
    quarter = fxb.at[c, pl.ds(1, 3), x]
    for t in (1, 3):
        send(quarter, quarter, f2_s.at[t // 2], f2_r.at[t // 2], place(xs[t], y, z, c))
    send(quarter, quarter, fr_s.at[0], fr_r.at[0], sib)

    ring(1)

    for k, (d, dz, cols) in enumerate(F_ONE):
        arrived(fxb.at[c, d, x2, :, cols], f1_r.at[k, 1])
    quarter = fxb.at[c, pl.ds(1, 3), x2]
    send(quarter, quarter, fr_s.at[2], fr_r.at[2], sib)

    for t in (1, 3):
        part = fxb.at[c, pl.ds(1, 3), xs[4 - t]]
        arrived(part, f2_r.at[t // 2])
        send(part, part, fr_s.at[t], fr_r.at[t], sib)

    loads[0].wait()
    loads[1].wait()
    arrived(fxb.at[o, 0], fo_r.at[0])
    for t in range(4):
        arrived(fxb.at[o, pl.ds(1, 3), xs[(4 - t) % 4]], fr_r.at[t])

    mine = c * 4 + x
    zo = 1 - zh
    for h in range(2):
        for t in (3, 1, 2):
            for s in range(4):
                arrived(cg.at[h, pl.ds(ys[4 - t] * 8 + 2 * s, 2)], s1_r.at[h, t - 1, s])
        for g in range(2):
            k = 2 * h + g
            rows = pl.ds(g * 128, 128)
            a = fxb[:, 2 * g:2 * g + 2].reshape(256, 2048)
            v = jnp.dot(a, cg[h].reshape(2048, 128), preferred_element_type=F32)
            s1b[h, :, rows] = v.astype(BF16).reshape(2, 128, 128)
            for t in (2, 1, 3):
                for r in range(2):
                    send(s1b.at[h, r, rows], s1g.at[h, mine, rows],
                         s2_s.at[k, t, r], s2_r.at[k, t, c], place(xs[t], y, z, r))
            send(s1b.at[h, o, rows], s1g.at[h, mine, rows], s2_s.at[k, 0, 0], s2_r.at[k, 0, 0], sib)
        s1g[h, mine] = s1b[h, c]
        if h == 0:
            arrived(fyb.at[zo, e], g1_r.at[0])
            for t in (2, 1, 3):
                send(fyb.at[zo, e], fyb.at[zo, e], g2_s.at[t - 1], g2_r.at[t - 1], place(x, ys[t], z, c))
            send(fyb.at[zo, e], fyb.at[zo, e], gr_s.at[0], gr_r.at[0], sib)

    def cols_dot(h, q, hh, g):
        cols = pl.ds(pl.multiple_of(q * 256 + h * 128, 128), 128)
        b = fyb[hh, :, :, cols].reshape(256, 128)
        a = s1g[h, q, g * 128:(g + 1) * 128, :]
        return lax.dot_general(a, b, (((1,), (1,)), ((), ())), preferred_element_type=F32)

    sources = [(0, 0, mine), (0, 0, o * 4 + x)]
    sources += [(t, cc, cc * 4 + xs[4 - t]) for t in (3, 1, 2) for cc in range(2)]

    def level_up(k, hh):
        for h in range(2):
            for g in range(2):
                rows = pl.ds(g * 128, 128)
                for i, (t, cc, q) in enumerate(sources):
                    if i and k == 0:
                        arrived(s1g.at[h, q, rows], s2_r.at[2 * h + g, t, cc])
                    term = cols_dot(h, q, hh, g)
                    acc2[g] = acc2[g] + term if h or i else term
                if h:
                    s2b[hh, 2 * g:2 * g + 2] = acc2[g].astype(BF16).reshape(2, 64, 256)
                    for d in ((1, 0) if g == 0 else (2, 3)):
                        if k or d:
                            send(s2b.at[hh, d], stg.at[z], s3_s.at[k * 4 + d], s3_r.at[k * 4 + d],
                                 place(x, y, hh * 4 + lax.rem(zl + d, 4), c))

    for t in (3, 1, 2):
        eq = ys[4 - t] * 2 + c
        arrived(fyb.at[zo, eq], g2_r.at[t - 1])
        send(fyb.at[zo, eq], fyb.at[zo, eq], gr_s.at[t], gr_r.at[t], sib)
    level_up(0, zh)
    stg[z] = s2b[zh, 0]
    for t in range(4):
        arrived(fyb.at[zo, ys[(4 - t) % 4] * 2 + o], gr_r.at[t])
    level_up(1, zo)

    def spread(l):
        value = stg[l].astype(F32)
        for h in range(2):
            st[h, pl.ds(16 + l, 64, stride=8), :] = value[:, h * 128:(h + 1) * 128]

    for k, hh in ((0, zh), (1, zo)):
        for d in range(4):
            if k or d:
                arrived(stg.at[hh * 4 + lax.rem(zl + 4 - d, 4)], s3_r.at[k * 4 + d])
    for l in range(8):
        spread(l)

    send(st.at[:, pl.ds(16, 16)], st.at[:, pl.ds(528, 16)], h_s.at[0], h_r.at[0], down)
    send(st.at[:, pl.ds(512, 16)], st.at[:, pl.ds(0, 16)], h_s.at[1], h_r.at[1], up)
    for k, (h, at) in enumerate(((1, 520), (0, 520), (1, 16), (0, 16))):
        send(st.at[h, pl.ds(at, 8)], cor.at[k], h_s.at[4 + k], h_r.at[4 + k], corners[k])
    hys[0] = st[0, 16:528, :].T[0:8]
    send(hys.at[0], hyr.at[0], h_s.at[2], h_r.at[2], left)
    hys[1] = st[1, 16:528, :].T[120:128]
    send(hys.at[1], hyr.at[1], h_s.at[3], h_r.at[3], right)
    for f in range(4):
        for k in range(2):
            arrived(frow.at[f, k], fw_r.at[f, k])
    for k in range(2):
        arrived(fcr.at[k], fc_r.at[k])
    arrived(st.at[:, pl.ds(528, 16)], h_r.at[0])
    arrived(st.at[:, pl.ds(0, 16)], h_r.at[1])
    for k in range(2):
        arrived(hyr.at[k], h_r.at[2 + k])
    for k in range(4):
        arrived(cor.at[k], h_r.at[4 + k])

    @pl.when(gx == 0)
    def _():
        st[:, 0:16, :] = jnp.zeros((2, 16, 128), F32)

    @pl.when(gx == 31)
    def _():
        st[:, 528:544, :] = jnp.zeros((2, 16, 128), F32)

    keep_u = jnp.where(gx == 0, 0.0, 1.0).astype(F32)
    keep_d = jnp.where(gx == 31, 0.0, 1.0).astype(F32)
    keep_l = jnp.where(gy == 0, 0.0, 1.0).astype(F32)
    keep_r = jnp.where(gy == 7, 0.0, 1.0).astype(F32)
    cor[0] = cor[0] * (keep_u * keep_l)
    cor[1] = cor[1] * (keep_u * keep_r)
    cor[2] = cor[2] * (keep_d * keep_l)
    cor[3] = cor[3] * (keep_d * keep_r)
    beyond_l = hyr[1, 6:8, :] * keep_l
    beyond_r = hyr[0, 0:2, :] * keep_r
    hr[...] = jnp.broadcast_to(beyond_r[0:1], (128, 512)).T
    hl[...] = jnp.broadcast_to(beyond_l[1:2], (128, 512)).T

    def beside(v0, v1, left_halo, right_halo):
        lane = lax.broadcasted_iota(jnp.int32, v0.shape, 1)
        f0, f1 = pltpu.roll(v0, 127, 1), pltpu.roll(v1, 127, 1)
        b0, b1 = pltpu.roll(v0, 1, 1), pltpu.roll(v1, 1, 1)
        after = (jnp.where(lane == 127, f1, f0), jnp.where(lane == 127, right_halo, f1))
        before = (jnp.where(lane == 0, left_halo, b0), jnp.where(lane == 0, b0, b1))
        return before, after

    for k, at, to, keep in ((0, 8, 0, keep_u), (1, 528, 520, keep_d)):
        v = [st[h, at:at + 8, :] for h in range(2)]
        before, after = beside(v[0], v[1], pltpu.roll(cor[2 * k], 1, 1), pltpu.roll(cor[2 * k + 1], 127, 1))
        for h in range(2):
            ln = slice(h * 128, (h + 1) * 128)
            cx, cy = frow[2, k, :, ln], frow[3, k, :, ln]
            end = (v[h] - cx * (st[h, at + 8:at + 16, :] - st[h, at - 8:at, :]) * 0.5
                   - cy * (after[h] - before[h]) * 0.5)
            qx[h, to:to + 8, :] = keep * cx * (frow[1, k, :, ln] * (end - frow[0, k, :, ln]))

    spot = lax.broadcasted_iota(jnp.int32, (8, 512), 1)
    level = lax.broadcasted_iota(jnp.int32, (8, 512), 0)
    ahead = lax.broadcasted_iota(jnp.int32, (1, 512), 1)

    def along(k, at):
        column = jnp.broadcast_to(cor[k][:, at:at + 1], (8, 512))
        return jnp.sum(jnp.where(lax.rem(spot, 8) == level, column, 0.0), axis=0, keepdims=True)

    def flux(k, value, low, high, first, last, keep):
        prev = jnp.where(ahead < 8, first, pltpu.roll(value, 8, 1))
        post = jnp.where(ahead >= 504, last, pltpu.roll(value, 504, 1))
        inn, wei, cx, cy = [fcr[k, f:f + 1, :] for f in range(4)]
        end = value - cx * (post - prev) * 0.5 - cy * (high - low) * 0.5
        return jnp.broadcast_to(keep * cy * (wei * (end - inn)), (128, 512)).T

    ql[...] = flux(1, beyond_l[1:2], beyond_l[0:1], hys[0, 0:1, :], along(0, 127), along(2, 127), keep_l)
    qr[...] = flux(0, beyond_r[0:1], hys[1, 7:8, :], beyond_r[1:2], along(1, 0), along(3, 0), keep_r)

    @pl.loop(0, 8)
    def _(i):
        at = pl.multiple_of(i * 64, 64)
        xr = pl.ds(i * 8, 8)
        v = [st[h, pl.ds(at + 16, 64), :] for h in range(2)]
        before, after = beside(v[0], v[1], hl[pl.ds(at, 64), :], hr[pl.ds(at, 64), :])
        for h in range(2):
            ln = slice(h * 128, (h + 1) * 128)
            cx = cx_v[xr, :, ln].reshape(64, 128)
            cy = cy_v[xr, :, ln].reshape(64, 128)
            prev = st[h, pl.ds(at + 8, 64), :]
            post = st[h, pl.ds(at + 24, 64), :]
            end = v[h] - cx * (post - prev) * 0.5 - cy * (after[h] - before[h]) * 0.5
            end_out[xr, :, ln] = end.reshape(8, 8, 128)
            m = wei_v[xr, :, ln].reshape(64, 128) * (end - inn_v[xr, :, ln].reshape(64, 128))
            mis[h, pl.ds(at, 64), :] = m
            qx[h, pl.ds(at + 8, 64), :] = cx * m
            py[h, pl.ds(at, 64), :] = cy * m

    @pl.loop(0, 8)
    def _(i):
        at = pl.multiple_of(i * 64, 64)
        v = [py[h, pl.ds(at, 64), :] for h in range(2)]
        before, after = beside(v[0], v[1], ql[pl.ds(at, 64), :], qr[pl.ds(at, 64), :])
        for h in range(2):
            prev = qx[h, pl.ds(at, 64), :]
            post = qx[h, pl.ds(at + 16, 64), :]
            adj[h, pl.ds(at, 64), :] = (
                mis[h, pl.ds(at, 64), :] + 0.5 * (post - prev) + 0.5 * (after[h] - before[h]))

    for l in range(8):
        for h in range(2):
            ags[l, :, h * 128:(h + 1) * 128] = adj[h, pl.ds(l, 64, stride=8), :].astype(BF16)

    for t in (4, 3, 7, 2, 6, 5, 1):
        send(ags.at[zs[t]], ag.at[zh, (4 - t % 4) % 4], s5_s.at[t - 1], s5_r.at[t - 1], place(x, y, zs[t], c))
    ag[zh, 0] = ags[z]

    def share(g, q):
        cols = pl.ds(pl.multiple_of(q * 256, 256), 256)
        total = None
        for hh in range(2):
            a = ag[hh, 2 * g:2 * g + 2].reshape(128, 256)
            b = fyb[hh, :, :, cols].reshape(256, 256)
            term = jnp.dot(a, b, preferred_element_type=F32)
            total = term if total is None else total + term
        return total

    targets = [(t, r, r * 4 + xs[t], place(xs[t], y, z, r)) for t in (2, 1, 3) for r in range(2)]
    targets += [(0, 0, o * 4 + x, sib)]

    def hand(h, k, rows):
        for t, r, q, dev in targets:
            send(psend.at[h, t, r, rows], pg.at[h, t, c, rows],
                 s6_s.at[k, t, r], s6_r.at[k, t, c], dev)

    for g in range(2):
        rows = pl.ds(g * 128, 128)
        for t in ((4, 3, 7) if g == 0 else (2, 6, 5, 1)):
            arrived(ag.at[zs[8 - t] // 4, (4 - t % 4) % 4], s5_r.at[t - 1])
        for t, r, q, dev in targets:
            value = share(g, q).astype(BF16)
            for h in range(2):
                psend[h, t, r, rows] = value[:, h * 128:(h + 1) * 128]
            send(psend.at[0, t, r, rows], pg.at[0, t, c, rows],
                 s6_s.at[g, t, r], s6_r.at[g, t, c], dev)
        value = share(g, mine)
        for h in range(2):
            pown[h, rows] = value[:, h * 128:(h + 1) * 128]

    def lines(h, q):
        cols = pl.ds(pl.multiple_of(q * 512, 512), 512)
        a = fxb[:, :, :, :, cols].reshape(512, 512)
        b = pb[h].reshape(512, 128)
        return lax.dot_general(a, b, (((0,), (0,)), ((), ())), preferred_element_type=F32)

    def three(h, r):
        return pg[h, 1, r].astype(F32) + pg[h, 2, r].astype(F32) + pg[h, 3, r].astype(F32)

    for h in range(2):
        for k, rows in ((0, pl.ds(0, 128)), (1, pl.ds(128, 128))) if h == 0 else ((2, pl.ds(0, 256)),):
            arrived(pg.at[h, 0, o, rows], s6_r.at[k, 0, o])
            for t in (1, 3, 2):
                for cc in range(2):
                    arrived(pg.at[h, t, cc, rows], s6_r.at[k, t, cc])
            if k == 0:
                hand(1, 2, pl.ds(0, 256))
        pb[h, c] = (three(h, c) + pown[h]).astype(BF16)
        pb[h, o] = (three(h, o) + pg[h, 0, o].astype(F32)).astype(BF16)
        for t in (2, 1, 3):
            gsend[h, t - 1] = lines(h, ys[t]).astype(BF16)
            send(gsend.at[h, t - 1], gg.at[h, t - 1], s7_s.at[h, t - 1], s7_r.at[h, t - 1], place(x, ys[t], z, c))
        gown[h] = lines(h, y)

    own8, far8 = [], []
    for h in range(2):
        for t in range(1, 4):
            arrived(gg.at[h, t - 1], s7_r.at[h, t - 1])
        total = gown[h] + gg[h, 0].astype(F32) + gg[h, 1].astype(F32) + gg[h, 2].astype(F32)
        gs[h] = total.astype(BF16).reshape(8, 64, 128)
        for u in (2, 1, 3, 0):
            zq = lax.rem(zl + u, 4)
            for v in range(2):
                cq = o if v else c
                if u or v:
                    send(gs.at[h, zq * 2 + cq], go.at[h, z], s8_s.at[h, u, v], s8_r.at[h, z],
                         place(x, y, c * 4 + zq, cq))
        src, dst = gs.at[h, zl * 2 + c], go.at[h, z]
        own8.append(pltpu.make_async_copy(src, dst, s8_r.at[h, z]))
        far8.append(pltpu.make_async_remote_copy(
            src_ref=src, dst_ref=dst, send_sem=s8_s.at[h, 0, 0], recv_sem=s8_r.at[h, z],
            device_id=place(x, y, c * 4 + zl, c), device_id_type=MESH))

        @pl.when(zh == c)
        def _():
            own8[h].start()

        @pl.when(zh != c)
        def _():
            far8[h].start()

    for h in range(2):
        ln = slice(h * 128, (h + 1) * 128)
        for l in range(8):
            arrived(go.at[h, l], s8_r.at[h, l])
        for l in range(8):
            nat[h, pl.ds(l, 64, stride=8), :] = go[h, l].astype(F32)
        grad_out[:, :, ln] = ctl_v[:, :, ln].astype(F32) + nat[h].reshape(64, 8, 128)
    for copy in pending:
        copy.wait_send()

    @pl.when(zh != c)
    def _():
        for h in range(2):
            far0[h].wait_send()
            far8[h].wait_send()


def per_device(control, innovation, obs_weight, courant_x, courant_y, filter_x, filter_y):
    dma = lambda *shape: pltpu.SemaphoreType.DMA(shape)
    big = pltpu.VMEM((64, 8, 256), F32)
    half = pltpu.VMEM((2, 512, 128), F32)
    ext = pltpu.VMEM((2, 528, 128), F32)
    col = pltpu.VMEM((512, 128), F32)
    lev = pltpu.VMEM((8, 64, 256), BF16)
    levh = pltpu.VMEM((2, 8, 64, 128), BF16)
    halo = pltpu.VMEM((2, 8, 512), F32)
    planes = pltpu.VMEM((2, 4, 64, 256), BF16)
    shares = pltpu.VMEM((2, 4, 2, 256, 128), BF16)
    sums = pltpu.VMEM((2, 3, 512, 128), BF16)
    scratch = [
        pltpu.VMEM((64, 8, 256), BF16), big, big, big, big,
        half, levh,
        pltpu.VMEM((2, 32, 64, 128), BF16),
        pltpu.VMEM((2, 4, 4, 16, 2048), BF16),
        pltpu.VMEM((2, 8, 32, 2048), BF16),
        pltpu.VMEM((2, 2, 256, 128), BF16),
        pltpu.VMEM((2, 8, 256, 128), BF16),
        pltpu.VMEM((2, 128, 256), F32),
        planes, lev,
        pltpu.VMEM((2, 544, 128), F32), halo, halo,
        pltpu.VMEM((4, 8, 128), F32),
        pltpu.VMEM((4, 2, 8, 256), F32), halo, halo,
        col, col, col, col, ext, half, half, half, lev, planes,
        shares,
        pltpu.VMEM((2, 256, 128), F32),
        shares,
        pltpu.VMEM((2, 2, 256, 128), BF16),
        sums,
        pltpu.VMEM((2, 512, 128), F32),
        sums, levh, levh,
        dma(7), dma(4, 2), dma(4, 2), dma(1), dma(1), dma(2), dma(2), dma(4), dma(4),
        dma(1), dma(1), dma(3), dma(3), dma(4), dma(4),
        dma(2, 8), dma(2, 8), dma(2, 3, 4), dma(2, 3, 4), dma(4, 4, 2), dma(4, 4, 2), dma(8), dma(8),
        dma(8), dma(8), dma(4, 2), dma(4, 2), dma(2), dma(2), dma(7), dma(7), dma(3, 4, 2), dma(3, 4, 2),
        dma(2, 3), dma(2, 3), dma(2, 4, 2), dma(2, 8),
    ]
    out = pltpu.VMEM((64, 8, 256), F32)
    anywhere = pl.BlockSpec(memory_space=pl.ANY)
    return pl.pallas_call(
        kernel,
        out_shape=(out, out),
        in_specs=[anywhere] * 7,
        out_specs=(pl.BlockSpec(memory_space=pltpu.VMEM),) * 2,
        scratch_shapes=scratch,
        compiler_params=pltpu.CompilerParams(
            collective_id=0, has_side_effects=True, vmem_limit_bytes=62 * 1024 * 1024),
        cost_estimate=pl.CostEstimate(flops=2150000000, bytes_accessed=5000000, transcendentals=0),
    )(control, innovation, obs_weight, courant_x, courant_y,
      filter_x.reshape(4, 16, 2048), filter_y.reshape(8, 32, 2048))


def solution(mesh):
    grid = P("gx", None, "gy")
    placed = (grid, grid, grid, grid, grid, P("gx", None), P("gy", None))
    return jax.shard_map(
        per_device, mesh=mesh, in_specs=placed, out_specs=(grid, grid), check_vma=False)
```

```python
import jax
import jax.numpy as jnp
from jax import lax
from jax.experimental import pallas as pl
from jax.experimental.pallas import tpu as pltpu
from jax.sharding import PartitionSpec as P

MESH = pl.DeviceIdType.MESH
F32 = jnp.float32
BF16 = jnp.bfloat16
F_ONE = ((2, 2, pl.ds(0, 1024)), (2, 6, pl.ds(1024, 1024)), (1, 7, pl.ds(0, 2048)), (3, 1, pl.ds(0, 2048)))


def place(x, y, z, c):
    return (y * 8 + lax.rem(z, 4) * 2 + c, (z // 4) * 4 + x)


def kernel(
    ctl, innov, weight, cou_x, cou_y, fx, fy,
    end_out, grad_out,
    ctl_v, inn_v, wei_v, cx_v, cy_v,
    nat, snd0, cg, fxb, fyb, s1b, s1g, acc2, s2b, stg,
    st, hys, hyr, cor, frow, fcs, fcr, hl, hr, ql, qr, qx, py, mis, adj, ags, ag,
    psend, pown, pg, pb, gsend, gown, gg, gs, go,
    loc_sem, f1_s, f1_r, fo_s, fo_r, f2_s, f2_r, fr_s, fr_r,
    g1_s, g1_r, g2_s, g2_r, gr_s, gr_r,
    s0_s, s0_r, s1_s, s1_r, s2_s, s2_r, s3_s, s3_r,
    h_s, h_r, fw_s, fw_r, fc_s, fc_r, s5_s, s5_r, s6_s, s6_r, s7_s, s7_r, s8_s, s8_r,
):
    gx = lax.axis_index("gx")
    gy = lax.axis_index("gy")
    y = gx // 8
    zl = lax.rem(gx // 2, 4)
    c = lax.rem(gx, 2)
    zh = gy // 4
    x = lax.rem(gy, 4)
    z = zh * 4 + zl
    o = 1 - c
    sib = place(x, y, z, o)
    e = y * 2 + c
    pending = []

    def send(src, dst, ssem, rsem, dev):
        copy = pltpu.make_async_remote_copy(
            src_ref=src, dst_ref=dst, send_sem=ssem, recv_sem=rsem,
            device_id=dev, device_id_type=MESH)
        copy.start()
        pending.append(copy)

    def arrived(dst, rsem):
        pltpu.make_async_copy(dst, dst, rsem).wait()

    xs = [lax.rem(x + t, 4) for t in range(4)]
    ys = [lax.rem(y + t, 4) for t in range(4)]
    zs = [lax.rem(z + t, 8) for t in range(8)]
    up = (lax.rem(gx + 1, 32), gy)
    down = (lax.rem(gx + 31, 32), gy)
    right = (gx, lax.rem(gy + 1, 8))
    left = (gx, lax.rem(gy + 7, 8))
    corners = [(up[0], right[1]), (up[0], left[1]), (down[0], right[1]), (down[0], left[1])]

    load_ctl = pltpu.make_async_copy(ctl, ctl_v, loc_sem.at[0])
    load_ctl.start()
    loads = [
        pltpu.make_async_copy(s, d, loc_sem.at[1 + i])
        for i, (s, d) in enumerate([
            (fx, fxb.at[c, 0]), (fy, fyb.at[zh]), (innov, inn_v),
            (weight, wei_v), (cou_x, cx_v), (cou_y, cy_v)])
    ]
    for load in loads:
        load.start()

    barrier = pltpu.get_barrier_semaphore()
    partners = [sib]
    for t in range(1, 8):
        partners += [place(x, y, zs[t], c), place(x, y, zs[t], o)]
    for t in range(1, 4):
        partners += [place(xs[t], y, z, c), place(xs[t], y, z, o)]
        partners += [place(x, ys[t], z, c)]
    partners += [up, down, left, right] + corners
    for dev in partners:
        pl.semaphore_signal(barrier, inc=1, device_id=dev, device_id_type=MESH)

    load_ctl.wait()
    for h in range(2):
        nat[h] = ctl_v[:, :, h * 128:(h + 1) * 128].astype(F32).reshape(512, 128)
    for l in range(8):
        for h in range(2):
            snd0[h, l] = nat[h, pl.ds(l, 64, stride=8), :].astype(BF16)

    pl.semaphore_wait(barrier, len(partners))

    slot0 = zl * 2 + c
    x2 = xs[2]
    own0, far0 = [], []
    for h in range(2):
        for t in (4, 3, 5, 2, 6, 1, 7):
            send(snd0.at[h, zs[t]], cg.at[h, gx], s0_s.at[h, t], s0_r.at[h, slot0], place(x, y, zs[t], zh))
        src, dst = snd0.at[h, z], cg.at[h, gx]
        own0.append(pltpu.make_async_copy(src, dst, s0_r.at[h, slot0]))
        far0.append(pltpu.make_async_remote_copy(
            src_ref=src, dst_ref=dst, send_sem=s0_s.at[h, 0], recv_sem=s0_r.at[h, slot0],
            device_id=sib, device_id_type=MESH))

        @pl.when(zh == c)
        def _():
            own0[h].start()

        @pl.when(zh != c)
        def _():
            far0[h].start()

        q = x2 if h else x
        for k, (d, dz, cols) in enumerate(F_ONE):
            send(fx.at[q, :, cols], fxb.at[c, d, q, :, cols], f1_s.at[k, h], f1_r.at[k, h], place(x, y, zs[dz], c))

    send(fx, fxb.at[c, 0], fo_s.at[0], fo_r.at[0], sib)

    for f, (field, held) in enumerate(((innov, inn_v), (weight, wei_v), (cou_x, cx_v), (cou_y, cy_v))):
        loads[2 + f].wait()
        send(field.at[0], frow.at[f, 1], fw_s.at[f, 0], fw_r.at[f, 1], down)
        send(field.at[63], frow.at[f, 0], fw_s.at[f, 1], fw_r.at[f, 0], up)
        fcs[0, f:f + 1, :] = held[:, :, 0:128].reshape(512, 128).T[0:1]
        fcs[1, f:f + 1, :] = held[:, :, 128:256].reshape(512, 128).T[127:128]
    send(fcs.at[0], fcr.at[0], fc_s.at[0], fc_r.at[0], left)
    send(fcs.at[1], fcr.at[1], fc_s.at[1], fc_r.at[1], right)

    def ring(h):
        for s in range(4):
            for cc in range(2):
                arrived(cg.at[h, y * 8 + 2 * s + cc], s0_r.at[h, 2 * s + cc])
            block = cg.at[h, pl.ds(y * 8 + 2 * s, 2)]
            for t in (2, 1, 3):
                send(block, block, s1_s.at[h, t - 1, s], s1_r.at[h, t - 1, s], place(x, ys[t], z, c))

    ring(0)

    send(fy.at[e], fyb.at[zh, e], g1_s.at[0], g1_r.at[0], place(x, y, zs[4], c))

    for k, (d, dz, cols) in enumerate(F_ONE):
        arrived(fxb.at[c, d, x, :, cols], f1_r.at[k, 0])
    quarter = fxb.at[c, pl.ds(1, 3), x]
    for t in (1, 3):
        send(quarter, quarter, f2_s.at[t // 2], f2_r.at[t // 2], place(xs[t], y, z, c))
    send(quarter, quarter, fr_s.at[0], fr_r.at[0], sib)

    ring(1)

    for k, (d, dz, cols) in enumerate(F_ONE):
        arrived(fxb.at[c, d, x2, :, cols], f1_r.at[k, 1])
    quarter = fxb.at[c, pl.ds(1, 3), x2]
    send(quarter, quarter, fr_s.at[2], fr_r.at[2], sib)

    for t in (1, 3):
        part = fxb.at[c, pl.ds(1, 3), xs[4 - t]]
        arrived(part, f2_r.at[t // 2])
        send(part, part, fr_s.at[t], fr_r.at[t], sib)

    loads[0].wait()
    loads[1].wait()
    arrived(fxb.at[o, 0], fo_r.at[0])
    for t in range(4):
        arrived(fxb.at[o, pl.ds(1, 3), xs[(4 - t) % 4]], fr_r.at[t])

    mine = c * 4 + x
    zo = 1 - zh
    for h in range(2):
        for t in (3, 1, 2):
            for s in range(4):
                arrived(cg.at[h, pl.ds(ys[4 - t] * 8 + 2 * s, 2)], s1_r.at[h, t - 1, s])
        for g in range(2):
            k = 2 * h + g
            rows = pl.ds(g * 128, 128)
            a = fxb[:, 2 * g:2 * g + 2].reshape(256, 2048)
            v = jnp.dot(a, cg[h].reshape(2048, 128), preferred_element_type=F32)
            s1b[h, :, rows] = v.astype(BF16).reshape(2, 128, 128)
            for t in (2, 1, 3):
                for r in range(2):
                    send(s1b.at[h, r, rows], s1g.at[h, mine, rows],
                         s2_s.at[k, t, r], s2_r.at[k, t, c], place(xs[t], y, z, r))
            send(s1b.at[h, o, rows], s1g.at[h, mine, rows], s2_s.at[k, 0, 0], s2_r.at[k, 0, 0], sib)
        s1g[h, mine] = s1b[h, c]
        if h == 0:
            arrived(fyb.at[zo, e], g1_r.at[0])
            for t in (2, 1, 3):
                send(fyb.at[zo, e], fyb.at[zo, e], g2_s.at[t - 1], g2_r.at[t - 1], place(x, ys[t], z, c))
            send(fyb.at[zo, e], fyb.at[zo, e], gr_s.at[0], gr_r.at[0], sib)

    def cols_dot(h, q, hh, g):
        cols = pl.ds(pl.multiple_of(q * 256 + h * 128, 128), 128)
        b = fyb[hh, :, :, cols].reshape(256, 128)
        a = s1g[h, q, g * 128:(g + 1) * 128, :]
        return lax.dot_general(a, b, (((1,), (1,)), ((), ())), preferred_element_type=F32)

    sources = [(0, 0, mine), (0, 0, o * 4 + x)]
    sources += [(t, cc, cc * 4 + xs[4 - t]) for t in (3, 1, 2) for cc in range(2)]

    def level_up(k, hh):
        for h in range(2):
            for g in range(2):
                rows = pl.ds(g * 128, 128)
                for i, (t, cc, q) in enumerate(sources):
                    if i and k == 0:
                        arrived(s1g.at[h, q, rows], s2_r.at[2 * h + g, t, cc])
                    term = cols_dot(h, q, hh, g)
                    acc2[g] = acc2[g] + term if h or i else term
                if h:
                    s2b[hh, 2 * g:2 * g + 2] = acc2[g].astype(BF16).reshape(2, 64, 256)
                    for d in ((1, 0) if g == 0 else (2, 3)):
                        if k or d:
                            send(s2b.at[hh, d], stg.at[z], s3_s.at[k * 4 + d], s3_r.at[k * 4 + d],
                                 place(x, y, hh * 4 + lax.rem(zl + d, 4), c))

    for t in (3, 1, 2):
        eq = ys[4 - t] * 2 + c
        arrived(fyb.at[zo, eq], g2_r.at[t - 1])
        send(fyb.at[zo, eq], fyb.at[zo, eq], gr_s.at[t], gr_r.at[t], sib)
    level_up(0, zh)
    stg[z] = s2b[zh, 0]
    for t in range(4):
        arrived(fyb.at[zo, ys[(4 - t) % 4] * 2 + o], gr_r.at[t])
    level_up(1, zo)

    def spread(l):
        value = stg[l].astype(F32)
        for h in range(2):
            st[h, pl.ds(16 + l, 64, stride=8), :] = value[:, h * 128:(h + 1) * 128]

    for k, hh in ((0, zh), (1, zo)):
        for d in range(4):
            if k or d:
                arrived(stg.at[hh * 4 + lax.rem(zl + 4 - d, 4)], s3_r.at[k * 4 + d])
    for l in range(8):
        spread(l)

    send(st.at[:, pl.ds(16, 16)], st.at[:, pl.ds(528, 16)], h_s.at[0], h_r.at[0], down)
    send(st.at[:, pl.ds(512, 16)], st.at[:, pl.ds(0, 16)], h_s.at[1], h_r.at[1], up)
    for k, (h, at) in enumerate(((1, 520), (0, 520), (1, 16), (0, 16))):
        send(st.at[h, pl.ds(at, 8)], cor.at[k], h_s.at[4 + k], h_r.at[4 + k], corners[k])
    hys[0] = st[0, 16:528, :].T[0:8]
    send(hys.at[0], hyr.at[0], h_s.at[2], h_r.at[2], left)
    hys[1] = st[1, 16:528, :].T[120:128]
    send(hys.at[1], hyr.at[1], h_s.at[3], h_r.at[3], right)
    for f in range(4):
        for k in range(2):
            arrived(frow.at[f, k], fw_r.at[f, k])
    for k in range(2):
        arrived(fcr.at[k], fc_r.at[k])
    arrived(st.at[:, pl.ds(528, 16)], h_r.at[0])
    arrived(st.at[:, pl.ds(0, 16)], h_r.at[1])
    for k in range(2):
        arrived(hyr.at[k], h_r.at[2 + k])
    for k in range(4):
        arrived(cor.at[k], h_r.at[4 + k])

    @pl.when(gx == 0)
    def _():
        st[:, 0:16, :] = jnp.zeros((2, 16, 128), F32)

    @pl.when(gx == 31)
    def _():
        st[:, 528:544, :] = jnp.zeros((2, 16, 128), F32)

    keep_u = jnp.where(gx == 0, 0.0, 1.0).astype(F32)
    keep_d = jnp.where(gx == 31, 0.0, 1.0).astype(F32)
    keep_l = jnp.where(gy == 0, 0.0, 1.0).astype(F32)
    keep_r = jnp.where(gy == 7, 0.0, 1.0).astype(F32)
    cor[0] = cor[0] * (keep_u * keep_l)
    cor[1] = cor[1] * (keep_u * keep_r)
    cor[2] = cor[2] * (keep_d * keep_l)
    cor[3] = cor[3] * (keep_d * keep_r)
    beyond_l = hyr[1, 6:8, :] * keep_l
    beyond_r = hyr[0, 0:2, :] * keep_r
    hr[...] = jnp.broadcast_to(beyond_r[0:1], (128, 512)).T
    hl[...] = jnp.broadcast_to(beyond_l[1:2], (128, 512)).T

    def beside(v0, v1, left_halo, right_halo):
        lane = lax.broadcasted_iota(jnp.int32, v0.shape, 1)
        f0, f1 = pltpu.roll(v0, 127, 1), pltpu.roll(v1, 127, 1)
        b0, b1 = pltpu.roll(v0, 1, 1), pltpu.roll(v1, 1, 1)
        after = (jnp.where(lane == 127, f1, f0), jnp.where(lane == 127, right_halo, f1))
        before = (jnp.where(lane == 0, left_halo, b0), jnp.where(lane == 0, b0, b1))
        return before, after

    for k, at, to, keep in ((0, 8, 0, keep_u), (1, 528, 520, keep_d)):
        v = [st[h, at:at + 8, :] for h in range(2)]
        before, after = beside(v[0], v[1], pltpu.roll(cor[2 * k], 1, 1), pltpu.roll(cor[2 * k + 1], 127, 1))
        for h in range(2):
            ln = slice(h * 128, (h + 1) * 128)
            cx, cy = frow[2, k, :, ln], frow[3, k, :, ln]
            end = (v[h] - cx * (st[h, at + 8:at + 16, :] - st[h, at - 8:at, :]) * 0.5
                   - cy * (after[h] - before[h]) * 0.5)
            qx[h, to:to + 8, :] = keep * cx * (frow[1, k, :, ln] * (end - frow[0, k, :, ln]))

    spot = lax.broadcasted_iota(jnp.int32, (8, 512), 1)
    level = lax.broadcasted_iota(jnp.int32, (8, 512), 0)
    ahead = lax.broadcasted_iota(jnp.int32, (1, 512), 1)

    def along(k, at):
        column = jnp.broadcast_to(cor[k][:, at:at + 1], (8, 512))
        return jnp.sum(jnp.where(lax.rem(spot, 8) == level, column, 0.0), axis=0, keepdims=True)

    def flux(k, value, low, high, first, last, keep):
        prev = jnp.where(ahead < 8, first, pltpu.roll(value, 8, 1))
        post = jnp.where(ahead >= 504, last, pltpu.roll(value, 504, 1))
        inn, wei, cx, cy = [fcr[k, f:f + 1, :] for f in range(4)]
        end = value - cx * (post - prev) * 0.5 - cy * (high - low) * 0.5
        return jnp.broadcast_to(keep * cy * (wei * (end - inn)), (128, 512)).T

    ql[...] = flux(1, beyond_l[1:2], beyond_l[0:1], hys[0, 0:1, :], along(0, 127), along(2, 127), keep_l)
    qr[...] = flux(0, beyond_r[0:1], hys[1, 7:8, :], beyond_r[1:2], along(1, 0), along(3, 0), keep_r)

    @pl.loop(0, 8)
    def _(i):
        at = pl.multiple_of(i * 64, 64)
        xr = pl.ds(i * 8, 8)
        v = [st[h, pl.ds(at + 16, 64), :] for h in range(2)]
        before, after = beside(v[0], v[1], hl[pl.ds(at, 64), :], hr[pl.ds(at, 64), :])
        for h in range(2):
            ln = slice(h * 128, (h + 1) * 128)
            cx = cx_v[xr, :, ln].reshape(64, 128)
            cy = cy_v[xr, :, ln].reshape(64, 128)
            prev = st[h, pl.ds(at + 8, 64), :]
            post = st[h, pl.ds(at + 24, 64), :]
            end = v[h] - cx * (post - prev) * 0.5 - cy * (after[h] - before[h]) * 0.5
            end_out[xr, :, ln] = end.reshape(8, 8, 128)
            m = wei_v[xr, :, ln].reshape(64, 128) * (end - inn_v[xr, :, ln].reshape(64, 128))
            mis[h, pl.ds(at, 64), :] = m
            qx[h, pl.ds(at + 8, 64), :] = cx * m
            py[h, pl.ds(at, 64), :] = cy * m

    @pl.loop(0, 8)
    def _(i):
        at = pl.multiple_of(i * 64, 64)
        v = [py[h, pl.ds(at, 64), :] for h in range(2)]
        before, after = beside(v[0], v[1], ql[pl.ds(at, 64), :], qr[pl.ds(at, 64), :])
        for h in range(2):
            prev = qx[h, pl.ds(at, 64), :]
            post = qx[h, pl.ds(at + 16, 64), :]
            adj[h, pl.ds(at, 64), :] = (
                mis[h, pl.ds(at, 64), :] + 0.5 * (post - prev) + 0.5 * (after[h] - before[h]))

    for l in range(8):
        for h in range(2):
            ags[l, :, h * 128:(h + 1) * 128] = adj[h, pl.ds(l, 64, stride=8), :].astype(BF16)

    for t in (4, 3, 7, 2, 6, 5, 1):
        send(ags.at[zs[t]], ag.at[zh, (4 - t % 4) % 4], s5_s.at[t - 1], s5_r.at[t - 1], place(x, y, zs[t], c))
    ag[zh, 0] = ags[z]

    def share(g, q):
        cols = pl.ds(pl.multiple_of(q * 256, 256), 256)
        total = None
        for hh in range(2):
            a = ag[hh, 2 * g:2 * g + 2].reshape(128, 256)
            b = fyb[hh, :, :, cols].reshape(256, 256)
            term = jnp.dot(a, b, preferred_element_type=F32)
            total = term if total is None else total + term
        return total

    targets = [(t, r, r * 4 + xs[t], place(xs[t], y, z, r)) for t in (2, 1, 3) for r in range(2)]
    targets += [(0, 0, o * 4 + x, sib)]

    def hand(h, k, rows):
        for t, r, q, dev in targets:
            send(psend.at[h, t, r, rows], pg.at[h, t, c, rows],
                 s6_s.at[k, t, r], s6_r.at[k, t, c], dev)

    for g in range(2):
        rows = pl.ds(g * 128, 128)
        for t in ((4, 3, 7) if g == 0 else (2, 6, 5, 1)):
            arrived(ag.at[zs[8 - t] // 4, (4 - t % 4) % 4], s5_r.at[t - 1])
        for t, r, q, dev in targets:
            value = share(g, q).astype(BF16)
            for h in range(2):
                psend[h, t, r, rows] = value[:, h * 128:(h + 1) * 128]
            send(psend.at[0, t, r, rows], pg.at[0, t, c, rows],
                 s6_s.at[g, t, r], s6_r.at[g, t, c], dev)
        value = share(g, mine)
        for h in range(2):
            pown[h, rows] = value[:, h * 128:(h + 1) * 128]

    def lines(h, q, part):
        cols = pl.ds(pl.multiple_of(q * 512 + part * 256, 256), 256)
        a = fxb[:, :, :, :, cols].reshape(512, 256)
        b = pb[h].reshape(512, 128)
        return lax.dot_general(a, b, (((0,), (0,)), ((), ())), preferred_element_type=F32)

    def three(h, r):
        return pg[h, 1, r].astype(F32) + pg[h, 2, r].astype(F32) + pg[h, 3, r].astype(F32)

    for h in range(2):
        for k, rows in ((0, pl.ds(0, 128)), (1, pl.ds(128, 128))) if h == 0 else ((2, pl.ds(0, 256)),):
            arrived(pg.at[h, 0, o, rows], s6_r.at[k, 0, o])
            for t in (1, 3, 2):
                for cc in range(2):
                    arrived(pg.at[h, t, cc, rows], s6_r.at[k, t, cc])
            if k == 0:
                hand(1, 2, pl.ds(0, 256))
        pb[h, c] = (three(h, c) + pown[h]).astype(BF16)
        pb[h, o] = (three(h, o) + pg[h, 0, o].astype(F32)).astype(BF16)
        for part in range(2):
            rows = pl.ds(part * 256, 256)
            for t in (2, 1, 3):
                gsend[h, t - 1, rows] = lines(h, ys[t], part).astype(BF16)
                send(gsend.at[h, t - 1, rows], gg.at[h, t - 1, rows],
                     s7_s.at[h, part, t - 1], s7_r.at[h, part, t - 1], place(x, ys[t], z, c))
        for part in range(2):
            gown[h, pl.ds(part * 256, 256)] = lines(h, y, part)

    far8 = []
    for h in range(2):
        for part in range(2):
            rows = pl.ds(part * 256, 256)
            total = gown[h, rows]
            for t in (1, 3, 2):
                arrived(gg.at[h, t - 1, rows], s7_r.at[h, part, t - 1])
                total += gg[h, t - 1, rows].astype(F32)
            gs[h, 4 * part:4 * part + 4] = total.astype(BF16).reshape(4, 64, 128)
            for zq in (2 * part, 2 * part + 1):
                send(gs.at[h, zq * 2 + o], go.at[h, z], s8_s.at[h, zq, 1], s8_r.at[h, z],
                     place(x, y, c * 4 + zq, o))
                here = jnp.logical_and(zl == zq, zh == c)
                src, dst = gs.at[h, zq * 2 + c], go.at[h, z]
                own = pltpu.make_async_copy(src, dst, s8_r.at[h, z])
                far = pltpu.make_async_remote_copy(
                    src_ref=src, dst_ref=dst, send_sem=s8_s.at[h, zq, 0], recv_sem=s8_r.at[h, z],
                    device_id=place(x, y, c * 4 + zq, c), device_id_type=MESH)
                pl.when(here)(own.start)
                pl.when(jnp.logical_not(here))(far.start)
                far8.append((here, far))

    for h in range(2):
        ln = slice(h * 128, (h + 1) * 128)
        for l in range(8):
            arrived(go.at[h, l], s8_r.at[h, l])
        for l in range(8):
            nat[h, pl.ds(l, 64, stride=8), :] = go[h, l].astype(F32)
        grad_out[:, :, ln] = ctl_v[:, :, ln].astype(F32) + nat[h].reshape(64, 8, 128)
    for copy in pending:
        copy.wait_send()

    @pl.when(zh != c)
    def _():
        for h in range(2):
            far0[h].wait_send()

    for here, far in far8:
        pl.when(jnp.logical_not(here))(far.wait_send)


def per_device(control, innovation, obs_weight, courant_x, courant_y, filter_x, filter_y):
    dma = lambda *shape: pltpu.SemaphoreType.DMA(shape)
    big = pltpu.VMEM((64, 8, 256), F32)
    half = pltpu.VMEM((2, 512, 128), F32)
    ext = pltpu.VMEM((2, 528, 128), F32)
    col = pltpu.VMEM((512, 128), F32)
    lev = pltpu.VMEM((8, 64, 256), BF16)
    levh = pltpu.VMEM((2, 8, 64, 128), BF16)
    halo = pltpu.VMEM((2, 8, 512), F32)
    planes = pltpu.VMEM((2, 4, 64, 256), BF16)
    shares = pltpu.VMEM((2, 4, 2, 256, 128), BF16)
    sums = pltpu.VMEM((2, 3, 512, 128), BF16)
    scratch = [
        pltpu.VMEM((64, 8, 256), BF16), big, big, big, big,
        half, levh,
        pltpu.VMEM((2, 32, 64, 128), BF16),
        pltpu.VMEM((2, 4, 4, 16, 2048), BF16),
        pltpu.VMEM((2, 8, 32, 2048), BF16),
        pltpu.VMEM((2, 2, 256, 128), BF16),
        pltpu.VMEM((2, 8, 256, 128), BF16),
        pltpu.VMEM((2, 128, 256), F32),
        planes, lev,
        pltpu.VMEM((2, 544, 128), F32), halo, halo,
        pltpu.VMEM((4, 8, 128), F32),
        pltpu.VMEM((4, 2, 8, 256), F32), halo, halo,
        col, col, col, col, ext, half, half, half, lev, planes,
        shares,
        pltpu.VMEM((2, 256, 128), F32),
        shares,
        pltpu.VMEM((2, 2, 256, 128), BF16),
        sums,
        pltpu.VMEM((2, 512, 128), F32),
        sums, levh, levh,
        dma(7), dma(4, 2), dma(4, 2), dma(1), dma(1), dma(2), dma(2), dma(4), dma(4),
        dma(1), dma(1), dma(3), dma(3), dma(4), dma(4),
        dma(2, 8), dma(2, 8), dma(2, 3, 4), dma(2, 3, 4), dma(4, 4, 2), dma(4, 4, 2), dma(8), dma(8),
        dma(8), dma(8), dma(4, 2), dma(4, 2), dma(2), dma(2), dma(7), dma(7), dma(3, 4, 2), dma(3, 4, 2),
        dma(2, 2, 3), dma(2, 2, 3), dma(2, 4, 2), dma(2, 8),
    ]
    out = pltpu.VMEM((64, 8, 256), F32)
    anywhere = pl.BlockSpec(memory_space=pl.ANY)
    return pl.pallas_call(
        kernel,
        out_shape=(out, out),
        in_specs=[anywhere] * 7,
        out_specs=(pl.BlockSpec(memory_space=pltpu.VMEM),) * 2,
        scratch_shapes=scratch,
        compiler_params=pltpu.CompilerParams(
            collective_id=0, has_side_effects=True, vmem_limit_bytes=62 * 1024 * 1024),
        cost_estimate=pl.CostEstimate(flops=2150000000, bytes_accessed=5000000, transcendentals=0),
    )(control, innovation, obs_weight, courant_x, courant_y,
      filter_x.reshape(4, 16, 2048), filter_y.reshape(8, 32, 2048))


def solution(mesh):
    grid = P("gx", None, "gy")
    placed = (grid, grid, grid, grid, grid, P("gx", None), P("gy", None))
    return jax.shard_map(
        per_device, mesh=mesh, in_specs=placed, out_specs=(grid, grid), check_vma=False)
```

```python
import jax
import jax.numpy as jnp
from jax import lax
from jax.experimental import pallas as pl
from jax.experimental.pallas import tpu as pltpu
from jax.sharding import PartitionSpec as P

MESH = pl.DeviceIdType.MESH
F32 = jnp.float32
BF16 = jnp.bfloat16
F_ONE = ((2, 2, pl.ds(0, 1024)), (2, 6, pl.ds(1024, 1024)), (1, 7, pl.ds(0, 2048)), (3, 1, pl.ds(0, 2048)))


def place(x, y, z, c):
    return (y * 8 + lax.rem(z, 4) * 2 + c, (z // 4) * 4 + x)


def kernel(
    ctl, innov, weight, cou_x, cou_y, fx, fy,
    end_out, grad_out,
    ctl_v, inn_v, wei_v, cx_v, cy_v,
    nat, snd0, cg, fxb, fyb, s1b, s1g, acc2, s2b, stg,
    st, hys, hyr, cor, frow, fcs, fcr, hl, hr, ql, qr, qx, py, mis, adj, ags, ag,
    psend, pown, pg, pb, gsend, gown, gg, gs, go,
    loc_sem, f1_s, f1_r, fo_s, fo_r, f2_s, f2_r, fr_s, fr_r,
    g1_s, g1_r, g2_s, g2_r, gr_s, gr_r,
    s0_s, s0_r, s1_s, s1_r, s2_s, s2_r, s3_s, s3_r,
    h_s, h_r, fw_s, fw_r, fc_s, fc_r, s5_s, s5_r, s6_s, s6_r, s7_s, s7_r, s8_s, s8_r,
):
    gx = lax.axis_index("gx")
    gy = lax.axis_index("gy")
    y = gx // 8
    zl = lax.rem(gx // 2, 4)
    c = lax.rem(gx, 2)
    zh = gy // 4
    x = lax.rem(gy, 4)
    z = zh * 4 + zl
    o = 1 - c
    sib = place(x, y, z, o)
    e = y * 2 + c
    pending = []

    def send(src, dst, ssem, rsem, dev):
        copy = pltpu.make_async_remote_copy(
            src_ref=src, dst_ref=dst, send_sem=ssem, recv_sem=rsem,
            device_id=dev, device_id_type=MESH)
        copy.start()
        pending.append(copy)

    def arrived(dst, rsem):
        pltpu.make_async_copy(dst, dst, rsem).wait()

    xs = [lax.rem(x + t, 4) for t in range(4)]
    ys = [lax.rem(y + t, 4) for t in range(4)]
    zs = [lax.rem(z + t, 8) for t in range(8)]
    up = (lax.rem(gx + 1, 32), gy)
    down = (lax.rem(gx + 31, 32), gy)
    right = (gx, lax.rem(gy + 1, 8))
    left = (gx, lax.rem(gy + 7, 8))
    corners = [(up[0], right[1]), (up[0], left[1]), (down[0], right[1]), (down[0], left[1])]

    load_ctl = pltpu.make_async_copy(ctl, ctl_v, loc_sem.at[0])
    load_ctl.start()
    loads = [
        pltpu.make_async_copy(s, d, loc_sem.at[1 + i])
        for i, (s, d) in enumerate([
            (fx, fxb.at[c, 0]), (fy, fyb.at[zh]), (innov, inn_v),
            (weight, wei_v), (cou_x, cx_v), (cou_y, cy_v)])
    ]
    for load in loads:
        load.start()

    barrier = pltpu.get_barrier_semaphore()
    partners = [sib]
    for t in range(1, 8):
        partners += [place(x, y, zs[t], c), place(x, y, zs[t], o)]
    for t in range(1, 4):
        partners += [place(xs[t], y, z, c), place(xs[t], y, z, o)]
        partners += [place(x, ys[t], z, c)]
    partners += [up, down, left, right] + corners
    for dev in partners:
        pl.semaphore_signal(barrier, inc=1, device_id=dev, device_id_type=MESH)

    load_ctl.wait()
    for h in range(2):
        nat[h] = ctl_v[:, :, h * 128:(h + 1) * 128].astype(F32).reshape(512, 128)
    for l in range(8):
        for h in range(2):
            snd0[h, l] = nat[h, pl.ds(l, 64, stride=8), :].astype(BF16)

    pl.semaphore_wait(barrier, len(partners))

    slot0 = zl * 2 + c
    x2 = xs[2]
    own0, far0 = [], []
    for h in range(2):
        for t in (4, 3, 5, 2, 6, 1, 7):
            send(snd0.at[h, zs[t]], cg.at[h, gx], s0_s.at[h, t], s0_r.at[h, slot0], place(x, y, zs[t], zh))
        src, dst = snd0.at[h, z], cg.at[h, gx]
        own0.append(pltpu.make_async_copy(src, dst, s0_r.at[h, slot0]))
        far0.append(pltpu.make_async_remote_copy(
            src_ref=src, dst_ref=dst, send_sem=s0_s.at[h, 0], recv_sem=s0_r.at[h, slot0],
            device_id=sib, device_id_type=MESH))

        @pl.when(zh == c)
        def _():
            own0[h].start()

        @pl.when(zh != c)
        def _():
            far0[h].start()

        q = x2 if h else x
        for k, (d, dz, cols) in enumerate(F_ONE):
            send(fx.at[q, :, cols], fxb.at[c, d, q, :, cols], f1_s.at[k, h], f1_r.at[k, h], place(x, y, zs[dz], c))

    send(fx, fxb.at[c, 0], fo_s.at[0], fo_r.at[0], sib)

    for f, (field, held) in enumerate(((innov, inn_v), (weight, wei_v), (cou_x, cx_v), (cou_y, cy_v))):
        loads[2 + f].wait()
        send(field.at[0], frow.at[f, 1], fw_s.at[f, 0], fw_r.at[f, 1], down)
        send(field.at[63], frow.at[f, 0], fw_s.at[f, 1], fw_r.at[f, 0], up)
        fcs[0, f:f + 1, :] = held[:, :, 0:128].reshape(512, 128).T[0:1]
        fcs[1, f:f + 1, :] = held[:, :, 128:256].reshape(512, 128).T[127:128]
    send(fcs.at[0], fcr.at[0], fc_s.at[0], fc_r.at[0], left)
    send(fcs.at[1], fcr.at[1], fc_s.at[1], fc_r.at[1], right)

    def ring(h):
        for s in range(4):
            for cc in range(2):
                arrived(cg.at[h, y * 8 + 2 * s + cc], s0_r.at[h, 2 * s + cc])
            block = cg.at[h, pl.ds(y * 8 + 2 * s, 2)]
            for t in (2, 1, 3):
                send(block, block, s1_s.at[h, t - 1, s], s1_r.at[h, t - 1, s], place(x, ys[t], z, c))

    ring(0)

    send(fy.at[e], fyb.at[zh, e], g1_s.at[0], g1_r.at[0], place(x, y, zs[4], c))

    for k, (d, dz, cols) in enumerate(F_ONE):
        arrived(fxb.at[c, d, x, :, cols], f1_r.at[k, 0])
    quarter = fxb.at[c, pl.ds(1, 3), x]
    for t in (1, 3):
        send(quarter, quarter, f2_s.at[t // 2], f2_r.at[t // 2], place(xs[t], y, z, c))
    send(quarter, quarter, fr_s.at[0], fr_r.at[0], sib)

    ring(1)

    for k, (d, dz, cols) in enumerate(F_ONE):
        arrived(fxb.at[c, d, x2, :, cols], f1_r.at[k, 1])
    quarter = fxb.at[c, pl.ds(1, 3), x2]
    send(quarter, quarter, fr_s.at[2], fr_r.at[2], sib)

    for t in (1, 3):
        part = fxb.at[c, pl.ds(1, 3), xs[4 - t]]
        arrived(part, f2_r.at[t // 2])
        send(part, part, fr_s.at[t], fr_r.at[t], sib)

    loads[0].wait()
    loads[1].wait()
    arrived(fxb.at[o, 0], fo_r.at[0])
    for t in range(4):
        arrived(fxb.at[o, pl.ds(1, 3), xs[(4 - t) % 4]], fr_r.at[t])

    mine = c * 4 + x
    zo = 1 - zh
    for h in range(2):
        for t in (3, 1, 2):
            for s in range(4):
                arrived(cg.at[h, pl.ds(ys[4 - t] * 8 + 2 * s, 2)], s1_r.at[h, t - 1, s])
        for g in range(2):
            k = 2 * h + g
            rows = pl.ds(g * 128, 128)
            a = fxb[:, 2 * g:2 * g + 2].reshape(256, 2048)
            v = jnp.dot(a, cg[h].reshape(2048, 128), preferred_element_type=F32)
            s1b[h, :, rows] = v.astype(BF16).reshape(2, 128, 128)
            for t in (2, 1, 3):
                for r in range(2):
                    send(s1b.at[h, r, rows], s1g.at[h, mine, rows],
                         s2_s.at[k, t, r], s2_r.at[k, t, c], place(xs[t], y, z, r))
            send(s1b.at[h, o, rows], s1g.at[h, mine, rows], s2_s.at[k, 0, 0], s2_r.at[k, 0, 0], sib)
        s1g[h, mine] = s1b[h, c]
        if h == 0:
            arrived(fyb.at[zo, e], g1_r.at[0])
            for t in (2, 1, 3):
                send(fyb.at[zo, e], fyb.at[zo, e], g2_s.at[t - 1], g2_r.at[t - 1], place(x, ys[t], z, c))
            send(fyb.at[zo, e], fyb.at[zo, e], gr_s.at[0], gr_r.at[0], sib)

    def cols_dot(h, q, hh, g):
        cols = pl.ds(pl.multiple_of(q * 256 + h * 128, 128), 128)
        b = fyb[hh, :, :, cols].reshape(256, 128)
        a = s1g[h, q, g * 128:(g + 1) * 128, :]
        return lax.dot_general(a, b, (((1,), (1,)), ((), ())), preferred_element_type=F32)

    sources = [(0, 0, mine), (0, 0, o * 4 + x)]
    sources += [(t, cc, cc * 4 + xs[4 - t]) for t in (3, 1, 2) for cc in range(2)]

    def level_up(k, hh):
        for h in range(2):
            for g in range(2):
                rows = pl.ds(g * 128, 128)
                for i, (t, cc, q) in enumerate(sources):
                    if i and k == 0:
                        arrived(s1g.at[h, q, rows], s2_r.at[2 * h + g, t, cc])
                    term = cols_dot(h, q, hh, g)
                    acc2[g] = acc2[g] + term if h or i else term
                if h:
                    s2b[hh, 2 * g:2 * g + 2] = acc2[g].astype(BF16).reshape(2, 64, 256)
                    for d in ((1, 0) if g == 0 else (2, 3)):
                        if k or d:
                            send(s2b.at[hh, d], stg.at[z], s3_s.at[k * 4 + d], s3_r.at[k * 4 + d],
                                 place(x, y, hh * 4 + lax.rem(zl + d, 4), c))

    for t in (3, 1, 2):
        eq = ys[4 - t] * 2 + c
        arrived(fyb.at[zo, eq], g2_r.at[t - 1])
        send(fyb.at[zo, eq], fyb.at[zo, eq], gr_s.at[t], gr_r.at[t], sib)
    level_up(0, zh)
    stg[z] = s2b[zh, 0]
    for t in range(4):
        arrived(fyb.at[zo, ys[(4 - t) % 4] * 2 + o], gr_r.at[t])
    level_up(1, zo)

    def spread(l):
        value = stg[l].astype(F32)
        for h in range(2):
            st[h, pl.ds(16 + l, 64, stride=8), :] = value[:, h * 128:(h + 1) * 128]

    for k, hh in ((0, zh), (1, zo)):
        for d in range(4):
            if k or d:
                arrived(stg.at[hh * 4 + lax.rem(zl + 4 - d, 4)], s3_r.at[k * 4 + d])
    for l in range(8):
        spread(l)

    send(st.at[:, pl.ds(16, 16)], st.at[:, pl.ds(528, 16)], h_s.at[0], h_r.at[0], down)
    send(st.at[:, pl.ds(512, 16)], st.at[:, pl.ds(0, 16)], h_s.at[1], h_r.at[1], up)
    for k, (h, at) in enumerate(((1, 520), (0, 520), (1, 16), (0, 16))):
        send(st.at[h, pl.ds(at, 8)], cor.at[k], h_s.at[4 + k], h_r.at[4 + k], corners[k])
    hys[0] = st[0, 16:528, :].T[0:8]
    send(hys.at[0], hyr.at[0], h_s.at[2], h_r.at[2], left)
    hys[1] = st[1, 16:528, :].T[120:128]
    send(hys.at[1], hyr.at[1], h_s.at[3], h_r.at[3], right)
    for f in range(4):
        for k in range(2):
            arrived(frow.at[f, k], fw_r.at[f, k])
    for k in range(2):
        arrived(fcr.at[k], fc_r.at[k])
    arrived(st.at[:, pl.ds(528, 16)], h_r.at[0])
    arrived(st.at[:, pl.ds(0, 16)], h_r.at[1])
    for k in range(2):
        arrived(hyr.at[k], h_r.at[2 + k])
    for k in range(4):
        arrived(cor.at[k], h_r.at[4 + k])

    @pl.when(gx == 0)
    def _():
        st[:, 0:16, :] = jnp.zeros((2, 16, 128), F32)

    @pl.when(gx == 31)
    def _():
        st[:, 528:544, :] = jnp.zeros((2, 16, 128), F32)

    keep_u = jnp.where(gx == 0, 0.0, 1.0).astype(F32)
    keep_d = jnp.where(gx == 31, 0.0, 1.0).astype(F32)
    keep_l = jnp.where(gy == 0, 0.0, 1.0).astype(F32)
    keep_r = jnp.where(gy == 7, 0.0, 1.0).astype(F32)
    cor[0] = cor[0] * (keep_u * keep_l)
    cor[1] = cor[1] * (keep_u * keep_r)
    cor[2] = cor[2] * (keep_d * keep_l)
    cor[3] = cor[3] * (keep_d * keep_r)
    beyond_l = hyr[1, 6:8, :] * keep_l
    beyond_r = hyr[0, 0:2, :] * keep_r
    hr[...] = jnp.broadcast_to(beyond_r[0:1], (128, 512)).T
    hl[...] = jnp.broadcast_to(beyond_l[1:2], (128, 512)).T

    def beside(v0, v1, left_halo, right_halo):
        lane = lax.broadcasted_iota(jnp.int32, v0.shape, 1)
        f0, f1 = pltpu.roll(v0, 127, 1), pltpu.roll(v1, 127, 1)
        b0, b1 = pltpu.roll(v0, 1, 1), pltpu.roll(v1, 1, 1)
        after = (jnp.where(lane == 127, f1, f0), jnp.where(lane == 127, right_halo, f1))
        before = (jnp.where(lane == 0, left_halo, b0), jnp.where(lane == 0, b0, b1))
        return before, after

    for k, at, to, keep in ((0, 8, 0, keep_u), (1, 528, 520, keep_d)):
        v = [st[h, at:at + 8, :] for h in range(2)]
        before, after = beside(v[0], v[1], pltpu.roll(cor[2 * k], 1, 1), pltpu.roll(cor[2 * k + 1], 127, 1))
        for h in range(2):
            ln = slice(h * 128, (h + 1) * 128)
            cx, cy = frow[2, k, :, ln], frow[3, k, :, ln]
            end = (v[h] - cx * (st[h, at + 8:at + 16, :] - st[h, at - 8:at, :]) * 0.5
                   - cy * (after[h] - before[h]) * 0.5)
            qx[h, to:to + 8, :] = keep * cx * (frow[1, k, :, ln] * (end - frow[0, k, :, ln]))

    spot = lax.broadcasted_iota(jnp.int32, (8, 512), 1)
    level = lax.broadcasted_iota(jnp.int32, (8, 512), 0)
    ahead = lax.broadcasted_iota(jnp.int32, (1, 512), 1)

    def along(k, at):
        column = jnp.broadcast_to(cor[k][:, at:at + 1], (8, 512))
        return jnp.sum(jnp.where(lax.rem(spot, 8) == level, column, 0.0), axis=0, keepdims=True)

    def flux(k, value, low, high, first, last, keep):
        prev = jnp.where(ahead < 8, first, pltpu.roll(value, 8, 1))
        post = jnp.where(ahead >= 504, last, pltpu.roll(value, 504, 1))
        inn, wei, cx, cy = [fcr[k, f:f + 1, :] for f in range(4)]
        end = value - cx * (post - prev) * 0.5 - cy * (high - low) * 0.5
        return jnp.broadcast_to(keep * cy * (wei * (end - inn)), (128, 512)).T

    ql[...] = flux(1, beyond_l[1:2], beyond_l[0:1], hys[0, 0:1, :], along(0, 127), along(2, 127), keep_l)
    qr[...] = flux(0, beyond_r[0:1], hys[1, 7:8, :], beyond_r[1:2], along(1, 0), along(3, 0), keep_r)

    @pl.loop(0, 8)
    def _(i):
        at = pl.multiple_of(i * 64, 64)
        xr = pl.ds(i * 8, 8)
        v = [st[h, pl.ds(at + 16, 64), :] for h in range(2)]
        before, after = beside(v[0], v[1], hl[pl.ds(at, 64), :], hr[pl.ds(at, 64), :])
        for h in range(2):
            ln = slice(h * 128, (h + 1) * 128)
            cx = cx_v[xr, :, ln].reshape(64, 128)
            cy = cy_v[xr, :, ln].reshape(64, 128)
            prev = st[h, pl.ds(at + 8, 64), :]
            post = st[h, pl.ds(at + 24, 64), :]
            end = v[h] - cx * (post - prev) * 0.5 - cy * (after[h] - before[h]) * 0.5
            end_out[xr, :, ln] = end.reshape(8, 8, 128)
            m = wei_v[xr, :, ln].reshape(64, 128) * (end - inn_v[xr, :, ln].reshape(64, 128))
            mis[h, pl.ds(at, 64), :] = m
            qx[h, pl.ds(at + 8, 64), :] = cx * m
            py[h, pl.ds(at, 64), :] = cy * m

    @pl.loop(0, 8)
    def _(i):
        at = pl.multiple_of(i * 64, 64)
        v = [py[h, pl.ds(at, 64), :] for h in range(2)]
        before, after = beside(v[0], v[1], ql[pl.ds(at, 64), :], qr[pl.ds(at, 64), :])
        for h in range(2):
            prev = qx[h, pl.ds(at, 64), :]
            post = qx[h, pl.ds(at + 16, 64), :]
            adj[h, pl.ds(at, 64), :] = (
                mis[h, pl.ds(at, 64), :] + 0.5 * (post - prev) + 0.5 * (after[h] - before[h]))

    for l in range(8):
        for h in range(2):
            ags[l, :, h * 128:(h + 1) * 128] = adj[h, pl.ds(l, 64, stride=8), :].astype(BF16)

    for t in (4, 3, 7, 2, 6, 5, 1):
        send(ags.at[zs[t]], ag.at[zh, (4 - t % 4) % 4], s5_s.at[t - 1], s5_r.at[t - 1], place(x, y, zs[t], c))
    ag[zh, 0] = ags[z]

    def share(g, q):
        cols = pl.ds(pl.multiple_of(q * 256, 256), 256)
        total = None
        for hh in range(2):
            a = ag[hh, 2 * g:2 * g + 2].reshape(128, 256)
            b = fyb[hh, :, :, cols].reshape(256, 256)
            term = jnp.dot(a, b, preferred_element_type=F32)
            total = term if total is None else total + term
        return total

    targets = [(t, r, r * 4 + xs[t], place(xs[t], y, z, r)) for t in (2, 1, 3) for r in range(2)]
    targets += [(0, 0, o * 4 + x, sib)]

    def hand(h, k, rows):
        for t, r, q, dev in targets:
            send(psend.at[h, t, r, rows], pg.at[h, t, c, rows],
                 s6_s.at[k, t, r], s6_r.at[k, t, c], dev)

    for g in range(2):
        rows = pl.ds(g * 128, 128)
        for t in ((4, 3, 7) if g == 0 else (2, 6, 5, 1)):
            arrived(ag.at[zs[8 - t] // 4, (4 - t % 4) % 4], s5_r.at[t - 1])
        for t, r, q, dev in targets:
            value = share(g, q).astype(BF16)
            for h in range(2):
                psend[h, t, r, rows] = value[:, h * 128:(h + 1) * 128]
            send(psend.at[0, t, r, rows], pg.at[0, t, c, rows],
                 s6_s.at[g, t, r], s6_r.at[g, t, c], dev)
        value = share(g, mine)
        for h in range(2):
            pown[h, rows] = value[:, h * 128:(h + 1) * 128]

    def lines(h, q, part):
        cols = pl.ds(pl.multiple_of(q * 512 + part * 256, 256), 256)
        a = fxb[:, :, :, :, cols].reshape(512, 256)
        b = pb[h].reshape(512, 128)
        return lax.dot_general(a, b, (((0,), (0,)), ((), ())), preferred_element_type=F32)

    def three(h, r):
        return pg[h, 1, r].astype(F32) + pg[h, 2, r].astype(F32) + pg[h, 3, r].astype(F32)

    for h in range(2):
        for k, rows in ((0, pl.ds(0, 128)), (1, pl.ds(128, 128))) if h == 0 else ((2, pl.ds(0, 256)),):
            arrived(pg.at[h, 0, o, rows], s6_r.at[k, 0, o])
            for t in (1, 3, 2):
                for cc in range(2):
                    arrived(pg.at[h, t, cc, rows], s6_r.at[k, t, cc])
            if k == 0:
                hand(1, 2, pl.ds(0, 256))
        pb[h, c] = (three(h, c) + pown[h]).astype(BF16)
        pb[h, o] = (three(h, o) + pg[h, 0, o].astype(F32)).astype(BF16)
        for part in range(2):
            rows = pl.ds(part * 256, 256)
            for t in (2, 1, 3):
                gsend[h, t - 1, rows] = lines(h, ys[t], part).astype(BF16)
                send(gsend.at[h, t - 1, rows], gg.at[h, t - 1, rows],
                     s7_s.at[h, part, t - 1], s7_r.at[h, part, t - 1], place(x, ys[t], z, c))
        for part in range(2):
            gown[h, pl.ds(part * 256, 256)] = lines(h, y, part)

    early = len(pending)
    far8 = []
    for h in range(2):
        for part in range(2):
            rows = pl.ds(part * 256, 256)
            total = gown[h, rows]
            for t in (1, 3, 2):
                arrived(gg.at[h, t - 1, rows], s7_r.at[h, part, t - 1])
                total += gg[h, t - 1, rows].astype(F32)
            gs[h, 4 * part:4 * part + 4] = total.astype(BF16).reshape(4, 64, 128)
            for zq in (2 * part, 2 * part + 1):
                send(gs.at[h, zq * 2 + o], go.at[h, z], s8_s.at[h, zq, 1], s8_r.at[h, z],
                     place(x, y, c * 4 + zq, o))
                here = jnp.logical_and(zl == zq, zh == c)
                src, dst = gs.at[h, zq * 2 + c], go.at[h, z]
                own = pltpu.make_async_copy(src, dst, s8_r.at[h, z])
                far = pltpu.make_async_remote_copy(
                    src_ref=src, dst_ref=dst, send_sem=s8_s.at[h, zq, 0], recv_sem=s8_r.at[h, z],
                    device_id=place(x, y, c * 4 + zq, c), device_id_type=MESH)
                pl.when(here)(own.start)
                pl.when(jnp.logical_not(here))(far.start)
                far8.append((here, far))

    for copy in pending[:early]:
        copy.wait_send()

    @pl.when(zh != c)
    def _():
        for h in range(2):
            far0[h].wait_send()

    for h in range(2):
        ln = slice(h * 128, (h + 1) * 128)
        for l in range(8):
            arrived(go.at[h, l], s8_r.at[h, l])
        for l in range(8):
            nat[h, pl.ds(l, 64, stride=8), :] = go[h, l].astype(F32)
        grad_out[:, :, ln] = ctl_v[:, :, ln].astype(F32) + nat[h].reshape(64, 8, 128)
    for copy in pending[early:]:
        copy.wait_send()

    for here, far in far8:
        pl.when(jnp.logical_not(here))(far.wait_send)


def per_device(control, innovation, obs_weight, courant_x, courant_y, filter_x, filter_y):
    dma = lambda *shape: pltpu.SemaphoreType.DMA(shape)
    big = pltpu.VMEM((64, 8, 256), F32)
    half = pltpu.VMEM((2, 512, 128), F32)
    ext = pltpu.VMEM((2, 528, 128), F32)
    col = pltpu.VMEM((512, 128), F32)
    lev = pltpu.VMEM((8, 64, 256), BF16)
    levh = pltpu.VMEM((2, 8, 64, 128), BF16)
    halo = pltpu.VMEM((2, 8, 512), F32)
    planes = pltpu.VMEM((2, 4, 64, 256), BF16)
    shares = pltpu.VMEM((2, 4, 2, 256, 128), BF16)
    sums = pltpu.VMEM((2, 3, 512, 128), BF16)
    scratch = [
        pltpu.VMEM((64, 8, 256), BF16), big, big, big, big,
        half, levh,
        pltpu.VMEM((2, 32, 64, 128), BF16),
        pltpu.VMEM((2, 4, 4, 16, 2048), BF16),
        pltpu.VMEM((2, 8, 32, 2048), BF16),
        pltpu.VMEM((2, 2, 256, 128), BF16),
        pltpu.VMEM((2, 8, 256, 128), BF16),
        pltpu.VMEM((2, 128, 256), F32),
        planes, lev,
        pltpu.VMEM((2, 544, 128), F32), halo, halo,
        pltpu.VMEM((4, 8, 128), F32),
        pltpu.VMEM((4, 2, 8, 256), F32), halo, halo,
        col, col, col, col, ext, half, half, half, lev, planes,
        shares,
        pltpu.VMEM((2, 256, 128), F32),
        shares,
        pltpu.VMEM((2, 2, 256, 128), BF16),
        sums,
        pltpu.VMEM((2, 512, 128), F32),
        sums, levh, levh,
        dma(7), dma(4, 2), dma(4, 2), dma(1), dma(1), dma(2), dma(2), dma(4), dma(4),
        dma(1), dma(1), dma(3), dma(3), dma(4), dma(4),
        dma(2, 8), dma(2, 8), dma(2, 3, 4), dma(2, 3, 4), dma(4, 4, 2), dma(4, 4, 2), dma(8), dma(8),
        dma(8), dma(8), dma(4, 2), dma(4, 2), dma(2), dma(2), dma(7), dma(7), dma(3, 4, 2), dma(3, 4, 2),
        dma(2, 2, 3), dma(2, 2, 3), dma(2, 4, 2), dma(2, 8),
    ]
    out = pltpu.VMEM((64, 8, 256), F32)
    anywhere = pl.BlockSpec(memory_space=pl.ANY)
    return pl.pallas_call(
        kernel,
        out_shape=(out, out),
        in_specs=[anywhere] * 7,
        out_specs=(pl.BlockSpec(memory_space=pltpu.VMEM),) * 2,
        scratch_shapes=scratch,
        compiler_params=pltpu.CompilerParams(
            collective_id=0, has_side_effects=True, vmem_limit_bytes=62 * 1024 * 1024),
        cost_estimate=pl.CostEstimate(flops=2150000000, bytes_accessed=5000000, transcendentals=0),
    )(control, innovation, obs_weight, courant_x, courant_y,
      filter_x.reshape(4, 16, 2048), filter_y.reshape(8, 32, 2048))


def solution(mesh):
    grid = P("gx", None, "gy")
    placed = (grid, grid, grid, grid, grid, P("gx", None), P("gy", None))
    return jax.shard_map(
        per_device, mesh=mesh, in_specs=placed, out_specs=(grid, grid), check_vma=False)
```

```python
import jax
import jax.numpy as jnp
from jax import lax
from jax.experimental import pallas as pl
from jax.experimental.pallas import tpu as pltpu
from jax.sharding import PartitionSpec as P

MESH = pl.DeviceIdType.MESH
F32 = jnp.float32
BF16 = jnp.bfloat16
F_ONE = ((2, 2, pl.ds(0, 1024)), (2, 6, pl.ds(1024, 1024)), (1, 7, pl.ds(0, 2048)), (3, 1, pl.ds(0, 2048)))


def place(x, y, z, c):
    return (y * 8 + lax.rem(z, 4) * 2 + c, (z // 4) * 4 + x)


def kernel(
    ctl, innov, weight, cou_x, cou_y, fx, fy,
    end_out, grad_out,
    ctl_v, inn_v, wei_v, cx_v, cy_v,
    nat, snd0, cg, fxb, fyb, s1b, s1g, acc2, s2b, stg,
    st, hys, hyr, cor, frow, fcs, fcr, hl, hr, ql, qr, qx, py, mis, adj, ags, ag,
    psend, pown, pg, pb, gsend, gown, gg, gs, go,
    loc_sem, f1_s, f1_r, fo_s, fo_r, f2_s, f2_r, fr_s, fr_r,
    g1_s, g1_r, g2_s, g2_r, gr_s, gr_r,
    s0_s, s0_r, s1_s, s1_r, s2_s, s2_r, s3_s, s3_r,
    h_s, h_r, fw_s, fw_r, fc_s, fc_r, s5_s, s5_r, s6_s, s6_r, s7_s, s7_r, s8_s, s8_r,
):
    gx = lax.axis_index("gx")
    gy = lax.axis_index("gy")
    y = gx // 8
    zl = lax.rem(gx // 2, 4)
    c = lax.rem(gx, 2)
    zh = gy // 4
    x = lax.rem(gy, 4)
    z = zh * 4 + zl
    o = 1 - c
    sib = place(x, y, z, o)
    e = y * 2 + c
    pending = []

    def send(src, dst, ssem, rsem, dev):
        copy = pltpu.make_async_remote_copy(
            src_ref=src, dst_ref=dst, send_sem=ssem, recv_sem=rsem,
            device_id=dev, device_id_type=MESH)
        copy.start()
        pending.append(copy)

    def arrived(dst, rsem):
        pltpu.make_async_copy(dst, dst, rsem).wait()

    xs = [lax.rem(x + t, 4) for t in range(4)]
    ys = [lax.rem(y + t, 4) for t in range(4)]
    zs = [lax.rem(z + t, 8) for t in range(8)]
    up = (lax.rem(gx + 1, 32), gy)
    down = (lax.rem(gx + 31, 32), gy)
    right = (gx, lax.rem(gy + 1, 8))
    left = (gx, lax.rem(gy + 7, 8))
    corners = [(up[0], right[1]), (up[0], left[1]), (down[0], right[1]), (down[0], left[1])]

    load_ctl = pltpu.make_async_copy(ctl, ctl_v, loc_sem.at[0])
    load_ctl.start()
    loads = [
        pltpu.make_async_copy(s, d, loc_sem.at[1 + i])
        for i, (s, d) in enumerate([
            (fx, fxb.at[c, 0]), (fy, fyb.at[zh]), (innov, inn_v),
            (weight, wei_v), (cou_x, cx_v), (cou_y, cy_v)])
    ]
    for load in loads:
        load.start()

    barrier = pltpu.get_barrier_semaphore()
    partners = [sib]
    for t in range(1, 8):
        partners += [place(x, y, zs[t], c), place(x, y, zs[t], o)]
    for t in range(1, 4):
        partners += [place(xs[t], y, z, c), place(xs[t], y, z, o)]
        partners += [place(x, ys[t], z, c)]
    partners += [up, down, left, right] + corners
    for dev in partners:
        pl.semaphore_signal(barrier, inc=1, device_id=dev, device_id_type=MESH)

    load_ctl.wait()

    def by_level(h):
        nat[h] = ctl_v[:, :, h * 128:(h + 1) * 128].astype(F32).reshape(512, 128)
        for l in range(8):
            snd0[h, l] = nat[h, pl.ds(l, 64, stride=8), :].astype(BF16)

    by_level(0)

    pl.semaphore_wait(barrier, len(partners))

    slot0 = zl * 2 + c
    x2 = xs[2]
    own0, far0 = [], []
    for h in range(2):
        if h:
            by_level(1)
        for t in (4, 3, 5, 2, 6, 1, 7):
            send(snd0.at[h, zs[t]], cg.at[h, gx], s0_s.at[h, t], s0_r.at[h, slot0], place(x, y, zs[t], zh))
        src, dst = snd0.at[h, z], cg.at[h, gx]
        own0.append(pltpu.make_async_copy(src, dst, s0_r.at[h, slot0]))
        far0.append(pltpu.make_async_remote_copy(
            src_ref=src, dst_ref=dst, send_sem=s0_s.at[h, 0], recv_sem=s0_r.at[h, slot0],
            device_id=sib, device_id_type=MESH))

        @pl.when(zh == c)
        def _():
            own0[h].start()

        @pl.when(zh != c)
        def _():
            far0[h].start()

        q = x2 if h else x
        for k, (d, dz, cols) in enumerate(F_ONE):
            send(fx.at[q, :, cols], fxb.at[c, d, q, :, cols], f1_s.at[k, h], f1_r.at[k, h], place(x, y, zs[dz], c))

    send(fx, fxb.at[c, 0], fo_s.at[0], fo_r.at[0], sib)

    for f, (field, held) in enumerate(((innov, inn_v), (weight, wei_v), (cou_x, cx_v), (cou_y, cy_v))):
        loads[2 + f].wait()
        send(field.at[0], frow.at[f, 1], fw_s.at[f, 0], fw_r.at[f, 1], down)
        send(field.at[63], frow.at[f, 0], fw_s.at[f, 1], fw_r.at[f, 0], up)
        fcs[0, f:f + 1, :] = held[:, :, 0:128].reshape(512, 128).T[0:1]
        fcs[1, f:f + 1, :] = held[:, :, 128:256].reshape(512, 128).T[127:128]
    send(fcs.at[0], fcr.at[0], fc_s.at[0], fc_r.at[0], left)
    send(fcs.at[1], fcr.at[1], fc_s.at[1], fc_r.at[1], right)

    def ring(h):
        for s in range(4):
            for cc in range(2):
                arrived(cg.at[h, y * 8 + 2 * s + cc], s0_r.at[h, 2 * s + cc])
            block = cg.at[h, pl.ds(y * 8 + 2 * s, 2)]
            for t in (2, 1, 3):
                send(block, block, s1_s.at[h, t - 1, s], s1_r.at[h, t - 1, s], place(x, ys[t], z, c))

    ring(0)

    send(fy.at[e], fyb.at[zh, e], g1_s.at[0], g1_r.at[0], place(x, y, zs[4], c))

    for k, (d, dz, cols) in enumerate(F_ONE):
        arrived(fxb.at[c, d, x, :, cols], f1_r.at[k, 0])
    quarter = fxb.at[c, pl.ds(1, 3), x]
    for t in (1, 3):
        send(quarter, quarter, f2_s.at[t // 2], f2_r.at[t // 2], place(xs[t], y, z, c))
    send(quarter, quarter, fr_s.at[0], fr_r.at[0], sib)

    ring(1)

    for k, (d, dz, cols) in enumerate(F_ONE):
        arrived(fxb.at[c, d, x2, :, cols], f1_r.at[k, 1])
    quarter = fxb.at[c, pl.ds(1, 3), x2]
    send(quarter, quarter, fr_s.at[2], fr_r.at[2], sib)

    for t in (1, 3):
        part = fxb.at[c, pl.ds(1, 3), xs[4 - t]]
        arrived(part, f2_r.at[t // 2])
        send(part, part, fr_s.at[t], fr_r.at[t], sib)

    loads[0].wait()
    loads[1].wait()
    arrived(fxb.at[o, 0], fo_r.at[0])
    for t in range(4):
        arrived(fxb.at[o, pl.ds(1, 3), xs[(4 - t) % 4]], fr_r.at[t])

    mine = c * 4 + x
    zo = 1 - zh
    for h in range(2):
        for t in (3, 1, 2):
            for s in range(4):
                arrived(cg.at[h, pl.ds(ys[4 - t] * 8 + 2 * s, 2)], s1_r.at[h, t - 1, s])
        for g in range(2):
            k = 2 * h + g
            rows = pl.ds(g * 128, 128)
            a = fxb[:, 2 * g:2 * g + 2].reshape(256, 2048)
            v = jnp.dot(a, cg[h].reshape(2048, 128), preferred_element_type=F32)
            s1b[h, :, rows] = v.astype(BF16).reshape(2, 128, 128)
            for t in (2, 1, 3):
                for r in range(2):
                    send(s1b.at[h, r, rows], s1g.at[h, mine, rows],
                         s2_s.at[k, t, r], s2_r.at[k, t, c], place(xs[t], y, z, r))
            send(s1b.at[h, o, rows], s1g.at[h, mine, rows], s2_s.at[k, 0, 0], s2_r.at[k, 0, 0], sib)
        s1g[h, mine] = s1b[h, c]
        if h == 0:
            arrived(fyb.at[zo, e], g1_r.at[0])
            for t in (2, 1, 3):
                send(fyb.at[zo, e], fyb.at[zo, e], g2_s.at[t - 1], g2_r.at[t - 1], place(x, ys[t], z, c))
            send(fyb.at[zo, e], fyb.at[zo, e], gr_s.at[0], gr_r.at[0], sib)

    def cols_dot(h, q, hh, g):
        cols = pl.ds(pl.multiple_of(q * 256 + h * 128, 128), 128)
        b = fyb[hh, :, :, cols].reshape(256, 128)
        a = s1g[h, q, g * 128:(g + 1) * 128, :]
        return lax.dot_general(a, b, (((1,), (1,)), ((), ())), preferred_element_type=F32)

    sources = [(0, 0, mine), (0, 0, o * 4 + x)]
    sources += [(t, cc, cc * 4 + xs[4 - t]) for t in (3, 1, 2) for cc in range(2)]

    def level_up(k, hh):
        for h in range(2):
            for g in range(2):
                rows = pl.ds(g * 128, 128)
                for i, (t, cc, q) in enumerate(sources):
                    if i and k == 0:
                        arrived(s1g.at[h, q, rows], s2_r.at[2 * h + g, t, cc])
                    term = cols_dot(h, q, hh, g)
                    acc2[g] = acc2[g] + term if h or i else term
                if h:
                    s2b[hh, 2 * g:2 * g + 2] = acc2[g].astype(BF16).reshape(2, 64, 256)
                    for d in ((1, 0) if g == 0 else (2, 3)):
                        if k or d:
                            send(s2b.at[hh, d], stg.at[z], s3_s.at[k * 4 + d], s3_r.at[k * 4 + d],
                                 place(x, y, hh * 4 + lax.rem(zl + d, 4), c))

    for t in (3, 1, 2):
        eq = ys[4 - t] * 2 + c
        arrived(fyb.at[zo, eq], g2_r.at[t - 1])
        send(fyb.at[zo, eq], fyb.at[zo, eq], gr_s.at[t], gr_r.at[t], sib)
    level_up(0, zh)
    stg[z] = s2b[zh, 0]
    for t in range(4):
        arrived(fyb.at[zo, ys[(4 - t) % 4] * 2 + o], gr_r.at[t])
    level_up(1, zo)

    def spread(l):
        value = stg[l].astype(F32)
        for h in range(2):
            st[h, pl.ds(16 + l, 64, stride=8), :] = value[:, h * 128:(h + 1) * 128]

    for k, hh in ((0, zh), (1, zo)):
        for d in range(4):
            if k or d:
                arrived(stg.at[hh * 4 + lax.rem(zl + 4 - d, 4)], s3_r.at[k * 4 + d])
    for l in range(8):
        spread(l)

    send(st.at[:, pl.ds(16, 16)], st.at[:, pl.ds(528, 16)], h_s.at[0], h_r.at[0], down)
    send(st.at[:, pl.ds(512, 16)], st.at[:, pl.ds(0, 16)], h_s.at[1], h_r.at[1], up)
    for k, (h, at) in enumerate(((1, 520), (0, 520), (1, 16), (0, 16))):
        send(st.at[h, pl.ds(at, 8)], cor.at[k], h_s.at[4 + k], h_r.at[4 + k], corners[k])
    hys[0] = st[0, 16:528, :].T[0:8]
    send(hys.at[0], hyr.at[0], h_s.at[2], h_r.at[2], left)
    hys[1] = st[1, 16:528, :].T[120:128]
    send(hys.at[1], hyr.at[1], h_s.at[3], h_r.at[3], right)
    for f in range(4):
        for k in range(2):
            arrived(frow.at[f, k], fw_r.at[f, k])
    for k in range(2):
        arrived(fcr.at[k], fc_r.at[k])
    arrived(st.at[:, pl.ds(528, 16)], h_r.at[0])
    arrived(st.at[:, pl.ds(0, 16)], h_r.at[1])
    for k in range(2):
        arrived(hyr.at[k], h_r.at[2 + k])
    for k in range(4):
        arrived(cor.at[k], h_r.at[4 + k])

    @pl.when(gx == 0)
    def _():
        st[:, 0:16, :] = jnp.zeros((2, 16, 128), F32)

    @pl.when(gx == 31)
    def _():
        st[:, 528:544, :] = jnp.zeros((2, 16, 128), F32)

    keep_u = jnp.where(gx == 0, 0.0, 1.0).astype(F32)
    keep_d = jnp.where(gx == 31, 0.0, 1.0).astype(F32)
    keep_l = jnp.where(gy == 0, 0.0, 1.0).astype(F32)
    keep_r = jnp.where(gy == 7, 0.0, 1.0).astype(F32)
    cor[0] = cor[0] * (keep_u * keep_l)
    cor[1] = cor[1] * (keep_u * keep_r)
    cor[2] = cor[2] * (keep_d * keep_l)
    cor[3] = cor[3] * (keep_d * keep_r)
    beyond_l = hyr[1, 6:8, :] * keep_l
    beyond_r = hyr[0, 0:2, :] * keep_r
    hr[...] = jnp.broadcast_to(beyond_r[0:1], (128, 512)).T
    hl[...] = jnp.broadcast_to(beyond_l[1:2], (128, 512)).T

    def beside(v0, v1, left_halo, right_halo):
        lane = lax.broadcasted_iota(jnp.int32, v0.shape, 1)
        f0, f1 = pltpu.roll(v0, 127, 1), pltpu.roll(v1, 127, 1)
        b0, b1 = pltpu.roll(v0, 1, 1), pltpu.roll(v1, 1, 1)
        after = (jnp.where(lane == 127, f1, f0), jnp.where(lane == 127, right_halo, f1))
        before = (jnp.where(lane == 0, left_halo, b0), jnp.where(lane == 0, b0, b1))
        return before, after

    for k, at, to, keep in ((0, 8, 0, keep_u), (1, 528, 520, keep_d)):
        v = [st[h, at:at + 8, :] for h in range(2)]
        before, after = beside(v[0], v[1], pltpu.roll(cor[2 * k], 1, 1), pltpu.roll(cor[2 * k + 1], 127, 1))
        for h in range(2):
            ln = slice(h * 128, (h + 1) * 128)
            cx, cy = frow[2, k, :, ln], frow[3, k, :, ln]
            end = (v[h] - cx * (st[h, at + 8:at + 16, :] - st[h, at - 8:at, :]) * 0.5
                   - cy * (after[h] - before[h]) * 0.5)
            qx[h, to:to + 8, :] = keep * cx * (frow[1, k, :, ln] * (end - frow[0, k, :, ln]))

    spot = lax.broadcasted_iota(jnp.int32, (8, 512), 1)
    level = lax.broadcasted_iota(jnp.int32, (8, 512), 0)
    ahead = lax.broadcasted_iota(jnp.int32, (1, 512), 1)

    def along(k, at):
        column = jnp.broadcast_to(cor[k][:, at:at + 1], (8, 512))
        return jnp.sum(jnp.where(lax.rem(spot, 8) == level, column, 0.0), axis=0, keepdims=True)

    def flux(k, value, low, high, first, last, keep):
        prev = jnp.where(ahead < 8, first, pltpu.roll(value, 8, 1))
        post = jnp.where(ahead >= 504, last, pltpu.roll(value, 504, 1))
        inn, wei, cx, cy = [fcr[k, f:f + 1, :] for f in range(4)]
        end = value - cx * (post - prev) * 0.5 - cy * (high - low) * 0.5
        return jnp.broadcast_to(keep * cy * (wei * (end - inn)), (128, 512)).T

    ql[...] = flux(1, beyond_l[1:2], beyond_l[0:1], hys[0, 0:1, :], along(0, 127), along(2, 127), keep_l)
    qr[...] = flux(0, beyond_r[0:1], hys[1, 7:8, :], beyond_r[1:2], along(1, 0), along(3, 0), keep_r)

    @pl.loop(0, 8)
    def _(i):
        at = pl.multiple_of(i * 64, 64)
        xr = pl.ds(i * 8, 8)
        v = [st[h, pl.ds(at + 16, 64), :] for h in range(2)]
        before, after = beside(v[0], v[1], hl[pl.ds(at, 64), :], hr[pl.ds(at, 64), :])
        for h in range(2):
            ln = slice(h * 128, (h + 1) * 128)
            cx = cx_v[xr, :, ln].reshape(64, 128)
            cy = cy_v[xr, :, ln].reshape(64, 128)
            prev = st[h, pl.ds(at + 8, 64), :]
            post = st[h, pl.ds(at + 24, 64), :]
            end = v[h] - cx * (post - prev) * 0.5 - cy * (after[h] - before[h]) * 0.5
            end_out[xr, :, ln] = end.reshape(8, 8, 128)
            m = wei_v[xr, :, ln].reshape(64, 128) * (end - inn_v[xr, :, ln].reshape(64, 128))
            mis[h, pl.ds(at, 64), :] = m
            qx[h, pl.ds(at + 8, 64), :] = cx * m
            py[h, pl.ds(at, 64), :] = cy * m

    @pl.loop(0, 8)
    def _(i):
        at = pl.multiple_of(i * 64, 64)
        v = [py[h, pl.ds(at, 64), :] for h in range(2)]
        before, after = beside(v[0], v[1], ql[pl.ds(at, 64), :], qr[pl.ds(at, 64), :])
        for h in range(2):
            prev = qx[h, pl.ds(at, 64), :]
            post = qx[h, pl.ds(at + 16, 64), :]
            adj[h, pl.ds(at, 64), :] = (
                mis[h, pl.ds(at, 64), :] + 0.5 * (post - prev) + 0.5 * (after[h] - before[h]))

    for l in range(8):
        for h in range(2):
            ags[l, :, h * 128:(h + 1) * 128] = adj[h, pl.ds(l, 64, stride=8), :].astype(BF16)

    for t in (4, 3, 7, 2, 6, 5, 1):
        send(ags.at[zs[t]], ag.at[zh, (4 - t % 4) % 4], s5_s.at[t - 1], s5_r.at[t - 1], place(x, y, zs[t], c))
    ag[zh, 0] = ags[z]

    def share(g, q):
        cols = pl.ds(pl.multiple_of(q * 256, 256), 256)
        total = None
        for hh in range(2):
            a = ag[hh, 2 * g:2 * g + 2].reshape(128, 256)
            b = fyb[hh, :, :, cols].reshape(256, 256)
            term = jnp.dot(a, b, preferred_element_type=F32)
            total = term if total is None else total + term
        return total

    targets = [(t, r, r * 4 + xs[t], place(xs[t], y, z, r)) for t in (2, 1, 3) for r in range(2)]
    targets += [(0, 0, o * 4 + x, sib)]

    def hand(h, k, rows):
        for t, r, q, dev in targets:
            send(psend.at[h, t, r, rows], pg.at[h, t, c, rows],
                 s6_s.at[k, t, r], s6_r.at[k, t, c], dev)

    for g in range(2):
        rows = pl.ds(g * 128, 128)
        for t in ((4, 3, 7) if g == 0 else (2, 6, 5, 1)):
            arrived(ag.at[zs[8 - t] // 4, (4 - t % 4) % 4], s5_r.at[t - 1])
        for t, r, q, dev in targets:
            value = share(g, q).astype(BF16)
            for h in range(2):
                psend[h, t, r, rows] = value[:, h * 128:(h + 1) * 128]
            send(psend.at[0, t, r, rows], pg.at[0, t, c, rows],
                 s6_s.at[g, t, r], s6_r.at[g, t, c], dev)
        value = share(g, mine)
        for h in range(2):
            pown[h, rows] = value[:, h * 128:(h + 1) * 128]

    def lines(h, q, part):
        cols = pl.ds(pl.multiple_of(q * 512 + part * 256, 256), 256)
        a = fxb[:, :, :, :, cols].reshape(512, 256)
        b = pb[h].reshape(512, 128)
        return lax.dot_general(a, b, (((0,), (0,)), ((), ())), preferred_element_type=F32)

    def three(h, r):
        return pg[h, 1, r].astype(F32) + pg[h, 2, r].astype(F32) + pg[h, 3, r].astype(F32)

    for h in range(2):
        for k, rows in ((0, pl.ds(0, 128)), (1, pl.ds(128, 128))) if h == 0 else ((2, pl.ds(0, 256)),):
            arrived(pg.at[h, 0, o, rows], s6_r.at[k, 0, o])
            for t in (1, 3, 2):
                for cc in range(2):
                    arrived(pg.at[h, t, cc, rows], s6_r.at[k, t, cc])
            if k == 0:
                hand(1, 2, pl.ds(0, 256))
        pb[h, c] = (three(h, c) + pown[h]).astype(BF16)
        pb[h, o] = (three(h, o) + pg[h, 0, o].astype(F32)).astype(BF16)
        for part in range(2):
            rows = pl.ds(part * 256, 256)
            for t in (2, 1, 3):
                gsend[h, t - 1, rows] = lines(h, ys[t], part).astype(BF16)
                send(gsend.at[h, t - 1, rows], gg.at[h, t - 1, rows],
                     s7_s.at[h, part, t - 1], s7_r.at[h, part, t - 1], place(x, ys[t], z, c))
        for part in range(2):
            gown[h, pl.ds(part * 256, 256)] = lines(h, y, part)

    early = len(pending)
    far8 = []
    for h in range(2):
        for part in range(2):
            rows = pl.ds(part * 256, 256)
            total = gown[h, rows]
            for t in (1, 3, 2):
                arrived(gg.at[h, t - 1, rows], s7_r.at[h, part, t - 1])
                total += gg[h, t - 1, rows].astype(F32)
            gs[h, 4 * part:4 * part + 4] = total.astype(BF16).reshape(4, 64, 128)
            for zq in (2 * part, 2 * part + 1):
                send(gs.at[h, zq * 2 + o], go.at[h, z], s8_s.at[h, zq, 1], s8_r.at[h, z],
                     place(x, y, c * 4 + zq, o))
                here = jnp.logical_and(zl == zq, zh == c)
                src, dst = gs.at[h, zq * 2 + c], go.at[h, z]
                own = pltpu.make_async_copy(src, dst, s8_r.at[h, z])
                far = pltpu.make_async_remote_copy(
                    src_ref=src, dst_ref=dst, send_sem=s8_s.at[h, zq, 0], recv_sem=s8_r.at[h, z],
                    device_id=place(x, y, c * 4 + zq, c), device_id_type=MESH)
                pl.when(here)(own.start)
                pl.when(jnp.logical_not(here))(far.start)
                far8.append((here, far))

    for copy in pending[:early]:
        copy.wait_send()

    @pl.when(zh != c)
    def _():
        for h in range(2):
            far0[h].wait_send()

    for h in range(2):
        ln = slice(h * 128, (h + 1) * 128)
        for l in range(8):
            arrived(go.at[h, l], s8_r.at[h, l])
        for l in range(8):
            nat[h, pl.ds(l, 64, stride=8), :] = go[h, l].astype(F32)
        grad_out[:, :, ln] = ctl_v[:, :, ln].astype(F32) + nat[h].reshape(64, 8, 128)
    for copy in pending[early:]:
        copy.wait_send()

    for here, far in far8:
        pl.when(jnp.logical_not(here))(far.wait_send)


def per_device(control, innovation, obs_weight, courant_x, courant_y, filter_x, filter_y):
    dma = lambda *shape: pltpu.SemaphoreType.DMA(shape)
    big = pltpu.VMEM((64, 8, 256), F32)
    half = pltpu.VMEM((2, 512, 128), F32)
    ext = pltpu.VMEM((2, 528, 128), F32)
    col = pltpu.VMEM((512, 128), F32)
    lev = pltpu.VMEM((8, 64, 256), BF16)
    levh = pltpu.VMEM((2, 8, 64, 128), BF16)
    halo = pltpu.VMEM((2, 8, 512), F32)
    planes = pltpu.VMEM((2, 4, 64, 256), BF16)
    shares = pltpu.VMEM((2, 4, 2, 256, 128), BF16)
    sums = pltpu.VMEM((2, 3, 512, 128), BF16)
    scratch = [
        pltpu.VMEM((64, 8, 256), BF16), big, big, big, big,
        half, levh,
        pltpu.VMEM((2, 32, 64, 128), BF16),
        pltpu.VMEM((2, 4, 4, 16, 2048), BF16),
        pltpu.VMEM((2, 8, 32, 2048), BF16),
        pltpu.VMEM((2, 2, 256, 128), BF16),
        pltpu.VMEM((2, 8, 256, 128), BF16),
        pltpu.VMEM((2, 128, 256), F32),
        planes, lev,
        pltpu.VMEM((2, 544, 128), F32), halo, halo,
        pltpu.VMEM((4, 8, 128), F32),
        pltpu.VMEM((4, 2, 8, 256), F32), halo, halo,
        col, col, col, col, ext, half, half, half, lev, planes,
        shares,
        pltpu.VMEM((2, 256, 128), F32),
        shares,
        pltpu.VMEM((2, 2, 256, 128), BF16),
        sums,
        pltpu.VMEM((2, 512, 128), F32),
        sums, levh, levh,
        dma(7), dma(4, 2), dma(4, 2), dma(1), dma(1), dma(2), dma(2), dma(4), dma(4),
        dma(1), dma(1), dma(3), dma(3), dma(4), dma(4),
        dma(2, 8), dma(2, 8), dma(2, 3, 4), dma(2, 3, 4), dma(4, 4, 2), dma(4, 4, 2), dma(8), dma(8),
        dma(8), dma(8), dma(4, 2), dma(4, 2), dma(2), dma(2), dma(7), dma(7), dma(3, 4, 2), dma(3, 4, 2),
        dma(2, 2, 3), dma(2, 2, 3), dma(2, 4, 2), dma(2, 8),
    ]
    out = pltpu.VMEM((64, 8, 256), F32)
    anywhere = pl.BlockSpec(memory_space=pl.ANY)
    return pl.pallas_call(
        kernel,
        out_shape=(out, out),
        in_specs=[anywhere] * 7,
        out_specs=(pl.BlockSpec(memory_space=pltpu.VMEM),) * 2,
        scratch_shapes=scratch,
        compiler_params=pltpu.CompilerParams(
            collective_id=0, has_side_effects=True, vmem_limit_bytes=62 * 1024 * 1024),
        cost_estimate=pl.CostEstimate(flops=2150000000, bytes_accessed=5000000, transcendentals=0),
    )(control, innovation, obs_weight, courant_x, courant_y,
      filter_x.reshape(4, 16, 2048), filter_y.reshape(8, 32, 2048))


def solution(mesh):
    grid = P("gx", None, "gy")
    placed = (grid, grid, grid, grid, grid, P("gx", None), P("gy", None))
    return jax.shard_map(
        per_device, mesh=mesh, in_specs=placed, out_specs=(grid, grid), check_vma=False)
```
